128 devices in a mesh: seq: 8 (over y_hi, x), batch: 16 (over y_lo, z, core).
Axes of the slice: x: 4, y: 4 (y_hi: 2, y_lo: 2; y = y_hi * 2 + y_lo), z: 4, core: 2. Of those that a mesh axis runs over, the one named last changes fastest.
Arguments:
- tokens: bfloat16 [16, 1024, 1536], P('batch', 'seq'), may hold values from -6 to 6
- cotangent: bfloat16 [16, 1024, 1536], P('batch', 'seq'), may hold values from -6 to 6
- segments: int32 [16, 1024], P('batch'), may hold values from 0 to 5, as said below
- routes: int32 [16, 1024, 8], P('batch', 'seq'), may hold values from 0 to 31, all different within a row; in each aligned block of 128 rows (0 to 127, 128 to 255, ..., all dimensions but the last counted through in order) at most 48 rows name the same one
- gate_weights: float32 [16, 1024, 8], P('batch', 'seq'), may hold values from 0.06 to 0.24
- w_query: bfloat16 [1536, 1536], P(('seq', 'batch')), may hold values from -0.15625 to 0.15625
- w_key: bfloat16 [1536, 512], P(('seq', 'batch')), may hold values from -0.15625 to 0.15625
- w_value: bfloat16 [1536, 512], P(('seq', 'batch')), may hold values from -0.15625 to 0.15625
- w_out: bfloat16 [1536, 1536], P(('seq', 'batch')), may hold values from -0.875 to 0.875
- norm_one: bfloat16 [1536], P(('seq', 'batch')), may hold values from 0.5 to 1.5
- norm_two: bfloat16 [1536], P(('seq', 'batch')), may hold values from 0.5 to 1.5
- w_gate: bfloat16 [32, 1536, 512], P('batch', 'seq'), may hold values from -0.15625 to 0.15625
- w_up: bfloat16 [32, 1536, 512], P('batch', 'seq'), may hold values from -0.15625 to 0.15625
- w_down: bfloat16 [32, 512, 1536], P('batch', 'seq'), may hold values from -1 to 1
Outputs:
- output: bfloat16 [16, 1024, 1536], P('batch', 'seq')
- grad_tokens: bfloat16 [16, 1024, 1536], P('batch', 'seq')
- grad_w_query: float32 [1536, 1536], P(('seq', 'batch'))
- grad_w_key: float32 [1536, 512], P(('seq', 'batch'))
- grad_w_value: float32 [1536, 512], P(('seq', 'batch'))
- grad_w_out: float32 [1536, 1536], P(('seq', 'batch'))
- grad_norm_one: float32 [1536], P(('seq', 'batch'))
- grad_norm_two: float32 [1536], P(('seq', 'batch'))
- grad_w_gate: float32 [32, 1536, 512], P('batch', 'seq')
- grad_w_up: float32 [32, 1536, 512], P('batch', 'seq')
- grad_w_down: float32 [32, 512, 1536], P('batch', 'seq')
The draws below stay inside these ranges and needn't reach their ends.
Inputs may be any that keep to these rules, and one draw needn't show every extreme that they name: `segments`: along each sequence the segment numbers start at 0 and never fall, rising by one at each document boundary; whole documents hold 204 to 801 tokens, or in one of the sequences up to 1023; the first and last document of a sequence may be cut by its ends. `routes`: each token names 8 different experts; among the 128 tokens of one device (aligned blocks of rows) no expert is named more than 48 times, a bound that some block reaches.
All inputs are finite; a program needn't handle non-finite values.
Results may differ from the reference program's by a relative error of at most 0.019.
Values may be sent and summed in bfloat16 or wider, within the bound.
No kernel may reach another device: no remote copies, remote signals or barrier semaphores. Data moves between devices by JAX's collectives and lax.ppermute only.
A program may use at most 192 MiB of HBM per device.

```python
import math
import jax
import jax.numpy as jnp
import numpy as np
from jax import lax

D = 1536
HEADS = 24
KV_HEADS = 8
HEAD_DIM = 64
FF_E = 512
TOPK = 8
TOK_DEV = 128
SEQ_LEN = 1024
SEQS = 16
EXPERTS = 32
CAP = 48


def draw_segments(key, part):
    key = jax.random.fold_in(key, 11)
    len_key, off_key, pick_key, first_key, last_key, other_key, dense_key = jax.random.split(key, 7)
    shortest = SEQ_LEN // 5
    longest = SEQ_LEN * 25 // 32 + 2
    lengths = jax.random.randint(len_key, (SEQS, 8), shortest, longest).astype(jnp.int32)
    offset = jax.random.randint(off_key, (SEQS, 1), 0, shortest).astype(jnp.int32)
    bounds = (jnp.cumsum(lengths, axis=1).astype(jnp.int32) - offset)[:, None, :]
    place_col = jnp.arange(SEQ_LEN, dtype=jnp.int32)[None, :, None]
    spread = jnp.sum((place_col >= bounds).astype(jnp.int32), axis=2).astype(jnp.int32)
    chosen = jax.random.randint(pick_key, (), 0, SEQS).astype(jnp.int32)
    start_at = jax.random.randint(first_key, (SEQS, 1), 1, TOK_DEV)
    finish_at = jax.random.randint(last_key, (SEQS, 1), SEQ_LEN - TOK_DEV + 1, SEQ_LEN)
    place = jnp.arange(SEQ_LEN, dtype=jnp.int32)[None, :]
    long_form = (place >= start_at).astype(jnp.int32) + (place >= finish_at).astype(jnp.int32)
    other = ((chosen + 1 + jax.random.randint(other_key, (), 0, SEQS - 1)) % SEQS).astype(jnp.int32)
    dense_start = jax.random.randint(dense_key, (), 1, SEQ_LEN - 4 * shortest).astype(jnp.int32)
    dense_bounds = dense_start + shortest * jnp.arange(5, dtype=jnp.int32)
    dense_form = jnp.sum((place[:, :, None] >= dense_bounds[None, None, :]).astype(jnp.int32), axis=2).astype(jnp.int32)
    seq_ids = jnp.arange(SEQS, dtype=jnp.int32)[:, None]
    result = jnp.where(seq_ids == other, dense_form, spread)
    result = jnp.where(seq_ids == chosen, long_form, result)
    return result.astype(jnp.int32)


def level_of(rng, dims, pieces, smallest, high):
    gain = 1.0
    for axis_at, parts in pieces:
        draws = jax.random.uniform(jax.random.fold_in(jax.random.fold_in(rng, 6), axis_at), (parts,), jnp.float32, smallest / len(pieces), high / len(pieces))
        gain = gain * jnp.repeat(jnp.exp(draws), dims[axis_at] // parts).reshape((-1,) + (1,) * (len(dims) - 1 - axis_at))
    return gain


def shared_out(key, own, number, rows, number_of, top, bound, skew):
    order = jax.random.permutation(key, number_of)
    crowded, common = shares(number_of, rows * top, bound, skew, True), shares(number_of, rows * top, bound, skew, False)
    places = jnp.arange(number_of)

    def named(sizes, rotation):
        used = int((sizes > 0).sum())
        fixed = max(1, used // 4)
        shifted = fixed + (places - fixed + rotation * (used - fixed)) % max(1, number_of - fixed)
        return jnp.zeros((number_of,), jnp.int32).at[order[jnp.where(places < fixed, places, shifted)]].set(jnp.asarray(sizes, jnp.int32))

    sizes = jnp.where(number % 4 == 0, named(crowded, number // 4), named(common, number - number // 4 - 1))
    mixed = jax.random.permutation(jax.random.fold_in(own, 3), number_of)
    donor, sink = mixed[0:number_of // 2 * 2:2], mixed[1:number_of // 2 * 2:2]
    slack = jnp.minimum(sizes[donor] - 1, bound - sizes[sink]) // 2
    slack = jnp.where((donor == order[0]) | (sink == order[0]) | (sizes[sink] == 0), 0, jnp.maximum(slack, 0))
    shifted = jax.random.randint(jax.random.fold_in(own, 4), (number_of // 2,), 0, 1 << 20) % (slack + 1)
    sizes = sizes.at[donor].add(-shifted).at[sink].add(shifted)
    members = jnp.searchsorted(jnp.cumsum(sizes), jnp.arange(rows * top), side="right").astype(jnp.int32)
    listing = members.reshape(top, rows).T
    listing = listing[jax.random.permutation(jax.random.fold_in(own, 1), rows)]
    rotation = jax.random.randint(jax.random.fold_in(own, 2), (rows, 1), 0, top)
    return jnp.take_along_axis(listing, (jnp.arange(top)[None, :] + rotation) % top, axis=1)


def shares(amount, total, most, skew, full):
    loads = [(1 << 20) // math.isqrt(standing ** skew) + 1 for standing in range(1, amount + 1)]
    largest = most if full else min(most, max(-(-total // amount), total * loads[0] // sum(loads)))
    least = 1 if total - largest >= amount - 1 else 0
    counts, spare = [largest] + [least] * (amount - 1), total - largest - least * (amount - 1)
    while spare > 0:
        free = [i for i in range(1, amount) if counts[i] < largest] or [i for i in range(1, amount) if counts[i] < most]
        pool, remaining = sum([loads[i] for i in free]), spare
        for i in free:
            addition = min(most - counts[i], max(1, remaining * loads[i] // pool), spare)
            counts[i] = counts[i] + addition
            spare = spare - addition
    return np.array(counts)


def gaussian(own_key, extent, width, bound, cuts=(), held_as=jnp.bfloat16):
    loudness = level_of(own_key, extent, cuts, -0.22, 0.18) if cuts else 1.0
    values = jax.random.normal(own_key, extent, jnp.float32) * width * loudness
    return jnp.minimum(jnp.maximum(values, -bound), bound).astype(held_as)


def setup_inputs(seed: int = 0) -> dict:
    splits = jax.random.split(jax.random.key(seed), 15)
    tokens = gaussian(splits[0], (SEQS, SEQ_LEN, D), 1.0, 6.0, ((0, 16), (1, 8)))
    cotangent = gaussian(splits[1], (SEQS, SEQ_LEN, D), 1.0, 6.0, ((0, 16), (1, 8)))
    segments = draw_segments(jax.random.fold_in(splits[14], 71), 0)
    routes_keys = jax.random.split(jax.random.fold_in(splits[3], 1), SEQS * SEQ_LEN // TOK_DEV)
    routes_turns = jax.random.permutation(jax.random.fold_in(splits[3], 3), SEQS * SEQ_LEN // TOK_DEV)
    routes = jax.vmap(lambda own, number: shared_out(jax.random.fold_in(splits[3], 2), own, number, TOK_DEV, EXPERTS, TOPK, CAP, 2))(routes_keys, routes_turns).reshape((SEQS, SEQ_LEN, TOPK))
    gate_weights = jnp.clip(jnp.exp(math.log(0.24) - 1.3862944 * jax.random.uniform(splits[4], (SEQS, SEQ_LEN, TOPK), jnp.float32) ** level_of(splits[4], (SEQS, SEQ_LEN, TOPK), ((0, 16), (1, 8)), -0.2, 0.2)), 0.06, 0.24)
    w_query = gaussian(splits[5], (D, HEADS * HEAD_DIM), D ** -0.5, 0.15625, ((0, 128),))
    w_key = gaussian(splits[6], (D, KV_HEADS * HEAD_DIM), D ** -0.5, 0.15625, ((0, 128),))
    w_value = gaussian(splits[7], (D, KV_HEADS * HEAD_DIM), D ** -0.5, 0.15625, ((0, 128),))
    w_out = gaussian(splits[8], (HEADS * HEAD_DIM, D), (HEADS * HEAD_DIM // 32) ** -0.5, 0.875, ((0, 128),))
    norm_one = jnp.clip(1.0 + 0.1 * jax.random.normal(splits[9], (D,), jnp.float32), 0.5, 1.5).astype(jnp.bfloat16)
    norm_two = jnp.clip(1.0 + 0.1 * jax.random.normal(splits[10], (D,), jnp.float32), 0.5, 1.5).astype(jnp.bfloat16)
    w_gate = gaussian(splits[11], (EXPERTS, D, FF_E), D ** -0.5, 0.15625, ((0, 16), (1, 8)))
    w_up = gaussian(splits[12], (EXPERTS, D, FF_E), D ** -0.5, 0.15625, ((0, 16), (1, 8)))
    w_down = gaussian(splits[13], (EXPERTS, FF_E, D), (FF_E // 16) ** -0.5, 1.0, ((0, 16), (1, 8)))
    return {"tokens": tokens, "cotangent": cotangent, "segments": segments, "routes": routes, "gate_weights": gate_weights, "w_query": w_query, "w_key": w_key, "w_value": w_value, "w_out": w_out, "norm_one": norm_one, "norm_two": norm_two, "w_gate": w_gate, "w_up": w_up, "w_down": w_down}


@jax.custom_vjp
def low(v):
    return lax.optimization_barrier(v.astype(jnp.bfloat16)).astype(jnp.float32)

@jax.custom_vjp
def low_back(v):
    return v

def low_keep(v):
    return (low(v), None)

def low_pass(kept, grad):
    return (grad,)

def back_keep(v):
    return (v, None)

def back_low(kept, grad):
    return (low(grad),)
low.defvjp(low_keep, low_pass)
low_back.defvjp(back_keep, back_low)
norm_eps = 1e-06
rope_base = 10000.0
masked_score = -1e+30

def highest(left_side, right_side):
    return jnp.dot(left_side, right_side, precision=lax.Precision.HIGHEST)

def rms_scale(values):
    return lax.rsqrt(lax.optimization_barrier(jnp.mean(values * values, axis=-1, keepdims=True)) + norm_eps)

def rotate(values, cosine, sine):
    half_dim = values.shape[-1] // 2
    turned = jnp.concatenate([-values[..., half_dim:], values[..., :half_dim]], axis=-1)
    return values * cosine + turned * sine

def rope_tables(position):
    freq_index = jnp.arange(HEAD_DIM // 2, dtype=jnp.float32) * (2.0 / HEAD_DIM)
    frequency = rope_base ** (-freq_index)
    angle = position.astype(jnp.float32)[..., None] * frequency
    angle = jnp.concatenate([angle, angle], axis=-1)
    return (jnp.cos(angle), jnp.sin(angle))

def doc_positions(segments):
    seq_index = jnp.arange(SEQ_LEN, dtype=jnp.int32)

    def one_sequence(seg_row):
        earlier = lax.optimization_barrier(jnp.sum((seg_row[None, :] < seg_row[:, None]).astype(jnp.int32), axis=1)).astype(jnp.int32)
        return seq_index - earlier
    return lax.map(one_sequence, segments)

def slot_tables(routes, gate_weights):
    blocks = SEQS * SEQ_LEN // TOK_DEV
    pair_count = TOK_DEV * TOPK
    route_rows = routes.reshape(blocks, pair_count).astype(jnp.int32)
    expert_ids = jnp.arange(EXPERTS, dtype=jnp.int32)
    hits = (route_rows[:, :, None] == expert_ids[None, None, :]).astype(jnp.int32)
    slot_index = lax.optimization_barrier(jnp.sum((jnp.cumsum(hits, axis=1).astype(jnp.int32) - 1) * hits, axis=2)).astype(jnp.int32)
    block_ids = jnp.arange(blocks, dtype=jnp.int32)[:, None]
    token_ids = block_ids * TOK_DEV + jnp.arange(pair_count, dtype=jnp.int32)[None, :] // TOPK
    target = (route_rows * (blocks * CAP) + block_ids * CAP + slot_index).reshape(-1).astype(jnp.int32)
    slot_token = jnp.zeros((EXPERTS * blocks * CAP,), jnp.int32).at[target].set(token_ids.reshape(-1).astype(jnp.int32))
    slot_gate = jnp.zeros((EXPERTS * blocks * CAP,), jnp.float32).at[target].set(gate_weights.reshape(-1).astype(jnp.float32))
    return (slot_token.reshape(EXPERTS, blocks * CAP), slot_gate.reshape(EXPERTS, blocks * CAP))

def reference(tokens, cotangent, segments, routes, gate_weights, w_query, w_key, w_value, w_out, norm_one, norm_two, w_gate, w_up, w_down):
    position = doc_positions(segments).reshape(-1)
    cosine, sine = rope_tables(position)
    cosine = cosine[:, None, :]
    sine = sine[:, None, :]
    slot_token, slot_gate = slot_tables(routes, gate_weights)
    group_size = HEADS // KV_HEADS
    score_scale = HEAD_DIM ** (-0.5)

    def attend(item_tuple):
        queries, key_rows, value_rows, seg_row = item_tuple
        query_heads = queries.reshape(SEQ_LEN, KV_HEADS, group_size, HEAD_DIM)
        key_heads = key_rows.reshape(SEQ_LEN, KV_HEADS, HEAD_DIM)
        value_heads = value_rows.reshape(SEQ_LEN, KV_HEADS, HEAD_DIM)
        place = jnp.arange(SEQ_LEN, dtype=jnp.int32)
        allowed = (seg_row[:, None] == seg_row[None, :]) & (place[None, :] <= place[:, None])
        scores = low_back(jnp.einsum('qkgd,tkd->kgqt', query_heads, key_heads, precision=lax.Precision.HIGHEST) * score_scale)
        scores = jnp.where(allowed[None, None], scores, masked_score)
        row_max = lax.optimization_barrier(jnp.max(scores, axis=-1, keepdims=True))
        exp_scores = jnp.exp(scores - row_max)
        soft_weights = exp_scores / lax.optimization_barrier(jnp.sum(exp_scores, axis=-1, keepdims=True))
        mixed = jnp.einsum('kgqt,tkd->qkgd', low(soft_weights), value_heads, precision=lax.Precision.HIGHEST)
        return low(low_back(mixed.reshape(SEQ_LEN, HEADS * HEAD_DIM)))

    def layer_forward(inputs, query_w, key_w, value_w, out_w, gain_first, gain_second, gate_w, up_w, down_w):
        flat_inputs = inputs.reshape(-1, D)
        normed_one = low(flat_inputs * rms_scale(flat_inputs) * gain_first)
        queries = low_back(highest(normed_one, query_w)).reshape(-1, HEADS, HEAD_DIM)
        key_rows = low_back(highest(normed_one, key_w)).reshape(-1, KV_HEADS, HEAD_DIM)
        value_rows = low(low_back(highest(normed_one, value_w)))
        queries = low(rotate(queries, cosine, sine)).reshape(SEQS, SEQ_LEN, HEADS * HEAD_DIM)
        key_rows = low(rotate(key_rows, cosine, sine)).reshape(SEQS, SEQ_LEN, KV_HEADS * HEAD_DIM)
        value_rows = value_rows.reshape(SEQS, SEQ_LEN, KV_HEADS * HEAD_DIM)
        mixed = lax.map(jax.checkpoint(attend), (queries, key_rows, value_rows, segments))
        mixed = mixed.reshape(-1, HEADS * HEAD_DIM)
        hidden = flat_inputs + low_back(highest(mixed, out_w))
        normed_two = low(hidden * rms_scale(hidden) * gain_second)

        def expert_rows(item_tuple):
            gate_one, up_one, down_one, slot_rows, slot_weight = item_tuple
            picked = low_back(normed_two[slot_rows])
            gate_pre = low_back(highest(picked, gate_one))
            up_pre = low_back(highest(picked, up_one))
            activated = low(jax.nn.silu(gate_pre) * up_pre)
            result = low(low_back(highest(activated, down_one)))
            return slot_weight[:, None] * result
        expert_out = lax.map(jax.checkpoint(expert_rows), (gate_w, up_w, down_w, slot_token, slot_gate))
        routed = jnp.zeros_like(hidden).at[slot_token.reshape(-1)].add(expert_out.reshape(-1, D))
        return (hidden + routed).reshape(inputs.shape)
    arrays = (tokens, w_query, w_key, w_value, w_out, norm_one, norm_two, w_gate, w_up, w_down)
    output, pull_back = jax.vjp(layer_forward, *[array_in.astype(jnp.float32) for array_in in arrays])
    grads = pull_back(cotangent.astype(jnp.float32))
    return (output.astype(jnp.bfloat16), grads[0].astype(jnp.bfloat16), grads[1], grads[2], grads[3], grads[4], grads[5], grads[6], grads[7], grads[8], grads[9])
```

```python
import jax
import jax.numpy as jnp
from jax import lax
from jax.sharding import Mesh, PartitionSpec as P

HEAD_DIM = 64
TOPK = 8
GROUP = 3
Q_OWN = GROUP * HEAD_DIM
norm_eps = 1e-06
rope_base = 10000.0
masked_score = -1e30
SEQ = ("yh", "x")
BATCH = ("yl", "z", "c")
SIZE = {"yh": 2, "x": 4, "yl": 2, "z": 4, "c": 2}
bf16 = jnp.bfloat16
f32 = jnp.float32


def dot(a, b):
    return jnp.dot(a, b, preferred_element_type=f32)


def shift(value, axis, by):
    size = SIZE[axis]
    return lax.ppermute(value, axis, [(i, (i + by) % size) for i in range(size)])


def gather_ring(block, axis):
    half = block.shape[0] // 2
    below = shift(block, axis, 1)
    above = shift(block, axis, -1)
    low = shift(below[:half], axis, 1)
    high = shift(above[half:], axis, -1)
    return [block, above, jnp.concatenate([low, high], axis=0), below]


def gather_seq(block):
    other = shift(block, "yh", 1)
    return gather_ring(block, "x") + gather_ring(other, "x")


def add_low(*parts):
    total = parts[0].astype(f32)
    for part in parts[1:]:
        total = total + part.astype(f32)
    return total


def reduce_ring(blocks, axis):
    half = blocks[0].shape[0] // 2
    ahead = shift(blocks[2][:half], axis, 1)
    behind = shift(blocks[2][half:], axis, -1)
    up = jnp.concatenate(
        [add_low(blocks[1][:half], ahead).astype(bf16), blocks[1][half:].astype(bf16)], axis=0
    )
    down = jnp.concatenate(
        [blocks[3][:half].astype(bf16), add_low(blocks[3][half:], behind).astype(bf16)], axis=0
    )
    return add_low(blocks[0], shift(up, axis, 1), shift(down, axis, -1))


def reduce_seq(blocks):
    far = reduce_ring(blocks[4:], "x").astype(bf16)
    far = shift(far, "yh", 1)
    return add_low(reduce_ring(blocks[:4], "x"), far)


def reduce_batch(blocks):
    sent = shift(blocks[:, :, 1], "c", 1)
    held = add_low(blocks[:, :, 0], sent).astype(bf16)
    ring = [jnp.swapaxes(held[:, k], 0, 1) for k in range(4)]
    total = reduce_ring(ring, "z")
    total = jnp.swapaxes(total, 0, 1)
    return total[0] + shift(total[1].astype(bf16), "yl", 1).astype(f32)


def to_relative(value, axes):
    for place, axis in enumerate(axes):
        value = jnp.roll(value, -lax.axis_index(axis), axis=place)
    return value


def to_absolute(value, axes):
    for place, axis in enumerate(axes):
        value = jnp.roll(value, lax.axis_index(axis), axis=place)
    return value


def seq_relative(rows):
    shape = rows.shape
    return to_relative(rows.reshape((2, 4, shape[0] // 8) + shape[1:]), SEQ).reshape(shape)


def seq_absolute(rows):
    shape = rows.shape
    return to_absolute(rows.reshape((2, 4, shape[0] // 8) + shape[1:]), SEQ).reshape(shape)


def rms_scale(values):
    return lax.rsqrt(jnp.mean(values * values, axis=-1, keepdims=True) + norm_eps)


def rotate(values, cosine, sine):
    half_dim = values.shape[-1] // 2
    turned = jnp.concatenate([-values[..., half_dim:], values[..., :half_dim]], axis=-1)
    return values * cosine + turned * sine


def rope_tables(position):
    freq_index = jnp.arange(HEAD_DIM // 2, dtype=f32) * (2.0 / HEAD_DIM)
    frequency = rope_base ** (-freq_index)
    angle = position.astype(f32)[..., None] * frequency
    angle = jnp.concatenate([angle, angle], axis=-1)
    return (jnp.cos(angle), jnp.sin(angle))


def shards(
    tokens,
    cotangent,
    segments,
    routes,
    gate_weights,
    w_query,
    w_key,
    w_value,
    w_out,
    norm_one,
    norm_two,
    w_gate,
    w_up,
    w_down,
):
    rows = tokens.shape[1]
    features = tokens.shape[2]
    length = segments.shape[1]
    experts = 32
    capacity = rows * TOPK * 3 // (2 * experts)
    score_scale = HEAD_DIM ** (-0.5)
    wide = 384

    strip = jnp.concatenate([w_query, w_key, w_value, w_out], axis=1)
    strip = lax.all_gather(strip, BATCH, axis=0, tiled=True)
    gains = jnp.stack([norm_one, norm_two], axis=1)
    gains = lax.all_gather(gains, BATCH, axis=0, tiled=True)
    part = strip.shape[0]
    by_head = jnp.concatenate(
        [
            strip[:, :1536].reshape(part, 8, Q_OWN),
            strip[:, 1536:2048].reshape(part, 8, HEAD_DIM),
            strip[:, 2048:2560].reshape(part, 8, HEAD_DIM),
            jnp.broadcast_to(jnp.pad(gains, ((0, 0), (0, 62)))[:, None, :], (part, 8, 64)),
        ],
        axis=2,
    )
    by_head = lax.all_to_all(jnp.swapaxes(by_head, 0, 1), SEQ, 0, 0, tiled=True)
    by_head = by_head.reshape(features, wide)
    w_own = by_head[:, :320]
    w_out_own = strip[:, 2560:]
    gain_one = by_head[:, 320].astype(f32)
    gain_two = by_head[:, 321].astype(f32)

    gate_full = lax.all_gather(w_gate, SEQ, axis=1, tiled=True)
    up_full = lax.all_gather(w_up, SEQ, axis=1, tiled=True)
    down_full = lax.all_gather(w_down, SEQ, axis=1, tiled=True)

    flat = routes[0]
    expert_ids = jnp.arange(experts, dtype=jnp.int32)
    gate_dense = jnp.sum(
        jnp.where(flat[:, :, None] == expert_ids, gate_weights[0][:, :, None], 0.0), axis=1
    )
    gate_all = lax.all_gather(gate_dense, BATCH, axis=0)
    grad_all = lax.all_gather(cotangent[0], BATCH, axis=0)
    batch_index = lax.axis_index(BATCH)
    gate_own = lax.dynamic_slice_in_dim(gate_all, batch_index * 2, 2, axis=2)
    gate_own = jnp.transpose(gate_own, (2, 0, 1))
    hit = (gate_own > 0).astype(f32)
    slot = (jnp.cumsum(hit, axis=2) - 1.0) * hit - (1.0 - hit)
    select = (
        slot[:, :, None, :] == jnp.arange(capacity, dtype=f32)[None, None, :, None]
    )
    gate_slot = jnp.sum(jnp.where(select, gate_own[:, :, None, :], 0.0), axis=3)
    select = select.astype(bf16)

    inputs = tokens[0].astype(f32)
    upstream = cotangent[0].astype(f32)
    seq_rows = jnp.concatenate(gather_seq(tokens[0]), axis=0).astype(f32)
    scale_all = rms_scale(seq_rows)
    normed_one = (seq_rows * scale_all * gain_one).astype(bf16)
    raw = seq_absolute(dot(normed_one, w_own))
    seg = segments[0]
    place = jnp.arange(length, dtype=jnp.int32)
    earlier = jnp.sum((seg[None, :] < seg[:, None]).astype(jnp.int32), axis=1)
    cosine, sine = rope_tables(place - earlier)
    queries = rotate(
        raw[:, :Q_OWN].reshape(length, GROUP, HEAD_DIM), cosine[:, None], sine[:, None]
    ).astype(bf16)
    keys = rotate(raw[:, Q_OWN : Q_OWN + HEAD_DIM], cosine, sine).astype(bf16)
    values = raw[:, Q_OWN + HEAD_DIM :].astype(bf16)
    allowed = (seg[None, :] == seg[:, None]) & (place[None, :] <= place[:, None])
    scores = jnp.einsum("qgd,td->gqt", queries, keys, preferred_element_type=f32) * score_scale
    scores = jnp.where(allowed[None], scores, masked_score)
    row_max = jnp.max(scores, axis=-1, keepdims=True)
    exp_scores = jnp.exp(scores - row_max)
    denominator = jnp.sum(exp_scores, axis=-1, keepdims=True)
    soft = exp_scores / denominator
    soft_low = soft.astype(bf16)
    mixed = jnp.einsum("gqt,td->qgd", soft_low, values, preferred_element_type=f32)
    mixed = seq_relative(mixed.reshape(length, Q_OWN).astype(bf16))
    partial = dot(mixed, w_out_own).astype(bf16)
    hidden = inputs + reduce_seq([partial[k * rows : (k + 1) * rows] for k in range(8)])

    scale_two = rms_scale(hidden)
    normed_two = (hidden * scale_two * gain_two).astype(bf16)
    normed_all = lax.all_gather(normed_two, BATCH, axis=0)
    expert_in = jnp.einsum(
        "ebct,btd->ebcd", select, normed_all, preferred_element_type=f32
    ).astype(bf16)
    expert_in = expert_in.reshape(2, -1, features)
    grad_rows = jnp.einsum("ebct,btd->ebcd", select, grad_all, preferred_element_type=f32)
    grad_rows = (grad_rows * gate_slot[..., None]).astype(bf16).reshape(2, -1, features)
    gate_pre = jnp.einsum("ecd,edf->ecf", expert_in, gate_full, preferred_element_type=f32)
    up_pre = jnp.einsum("ecd,edf->ecf", expert_in, up_full, preferred_element_type=f32)
    sigmoid_gate = jax.nn.sigmoid(gate_pre)
    activated = (gate_pre * sigmoid_gate * up_pre).astype(bf16)
    grad_act = jnp.einsum("ecd,efd->ecf", grad_rows, down_full, preferred_element_type=f32)
    grad_gate_pre = (
        grad_act * up_pre * sigmoid_gate * (1.0 + gate_pre * (1.0 - sigmoid_gate))
    ).astype(bf16)
    grad_up_pre = (grad_act * gate_pre * sigmoid_gate).astype(bf16)
    grad_in = jnp.einsum("ecf,edf->ecd", grad_gate_pre, gate_full, preferred_element_type=f32)
    grad_in = grad_in + jnp.einsum(
        "ecf,edf->ecd", grad_up_pre, up_full, preferred_element_type=f32
    )
    grad_in = grad_in.astype(bf16).reshape(2, 16, capacity, features)
    grad_part = jnp.einsum("ebct,ebcd->btd", select, grad_in, preferred_element_type=f32)
    grad_part = to_relative(grad_part.astype(bf16).reshape(2, 4, 2, rows, features), BATCH)
    grad_normed_two = reduce_batch(grad_part)

    expert_out = jnp.einsum("ecf,efd->ecd", activated, down_full, preferred_element_type=f32)
    expert_out = expert_out.reshape(2, 16, capacity, features) * gate_slot[..., None]
    out_part = jnp.einsum(
        "ebct,ebcd->btd", select, expert_out.astype(bf16), preferred_element_type=f32
    )
    out_part = to_relative(out_part.astype(bf16).reshape(2, 4, 2, rows, features), BATCH)
    output = hidden + reduce_batch(out_part)

    grad_down = jnp.einsum("ecf,ecd->efd", activated, grad_rows, preferred_element_type=f32)
    grad_gate = jnp.einsum("ecd,ecf->edf", expert_in, grad_gate_pre, preferred_element_type=f32)
    grad_up = jnp.einsum("ecd,ecf->edf", expert_in, grad_up_pre, preferred_element_type=f32)

    def reduce_expert(grad):
        shape = grad.shape
        parts = grad.astype(bf16).reshape(2, 2, 4, shape[1] // 8, shape[2])
        parts = to_relative(jnp.transpose(parts, (1, 2, 0, 3, 4)), SEQ)
        parts = parts.reshape((8, 2, shape[1] // 8, shape[2]))
        return reduce_seq([parts[k] for k in range(8)])

    sum_down = reduce_expert(grad_down)
    sum_gate = reduce_expert(grad_gate)
    sum_up = reduce_expert(grad_up)

    scaled_two = gain_two * grad_normed_two
    grad_gain_two = jnp.sum(grad_normed_two * hidden * scale_two, axis=0)
    grad_hidden = (
        upstream
        + scale_two * scaled_two
        - hidden * scale_two**3 * jnp.mean(scaled_two * hidden, axis=-1, keepdims=True)
    )
    grad_z = jnp.concatenate(gather_seq(grad_hidden.astype(bf16)), axis=0)
    grad_mixed = jnp.einsum("td,fd->tf", grad_z, w_out_own, preferred_element_type=f32)
    grad_mixed = seq_absolute(grad_mixed.astype(bf16)).reshape(length, GROUP, HEAD_DIM)
    grad_out_w = dot(mixed.T, grad_z)
    grad_soft = jnp.einsum("qgd,td->gqt", grad_mixed, values, preferred_element_type=f32)
    row_dot = jnp.sum(soft * grad_soft, axis=-1, keepdims=True)
    grad_scores = (soft * (grad_soft - row_dot)).astype(bf16)
    grad_query = (
        jnp.einsum("gqt,td->qgd", grad_scores, keys, preferred_element_type=f32) * score_scale
    )
    grad_key = (
        jnp.einsum("gqt,qgd->td", grad_scores, queries, preferred_element_type=f32) * score_scale
    )
    grad_value = jnp.einsum("gqt,qgd->td", soft_low, grad_mixed, preferred_element_type=f32)
    grad_query = rotate(grad_query, cosine[:, None], -sine[:, None])
    grad_key = rotate(grad_key, cosine, -sine)
    grad_raw = jnp.concatenate(
        [grad_query.reshape(length, Q_OWN), grad_key, grad_value], axis=1
    ).astype(bf16)
    grad_raw = seq_relative(grad_raw)
    grad_normed_part = jnp.einsum("tf,df->td", grad_raw, w_own, preferred_element_type=f32)
    gain_one_part = jnp.sum(grad_normed_part * seq_rows * scale_all, axis=0)
    grad_normed_part = grad_normed_part.astype(bf16)
    grad_normed_one = reduce_seq([grad_normed_part[k * rows : (k + 1) * rows] for k in range(8)])
    scaled_one = gain_one * grad_normed_one
    scale_one = rms_scale(inputs)
    grad_inputs = (
        grad_hidden
        + scale_one * scaled_one
        - inputs * scale_one**3 * jnp.mean(scaled_one * inputs, axis=-1, keepdims=True)
    )

    grad_own = dot(normed_one.T, grad_raw)
    gain_cols = jnp.stack([gain_one_part, grad_gain_two], axis=1)
    grad_own = jnp.concatenate([grad_own, jnp.pad(gain_cols, ((0, 0), (0, 62)))], axis=1)
    grad_own = grad_own.astype(bf16).reshape(8, part, wide)
    grad_own = lax.all_to_all(grad_own, SEQ, 0, 0, tiled=True)
    grad_own = jnp.swapaxes(grad_own, 0, 1)
    gain_sum = jnp.sum(grad_own[:, :, 320:].astype(f32), axis=1).astype(bf16)
    grad_cols = jnp.concatenate(
        [
            grad_own[:, :, :Q_OWN].reshape(part, 1536),
            grad_own[:, :, Q_OWN : Q_OWN + HEAD_DIM].reshape(part, 512),
            grad_own[:, :, Q_OWN + HEAD_DIM : 320].reshape(part, 512),
            jnp.pad(gain_sum, ((0, 0), (0, 64))),
        ],
        axis=1,
    )

    def reduce_rows(grad):
        parts = grad.astype(bf16).reshape(2, 4, 2, part // 16, grad.shape[1])
        return reduce_batch(to_relative(parts, BATCH))

    sum_out = reduce_rows(grad_out_w)
    sums = reduce_rows(grad_cols)
    return (
        output.astype(bf16)[None],
        grad_inputs.astype(bf16)[None],
        sums[:, :1536],
        sums[:, 1536:2048],
        sums[:, 2048:2560],
        sum_out,
        sums[:, 2560],
        sums[:, 2561],
        sum_gate,
        sum_up,
        sum_down,
    )


def solution(mesh):
    fine = Mesh(mesh.devices.reshape(2, 4, 2, 4, 2), SEQ + BATCH)
    both = SEQ + BATCH
    placed = (
        P(BATCH, SEQ, None),
        P(BATCH, SEQ, None),
        P(BATCH, None),
        P(BATCH, SEQ, None),
        P(BATCH, SEQ, None),
        P(both, None),
        P(both, None),
        P(both, None),
        P(both, None),
        P(both),
        P(both),
        P(BATCH, SEQ, None),
        P(BATCH, SEQ, None),
        P(BATCH, SEQ, None),
    )
    return jax.shard_map(
        shards,
        mesh=fine,
        in_specs=placed,
        out_specs=(
            P(BATCH, SEQ, None),
            P(BATCH, SEQ, None),
            P(both, None),
            P(both, None),
            P(both, None),
            P(both, None),
            P(both),
            P(both),
            P(BATCH, SEQ, None),
            P(BATCH, SEQ, None),
            P(BATCH, SEQ, None),
        ),
        check_vma=False,
    )
```

```python
import jax
import jax.numpy as jnp
from jax import lax
from jax.experimental import pallas as pl
from jax.experimental.pallas import tpu as pltpu
from jax.sharding import Mesh, PartitionSpec as P

HEAD_DIM = 64
TOPK = 8
GROUP = 3
Q_OWN = GROUP * HEAD_DIM
TOK = 128
HALF = 512
D = 1536
EXPERTS = 32
norm_eps = 1e-06
rope_base = 10000.0
masked_score = -1e30
SEQ = ("yh", "x")
BATCH = ("yl", "z", "c")
SIZE = {"yh": 2, "x": 4, "yl": 2, "z": 4, "c": 2}
bf16 = jnp.bfloat16
f32 = jnp.float32


def dot(a, b):
    return jnp.dot(a, b, preferred_element_type=f32)


def shift(value, axis, by):
    size = SIZE[axis]
    return lax.ppermute(value, axis, [(i, (i + by) % size) for i in range(size)])


def ring_pieces(block, axis):
    half = block.shape[0] // 2
    below = shift(block, axis, 1)
    above = shift(block, axis, -1)
    low = shift(below[:half], axis, 1)
    high = shift(above[half:], axis, -1)
    return block, above, low, high, below


def add_up(*parts):
    total = parts[0].astype(f32)
    for part in parts[1:]:
        total = total + part.astype(f32)
    return total


def ring_send(blocks, axis):
    half = blocks[0].shape[0] // 2
    return shift(blocks[2][:half], axis, 1), shift(blocks[2][half:], axis, -1)


def ring_add(blocks, got):
    half = blocks[0].shape[0] // 2
    up = [add_up(blocks[1][:half], got[0]).astype(bf16), blocks[1][half:]]
    down = [blocks[3][:half], add_up(blocks[3][half:], got[1]).astype(bf16)]
    return jnp.concatenate(up, axis=0), jnp.concatenate(down, axis=0)


def ring_next(hops, axis):
    return shift(hops[0], axis, 1), shift(hops[1], axis, -1)


def reduce_ring(blocks, axis):
    hops = ring_add(blocks, ring_send(blocks, axis))
    return add_up(blocks[0], *ring_next(hops, axis))


def reduce_plane(blocks, ring, pair):
    total = reduce_ring(blocks, ring)
    return add_up(total[0], shift(total[1].astype(bf16), pair, 1))


def reduce_batch(near, across):
    held = add_up(near, shift(across, "c", 1)).astype(bf16)
    return reduce_plane(held.reshape((4, 2) + near.shape[1:]), "z", "yl")


def tie(*values):
    return lax.optimization_barrier(values)


def ahead(axis, by):
    return lax.rem(lax.axis_index(axis) + by, SIZE[axis])


def distance(axis, place):
    return lax.rem(place - lax.axis_index(axis) + SIZE[axis], SIZE[axis])


def dot_nt(a, b):
    return lax.dot_general(a, b, (((1,), (1,)), ((), ())), preferred_element_type=f32)


def dot_tn(a, b):
    return lax.dot_general(a, b, (((0,), (0,)), ((), ())), preferred_element_type=f32)


def whole(shape):
    zeros = (0,) * len(shape)
    return pl.BlockSpec(shape, lambda *_: zeros)


def once(shape):
    zeros = (0,) * len(shape)
    return pl.BlockSpec(shape, lambda *_: zeros, pipeline_mode=pl.Buffered(1))


def run(body, out_shapes, in_specs, out_specs, grid, args, prefetch=None, scratch=(), micros=0):
    spec = pltpu.PrefetchScalarGridSpec(
        num_scalar_prefetch=0 if prefetch is None else 1,
        grid=grid,
        in_specs=in_specs,
        out_specs=out_specs,
        scratch_shapes=list(scratch),
    )
    head = () if prefetch is None else (prefetch,)
    return pl.pallas_call(
        body,
        grid_spec=spec,
        out_shape=out_shapes,
        compiler_params=pltpu.CompilerParams(vmem_limit_bytes=56 << 20),
        cost_estimate=pl.CostEstimate(flops=1100000000 * micros, bytes_accessed=0, transcendentals=0),
    )(*head, *args)


def struct(shape, dtype):
    return jax.ShapeDtypeStruct(shape, dtype)


def turned(values):
    lane = lax.broadcasted_iota(jnp.int32, values.shape, 1)
    first = (lane % HEAD_DIM) < HEAD_DIM // 2
    return jnp.where(first, -pltpu.roll(values, 96, 1), pltpu.roll(values, 32, 1))


def by_lanes(values, function):
    width = values.shape[1]
    return jnp.concatenate(
        [function(values[:, k : k + 128]) for k in range(0, width, 128)], axis=1
    )


def prepare_body(where, own, above, far_low, far_high, below, moving, xp_ref, scale_ref):
    for k in range(4):
        place = pl.ds(lax.rem(where[0] + k, 4) * TOK, TOK)
        if k == 2:
            block = jnp.concatenate([far_low[...], far_high[...]], axis=0)
        else:
            block = (own, above, None, below)[k][...]
        wide = block.astype(f32)
        scale = lax.rsqrt(jnp.mean(wide * wide, axis=1, keepdims=True) + norm_eps)
        scale_ref[place, :] = jnp.broadcast_to(scale, (TOK, 128))
        xp_ref[place, :] = dot(block, moving[...]).astype(bf16)


def prepare(where, pieces, moving):
    specs = [whole(p.shape) for p in pieces] + [whole(moving.shape)]
    return run(
        prepare_body,
        [struct((HALF, D), bf16), struct((HALF, 128), f32)],
        specs,
        [whole((HALF, D)), whole((HALF, 128))],
        (1,),
        (*pieces, moving),
        prefetch=where,
        micros=7,
    )


def project_body(xp, scale, weight, cosine, sine, n_ref, q_ref, kv_ref, sent_ref):
    pick = lax.broadcasted_iota(jnp.int32, (8, 128), 0) == lax.broadcasted_iota(
        jnp.int32, (8, 128), 1
    )
    gains = dot_nt(pick.astype(bf16), weight[:, 640:])
    normed = (xp[...].astype(f32) * scale[:, :1] * gains[:1]).astype(bf16)
    n_ref[...] = normed
    raw = dot(normed, weight[:, :640])
    cos, sin = cosine[...], sine[...]
    rotated = by_lanes(raw[:, :512], lambda u: u * cos + turned(u) * sin).astype(bf16)
    q_ref[...] = rotated[:, :384]
    both = jnp.concatenate([rotated[:, 384:], raw[:, 512:].astype(bf16)], axis=1)
    kv_ref[...] = both
    sent_ref[...] = swap_groups(both)


def swap_groups(both):
    wide = both.astype(f32)
    return by_lanes(wide, lambda u: pltpu.roll(u, 64, 1)).astype(bf16)


def tile(width):
    return pl.BlockSpec((TOK, width), lambda i, *_: (i, 0))


def project(xp, scale, gathered, cosine, sine):
    return run(
        project_body,
        [
            struct((HALF, D), bf16),
            struct((HALF, 384), bf16),
            struct((HALF, 256), bf16),
            struct((HALF, 256), bf16),
        ],
        [whole((HALF, D)), whole((HALF, 128)), whole((D, 768)), whole((HALF, 128)), whole((HALF, 128))],
        [whole((HALF, D)), whole((HALF, 384)), whole((HALF, 256)), whole((HALF, 256))],
        (1,),
        (xp, scale, gathered, cosine, sine),
        micros=5,
    )


def softmax_parts(where, step, q, own, other, seg_col, seg_row, group):
    place = lax.rem(where[0] + step, 4) * TOK
    row = lax.broadcasted_iota(jnp.int32, (TOK, HALF), 0) + place
    key = lax.broadcasted_iota(jnp.int32, (TOK, HALF), 1)
    segs = seg_col[:, :1]
    own_ok = (segs == seg_row[:, :HALF]) & (key <= row)
    other_ok = (segs == seg_row[:, HALF:]) & (where[1] == 1)
    first = group * HEAD_DIM
    heads = [q[:, (3 * group + h) * HEAD_DIM : (3 * group + h + 1) * HEAD_DIM] for h in range(3)]
    queries = jnp.concatenate(heads, axis=0) * jnp.asarray(0.125, bf16)
    scores = []
    for kv, ok in ((own, own_ok), (other, other_ok)):
        s = dot_nt(queries, kv[:, first : first + HEAD_DIM]).reshape(3, TOK, HALF)
        scores.append(jnp.where(ok[None], s, masked_score))
    top = jnp.maximum(
        jnp.max(scores[0], axis=2, keepdims=True), jnp.max(scores[1], axis=2, keepdims=True)
    )
    exps = [jnp.exp(s - top) for s in scores]
    total = jnp.sum(exps[0], axis=2, keepdims=True) + jnp.sum(exps[1], axis=2, keepdims=True)
    inverse = 1.0 / total
    return queries, [(e * inverse).reshape(3 * TOK, HALF) for e in exps]


def attend_body(where, q, own, other, seg_col, seg_row, w_own, w_other, att_ref, part_ref):
    step = pl.program_id(0)
    columns = []
    for group in range(2):
        _, probs = softmax_parts(where, step, q[...], own, other, seg_col, seg_row, group)
        first = 128 + group * HEAD_DIM
        mixed = dot(probs[0].astype(bf16), own[:, first : first + HEAD_DIM])
        mixed = mixed + dot(probs[1].astype(bf16), other[:, first : first + HEAD_DIM])
        columns += [mixed[h * TOK : (h + 1) * TOK] for h in range(3)]
    att = jnp.concatenate(columns, axis=1).astype(bf16)
    att_ref[...] = att
    part = dot(att[:, :Q_OWN], w_own[...]) + dot(att[:, Q_OWN:], w_other[...])
    part_ref[0] = part.astype(bf16)


def turn(width):
    return pl.BlockSpec((TOK, width), lambda i, where: (lax.rem(where[0] + i, 4), 0))


def step_block(shape):
    return pl.BlockSpec((1,) + shape, lambda i, *_: (i, 0, 0))


def attend(where, q, own, other, seg_col, seg_row, w_own, w_other):
    return run(
        attend_body,
        [struct((HALF, 384), bf16), struct((4, TOK, D), bf16)],
        [
            turn(384),
            whole((HALF, 256)),
            whole((HALF, 256)),
            turn(128),
            whole((1, 2 * HALF)),
            whole((Q_OWN, D)),
            whole((Q_OWN, D)),
        ],
        [turn(384), step_block((TOK, D))],
        (4,),
        (q, own, other, seg_col, seg_row, w_own, w_other),
        prefetch=where,
        micros=15,
    )


def attend_back_body(
    where, q, att, own, other, seg_col, seg_row, w_own, w_other, z0, z1, z2a, z2b, z3, cosine,
    sine, q_ref, own_ref, sent_ref, out_ref, sums, out_sum, z,
):
    step = pl.program_id(0)
    for k, pieces in enumerate(((z0,), (z1,), (z2a, z2b), (z3,))):

        @pl.when(step == k)
        def _(pieces=pieces):
            rows = TOK // len(pieces)
            for n, piece in enumerate(pieces):
                z[n * rows : (n + 1) * rows, :] = piece[...]

    @pl.when(step == 0)
    def _():
        sums[...] = jnp.zeros_like(sums)
        out_sum[...] = jnp.zeros_like(out_sum)

    place = pl.ds(lax.rem(where[0] + step, 4) * TOK, TOK)
    grad_z = z[...]
    out_sum[...] += dot_tn(att[...], grad_z)
    grad_att = jnp.concatenate([dot_nt(grad_z, w_own[...]), dot_nt(grad_z, w_other[...])], axis=1)
    grad_att = grad_att.astype(bf16)
    columns, keys, values = [], [[], []], [[], []]
    for group in range(2):
        queries, probs = softmax_parts(where, step, q[...], own, other, seg_col, seg_row, group)
        grads = jnp.concatenate(
            [
                grad_att[:, (3 * group + h) * HEAD_DIM : (3 * group + h + 1) * HEAD_DIM]
                for h in range(3)
            ],
            axis=0,
        )
        first = group * HEAD_DIM
        grad_probs = [dot_nt(grads, kv[:, 128 + first : 192 + first]) for kv in (own, other)]
        row_dot = jnp.sum(probs[0] * grad_probs[0], axis=1, keepdims=True)
        row_dot = row_dot + jnp.sum(probs[1] * grad_probs[1], axis=1, keepdims=True)
        total = None
        for n, kv in enumerate((own, other)):
            grad_score = (probs[n] * (grad_probs[n] - row_dot)).astype(bf16)
            term = dot(grad_score, kv[:, first : first + HEAD_DIM])
            total = term if total is None else total + term
            keys[n].append(dot_tn(grad_score, queries))
            values[n].append(dot_tn(probs[n].astype(bf16), grads))
        total = total * 0.125
        columns += [total[h * TOK : (h + 1) * TOK] for h in range(3)]
    for n in range(2):
        sums[n] += jnp.concatenate(keys[n] + values[n], axis=1)
    grad_q = jnp.concatenate(columns, axis=1)
    cos, sin = cosine[place, :], sine[place, :]
    q_ref[...] = by_lanes(grad_q, lambda u: u * cos - turned(u) * sin).astype(bf16)

    @pl.when(step == 3)
    def _():
        out_ref[...] = out_sum[...].astype(bf16)
        for n in range(2):
            at = slice(n * HALF, (n + 1) * HALF)
            grad_k = sums[n, :, :128]
            grad_k = grad_k * cosine[at, :] - turned(grad_k) * sine[at, :]
            both = jnp.concatenate([grad_k, sums[n, :, 128:]], axis=1)
            if n == 0:
                own_ref[...] = both
            else:
                sent_ref[...] = swap_groups(both)


def attend_back(where, q, att, own, other, seg_col, seg_row, w_own, w_other, pieces, cosine, sine):
    return run(
        attend_back_body,
        [
            struct((HALF, 384), bf16),
            struct((HALF, 256), f32),
            struct((HALF, 256), bf16),
            struct((384, D), bf16),
        ],
        [
            turn(384),
            turn(384),
            whole((HALF, 256)),
            whole((HALF, 256)),
            turn(128),
            whole((1, 2 * HALF)),
            whole((Q_OWN, D)),
            whole((Q_OWN, D)),
        ]
        + [whole(p.shape) for p in pieces]
        + [whole((2 * HALF, 128)), whole((2 * HALF, 128))],
        [turn(384), whole((HALF, 256)), whole((HALF, 256)), whole((384, D))],
        (4,),
        (q, att, own, other, seg_col, seg_row, w_own, w_other, *pieces, cosine, sine),
        prefetch=where,
        scratch=[
            pltpu.VMEM((2, HALF, 256), f32),
            pltpu.VMEM((384, D), f32),
            pltpu.VMEM((TOK, D), bf16),
        ],
        micros=22,
    )


def unproject_body(where, q, own, got, weight, moving, xp, scale, raw_ref, part_ref, gain_ref):
    both = (own[...] + got[...].astype(f32)).astype(bf16)
    raw = jnp.concatenate([q[...], both], axis=1)
    raw_ref[...] = raw
    grad = dot_nt(raw, weight[:, :640])
    term = jnp.sum(grad * (xp[...].astype(f32) * scale[:, :1]), axis=0, keepdims=True)
    gain_ref[...] = jnp.broadcast_to(term, (8, D))
    part = dot_nt(grad.astype(bf16), moving[...]).astype(bf16)
    for k in range(4):
        part_ref[lax.rem(k + 4 - where[0], 4)] = part[k * TOK : (k + 1) * TOK]


def unproject(where, q, own, got, gathered, moving, xp, scale):
    return run(
        unproject_body,
        [struct((HALF, 640), bf16), struct((4, TOK, D), bf16), struct((8, D), f32)],
        [
            whole((HALF, 384)),
            whole((HALF, 256)),
            whole((HALF, 256)),
            whole((D, 768)),
            whole((D, D)),
            whole((HALF, D)),
            whole((HALF, 128)),
        ],
        [whole((HALF, 640)), whole((4, TOK, D)), whole((8, D))],
        (1,),
        (q, own, got, gathered, moving, xp, scale),
        prefetch=where,
        micros=10,
    )


def weight_grad_body(order, normed, raw, gains, out_rows, out_ref):
    step = pl.program_id(0)
    grad = dot_tn(normed[...], raw[...]).astype(bf16)
    pick = lax.broadcasted_iota(jnp.int32, (8, 128), 0) == lax.broadcasted_iota(
        jnp.int32, (8, 128), 1
    )
    columns = dot_tn(gains[...].astype(bf16), pick.astype(bf16)).astype(bf16)
    for k in range(4):
        at = slice(k * 96, (k + 1) * 96)
        to = order[step * 4 + k]
        out_ref[to, :, :640] = grad[at]
        out_ref[to, :, 640:768] = columns[at]
        out_ref[to, :, 768:] = out_rows[k]


def weight_grad(order, normed, raw, gains, out_rows):
    return run(
        weight_grad_body,
        [struct((16, 96, 1152), bf16)],
        [
            pl.BlockSpec((HALF, 384), lambda i, *_: (0, i)),
            whole((HALF, 640)),
            pl.BlockSpec((8, 384), lambda i, *_: (0, i)),
            pl.BlockSpec((4, 96, 384), lambda i, *_: (i, 0, 0)),
        ],
        [whole((16, 96, 1152))],
        (4,),
        (normed, raw, gains, out_rows),
        prefetch=order,
        micros=6,
    )[0]


CAP = 48
BLOCKS = 8
NEAR = BLOCKS // 2
STEP = BLOCKS * CAP


def choices(gates):
    hit = gates > 0
    upper = lax.broadcasted_iota(jnp.int32, (TOK, TOK), 0) <= lax.broadcasted_iota(
        jnp.int32, (TOK, TOK), 1
    )
    count = dot(hit.astype(bf16), upper.astype(bf16))
    slot = lax.broadcasted_iota(jnp.int32, (CAP, TOK), 0).astype(f32) + 1.0
    picks, weights = [], []
    for e in range(2):
        pick = (count[e : e + 1] == slot) & hit[e : e + 1]
        picks.append(pick.astype(bf16))
        weights.append(jnp.sum(jnp.where(pick, gates[e : e + 1], 0.0), axis=1, keepdims=True))
    return jnp.concatenate(picks, axis=0), jnp.concatenate(weights, axis=0)


def experts_body(order, *refs):
    rows, grads, gates = (refs[k * BLOCKS : (k + 1) * BLOCKS] for k in range(3))
    w_gate, w_up, w_down = refs[3 * BLOCKS : 3 * BLOCKS + 3]
    near_ref, across_ref, in_ref, grad_ref, act_ref, da_ref, db_ref = refs[3 * BLOCKS + 3 :]
    picks = []
    for j in range(BLOCKS):
        pick, weight = choices(gates[j][0])
        picks.append(pick)
        taken = dot(pick, rows[j][0]).astype(bf16)
        graded = (dot(pick, grads[j][0]) * weight).astype(bf16)
        for e in range(2):
            at = slice(j * CAP, (j + 1) * CAP)
            in_ref[e, at, :] = taken[e * CAP : (e + 1) * CAP]
            grad_ref[e, at, :] = graded[e * CAP : (e + 1) * CAP]
    backs = []
    for e in range(2):
        taken, graded = in_ref[e], grad_ref[e]
        gate_pre = dot(taken, w_gate[e])
        up_pre = dot(taken, w_up[e])
        grad_act = dot_nt(graded, w_down[e])
        sig = 1.0 / (1.0 + jnp.exp(-gate_pre))
        silu = gate_pre * sig
        act_ref[e] = (silu * up_pre).astype(bf16)
        da = (grad_act * up_pre * sig * (1.0 + gate_pre * (1.0 - sig))).astype(bf16)
        db = (grad_act * silu).astype(bf16)
        da_ref[e] = da
        db_ref[e] = db
        backs.append((dot_nt(da, w_gate[e]) + dot_nt(db, w_up[e])).astype(bf16))
    for j in range(BLOCKS):
        at = slice(j * CAP, (j + 1) * CAP)
        back = dot_tn(picks[j], jnp.concatenate([backs[0][at], backs[1][at]], axis=0))
        target = near_ref if j < NEAR else across_ref
        target[j % NEAR] = back.astype(bf16)


def block_at(j, shape):
    def index(i, order):
        return (order[i * BLOCKS + j],) + (0,) * len(shape)

    return pl.BlockSpec((1,) + shape, index)


def expert_rows(width):
    return pl.BlockSpec((2, STEP, width), lambda i, *_: (0, i, 0))


def pair_block():
    return pl.BlockSpec((NEAR, TOK, D), lambda i, *_: (i, 0, 0))


def experts(order, rows, grads, gates, w_gate, w_up, w_down):
    slots = 16 * CAP
    return run(
        experts_body,
        [struct((8, TOK, D), bf16)] * 2
        + [struct((2, slots, D), bf16)] * 2
        + [struct((2, slots, 512), bf16)] * 3,
        [block_at(j, (TOK, D)) for j in range(BLOCKS)]
        + [block_at(j, (TOK, D)) for j in range(BLOCKS)]
        + [block_at(j, (2, TOK)) for j in range(BLOCKS)]
        + [once(w.shape) for w in (w_gate, w_up, w_down)],
        [pair_block(), pair_block(), expert_rows(D), expert_rows(D)] + [expert_rows(512)] * 3,
        (16 // BLOCKS,),
        (rows,) * BLOCKS + (grads,) * BLOCKS + (gates,) * BLOCKS + (w_gate, w_up, w_down),
        prefetch=order,
        micros=30,
    )


def expert_out_body(order, *refs):
    gates = refs[:BLOCKS]
    act, w_down, near_ref, across_ref = refs[BLOCKS:]
    outs = [dot(act[e], w_down[e]) for e in range(2)]
    for j in range(BLOCKS):
        pick, weight = choices(gates[j][0])
        at = slice(j * CAP, (j + 1) * CAP)
        both = jnp.concatenate([outs[0][at], outs[1][at]], axis=0) * weight
        target = near_ref if j < NEAR else across_ref
        target[j % NEAR] = dot_tn(pick, both.astype(bf16)).astype(bf16)


def expert_out(order, gates, act, w_down):
    slots = 16 * CAP
    return run(
        expert_out_body,
        [struct((8, TOK, D), bf16)] * 2,
        [block_at(j, (2, TOK)) for j in range(BLOCKS)] + [expert_rows(512), once(w_down.shape)],
        [pair_block(), pair_block()],
        (16 // BLOCKS,),
        (gates,) * BLOCKS + (act, w_down),
        prefetch=order,
        micros=13,
    )


def expert_grad_body(order, taken, graded, act, da, db, gate_ref, up_ref, down_ref):
    e = pl.program_id(0)
    gate_ref[0] = dot_tn(taken[0], da[0]).astype(bf16)
    up = dot_tn(taken[0], db[0]).astype(bf16)
    down_ref[0] = dot_tn(act[0], graded[0]).astype(bf16)
    for k in range(8):
        up_ref[order[k], e] = up[k * 192 : (k + 1) * 192]


def expert_grad(order, taken, graded, act, da, db):
    slots = 16 * CAP

    def one(rows, width):
        return pl.BlockSpec((1, rows, width), lambda e, *_: (e, 0, 0))

    return run(
        expert_grad_body,
        [struct((2, D, 512), bf16), struct((8, 2, 192, 512), bf16), struct((2, 512, D), bf16)],
        [one(slots, D), one(slots, D), one(slots, 512), one(slots, 512), one(slots, 512)],
        [one(D, 512), whole((8, 2, 192, 512)), one(512, D)],
        (2,),
        (taken, graded, act, da, db),
        prefetch=order,
        micros=14,
    )


def rms_scale(values):
    return lax.rsqrt(jnp.mean(values * values, axis=-1, keepdims=True) + norm_eps)


def three_parts(values):
    high = lax.reduce_precision(values, 8, 7)
    rest = values - high
    middle = lax.reduce_precision(rest, 8, 7)
    return [v.astype(bf16) for v in (high, middle, rest - middle)]


def shards(
    tokens,
    cotangent,
    segments,
    routes,
    gate_weights,
    w_query,
    w_key,
    w_value,
    w_out,
    norm_one,
    norm_two,
    w_gate,
    w_up,
    w_down,
):
    inputs = tokens[0].astype(f32)
    upstream = cotangent[0].astype(f32)
    yh, x = lax.axis_index("yh"), lax.axis_index("x")
    where = jnp.stack([x, yh]).astype(jnp.int32)
    order = jnp.stack(
        [
            (ahead("yl", m % 2) * 4 + ahead("z", m // 2)) * 2 + ahead("c", j // NEAR)
            for i in range(16 // BLOCKS)
            for j in range(BLOCKS)
            for m in (NEAR * i + j % NEAR,)
        ]
    ).astype(jnp.int32)
    batch_place = jnp.stack(
        [
            distance("c", b % 2) * 8 + distance("z", b // 2 % 4) * 2 + distance("yl", b // 8)
            for b in range(16)
        ]
    ).astype(jnp.int32)
    seq_place = jnp.stack(
        [distance("x", s % 4) * 2 + distance("yh", s // 4) for s in range(8)]
    ).astype(jnp.int32)

    def for_heads(weight, width):
        by_head = jnp.swapaxes(weight.reshape(-1, 8, width), 0, 1)
        return [by_head, jnp.concatenate([by_head[4:], by_head[:4]], axis=0)]

    gains = jnp.pad(jnp.stack([norm_one, norm_two], axis=1), ((0, 0), (0, 126)))
    strip = jnp.concatenate(
        for_heads(w_query, Q_OWN)
        + for_heads(w_key, HEAD_DIM)
        + for_heads(w_value, HEAD_DIM)
        + [jnp.broadcast_to(gains[None], (8,) + gains.shape)],
        axis=2,
    )
    strip = lax.all_to_all(strip, SEQ, 0, 0, tiled=True).reshape(96, 768)
    expert_ids = jnp.arange(EXPERTS, dtype=jnp.int32)[:, None, None]
    gate_dense = jnp.sum(jnp.where(routes[0][None] == expert_ids, gate_weights[0][None], 0.0), axis=2)
    strip = jnp.concatenate(
        [
            strip,
            jnp.concatenate(three_parts(gate_dense), axis=0),
            w_out.reshape(96, 192),
            shift(w_out, "yh", 1).reshape(96, 192),
        ],
        axis=1,
    )
    gathered = lax.all_gather(strip, BATCH, axis=0, tiled=True)
    grad_all = lax.all_gather(cotangent[0], BATCH, axis=0)

    feature = jnp.arange(D, dtype=jnp.int32)
    moved = feature % 192 // 12 * 96 + feature // 192 * 12 + feature % 12
    moving = (moved[:, None] == feature[None, :]).astype(bf16)
    pieces = ring_pieces(tokens[0], "x")
    xp, scale_half = prepare(where, pieces, moving)

    pack = jnp.concatenate([w_gate, w_up], axis=1)
    half_pack = pack.shape[1] // 2
    pack, _ = tie(pack, strip)
    pack_other = shift(pack, "yh", 1)
    pack, w_down, _, _ = tie(pack, w_down, pieces[2], pieces[3])
    down_below = shift(w_down, "x", 1)
    down_above = shift(w_down, "x", -1)
    pack_below = shift(pack, "x", 1)
    pack_above = shift(pack, "x", -1)

    def natural(row):
        return jnp.swapaxes(row.reshape(16, 8, 12), 0, 1).reshape(D)

    place = jnp.arange(2 * HALF, dtype=jnp.int32) + HALF * yh
    place = jnp.where(place >= 2 * HALF, place - 2 * HALF, place)
    seg = jnp.roll(segments[0], -HALF * yh)
    earlier = jnp.sum((seg[None, :] < seg[:, None]).astype(jnp.int32), axis=1)
    freq_index = jnp.arange(HEAD_DIM // 2, dtype=f32) * (2.0 / HEAD_DIM)
    frequency = jnp.tile(rope_base ** (-freq_index), 4)
    angle = (place - earlier).astype(f32)[:, None] * frequency
    cosine, sine = jnp.cos(angle), jnp.sin(angle)
    seg_row = seg[None, :]
    seg_col = jnp.broadcast_to(seg[:HALF, None], (HALF, 128))

    gathered, xp, pack_other, pack_below, pack_above, down_below, down_above = tie(
        gathered, xp, pack_other, pack_below, pack_above, down_below, down_above
    )
    down_low = shift(down_below[:1], "x", 1)
    down_high = shift(down_above[1:], "x", -1)
    pack_low = shift(pack_below[:, :half_pack], "x", 1)
    pack_high = shift(pack_above[:, half_pack:], "x", -1)

    normed, queries, own, sent = project(xp, scale_half, gathered, cosine, sine)
    other = shift(sent, "yh", 1)
    out_rows = gathered[:, 896:1088].reshape(192, D)
    out_other = gathered[:, 1088:].reshape(192, D)
    gain_one = natural(gathered[:, 640].astype(f32))
    gain_two = natural(gathered[:, 641].astype(f32))
    gates = jnp.sum(gathered[:, 768:896].reshape(16, 3, EXPERTS, TOK).astype(f32), axis=1)
    gates = lax.dynamic_slice_in_dim(gates, lax.axis_index(BATCH) * 2, 2, axis=1)
    mixed, partial = attend(where, queries, own, other, seg_col, seg_row, out_rows, out_other)
    partial, pack_low, pack_high, down_low, down_high = tie(
        partial, pack_low, pack_high, down_low, down_high
    )
    downs = [w_down, down_above, jnp.concatenate([down_low, down_high], axis=0), down_below]
    downs = jnp.stack(downs)
    downs_other = shift(downs, "yh", 1)
    hidden = inputs + reduce_ring(partial, "x")
    hidden, downs_other = tie(hidden, downs_other)
    pack_other, _ = tie(pack_other, hidden)
    other_below = shift(pack_other, "x", 1)
    other_above = shift(pack_other, "x", -1)
    downs = jnp.stack([downs, downs_other])
    downs = jnp.roll(jnp.roll(downs, yh, axis=0), x, axis=1)
    down_full = jnp.swapaxes(downs.reshape(8, 2, 64, D), 0, 1).reshape(2, 512, D)
    other_low = shift(other_below[:, :half_pack], "x", 1)
    other_high = shift(other_above[:, half_pack:], "x", -1)

    scale_two = rms_scale(hidden)
    normed_two = (hidden * scale_two * gain_two).astype(bf16)
    normed_all = lax.all_gather(normed_two, BATCH, axis=0)
    blocks = [
        pack,
        pack_above,
        jnp.concatenate([pack_low, pack_high], axis=1),
        pack_below,
        pack_other,
        other_above,
        jnp.concatenate([other_low, other_high], axis=1),
        other_below,
    ]
    gate_full = jnp.zeros((2, D, 512), bf16)
    up_full = jnp.zeros((2, D, 512), bf16)
    for k, block in enumerate(blocks):
        at = ahead("yh", k // 4) * 4 + ahead("x", k % 4)
        gate_full = lax.dynamic_update_slice(gate_full, block[:, :192], (0, at * 192, 0))
        up_full = lax.dynamic_update_slice(up_full, block[:, 192:384], (0, at * 192, 0))
    near, across, taken, graded, act, da, db = experts(
        order, normed_all, grad_all, gates, gate_full, up_full, down_full
    )
    got = shift(across, "c", 1)
    grad_gate, up_pack, grad_down = expert_grad(seq_place, taken, graded, act, da, db)
    up_pack, got = tie(up_pack, got)
    sum_gate = lax.psum_scatter(grad_gate, SEQ, scatter_dimension=1, tiled=True).astype(f32)
    sum_down = lax.psum_scatter(grad_down, SEQ, scatter_dimension=1, tiled=True).astype(f32)
    held = add_up(near, got).astype(bf16).reshape(4, 2, TOK, D)
    sent = ring_send(held, "z")
    act, _ = tie(act, held)
    out_near, out_across = expert_out(order, gates, act, down_full)
    out_near, out_across, *sent = tie(out_near, out_across, *sent)
    hops = ring_next(ring_add(held, sent), "z")
    up_pack = up_pack.reshape(4, 2, 2, 192, 512)
    up_sent = ring_send(up_pack, "x")
    total, *up_sent = tie(add_up(held[0], *hops), *up_sent)
    up_hops = ring_add(up_pack, up_sent)
    grad_normed_two = add_up(total[0], shift(total[1].astype(bf16), "yl", 1))

    scaled_two = gain_two * grad_normed_two
    grad_gain_two = jnp.sum(grad_normed_two * hidden * scale_two, axis=0)
    grad_hidden = (
        upstream
        + scale_two * scaled_two
        - hidden * scale_two**3 * jnp.mean(scaled_two * hidden, axis=-1, keepdims=True)
    )
    pieces = ring_pieces(grad_hidden.astype(bf16), "x")
    up_hops_0, up_hops_1, out_near, out_across, *pieces = tie(
        *up_hops, out_near, out_across, *pieces
    )
    out_got = shift(out_across, "c", 1)
    up_hops = ring_next((up_hops_0, up_hops_1), "x")
    back = attend_back(
        where, queries, mixed, own, other, seg_col, seg_row, out_rows, out_other, pieces, cosine, sine
    )
    *back, out_got, up_got_0, up_got_1 = tie(*back, out_got, *up_hops)
    grad_query, grad_own, grad_sent, grad_out_w = back
    up_total = add_up(up_pack[0], up_got_0, up_got_1)
    held = add_up(out_near, out_got).astype(bf16).reshape(4, 2, TOK, D)
    grad_out_w = jnp.swapaxes(grad_out_w.reshape(2, 16, 96, 192), 0, 1)
    grad_out_w = jnp.swapaxes(grad_out_w, 1, 2).reshape(16, 96, 384)
    grad_got = shift(grad_sent, "yh", 1)
    sent = ring_send(held, "z")
    grad_got, *sent = tie(grad_got, *sent)
    hops = ring_next(ring_add(held, sent), "z")
    back = unproject(where, grad_query, grad_own, grad_got, gathered, moving, xp, scale_half)
    *back, hop_0, hop_1 = tie(*back, *hops)
    grad_raw, grad_part, gain_one_part = back
    total = add_up(held[0], hop_0, hop_1)
    out_last = shift(total[1].astype(bf16), "yl", 1)
    up_last = shift(up_total[1].astype(bf16), "yh", 1)
    sent = ring_send(grad_part, "x")
    out_last, up_last, *sent = tie(out_last, up_last, *sent)
    output = hidden + add_up(total[0], out_last)
    sum_up = add_up(up_total[0], up_last)
    grad_normed_one = add_up(grad_part[0], *ring_next(ring_add(grad_part, sent), "x"))
    scaled_one = gain_one * grad_normed_one
    scale_one = rms_scale(inputs)
    grad_inputs = (
        grad_hidden
        + scale_one * scaled_one
        - inputs * scale_one**3 * jnp.mean(scaled_one * inputs, axis=-1, keepdims=True)
    )

    gain_two_part = jnp.swapaxes(grad_gain_two.reshape(8, 16, 12), 0, 1).reshape(1, D)
    gain_rows = jnp.concatenate([gain_one_part[:1], gain_two_part, jnp.zeros((6, D), f32)], axis=0)
    grad_w = weight_grad(batch_place, normed, grad_raw, gain_rows, grad_out_w)
    grad_w = reduce_batch(grad_w[:8], grad_w[8:])
    sum_out = add_up(grad_w[:, 768:960], shift(grad_w[:, 960:].astype(bf16), "yh", 1))
    sum_out = sum_out.reshape(12, D)
    grad_w = grad_w[:, :768].astype(bf16).reshape(8, 12, 768)
    grad_w = lax.all_to_all(grad_w, SEQ, 0, 0, tiled=True).astype(f32)

    def from_heads(first, width):
        total = grad_w[:, :, first : first + width]
        second = grad_w[:, :, first + width : first + 2 * width]
        total = total + jnp.concatenate([second[4:], second[:4]], axis=0)
        return jnp.swapaxes(total, 0, 1).reshape(12, 8 * width)

    gain_sum = jnp.sum(grad_w[:, :, 640:642], axis=0)
    return (
        output.astype(bf16)[None],
        grad_inputs.astype(bf16)[None],
        from_heads(0, Q_OWN),
        from_heads(2 * Q_OWN, HEAD_DIM),
        from_heads(2 * Q_OWN + 2 * HEAD_DIM, HEAD_DIM),
        sum_out,
        gain_sum[:, 0],
        gain_sum[:, 1],
        sum_gate,
        sum_up,
        sum_down,
    )


def solution(mesh):
    fine = Mesh(mesh.devices.reshape(2, 4, 2, 4, 2), SEQ + BATCH)
    both = SEQ + BATCH
    placed = (
        P(BATCH, SEQ, None),
        P(BATCH, SEQ, None),
        P(BATCH, None),
        P(BATCH, SEQ, None),
        P(BATCH, SEQ, None),
        P(both, None),
        P(both, None),
        P(both, None),
        P(both, None),
        P(both),
        P(both),
        P(BATCH, SEQ, None),
        P(BATCH, SEQ, None),
        P(BATCH, SEQ, None),
    )
    return jax.shard_map(
        shards,
        mesh=fine,
        in_specs=placed,
        out_specs=(
            P(BATCH, SEQ, None),
            P(BATCH, SEQ, None),
            P(both, None),
            P(both, None),
            P(both, None),
            P(both, None),
            P(both),
            P(both),
            P(BATCH, SEQ, None),
            P(BATCH, SEQ, None),
            P(BATCH, SEQ, None),
        ),
        check_vma=False,
    )
```

```python
import jax
import jax.numpy as jnp
from jax import lax
from jax.experimental import pallas as pl
from jax.experimental.pallas import tpu as pltpu
from jax.sharding import Mesh, PartitionSpec as P

HEAD_DIM = 64
TOPK = 8
GROUP = 3
Q_OWN = GROUP * HEAD_DIM
TOK = 128
HALF = 512
D = 1536
EXPERTS = 32
norm_eps = 1e-06
rope_base = 10000.0
masked_score = -1e30
SEQ = ("yh", "x")
BATCH = ("yl", "z", "c")
SIZE = {"yh": 2, "x": 4, "yl": 2, "z": 4, "c": 2}
bf16 = jnp.bfloat16
f32 = jnp.float32


def dot(a, b):
    return jnp.dot(a, b, preferred_element_type=f32)


def shift(value, axis, by):
    size = SIZE[axis]
    return lax.ppermute(value, axis, [(i, (i + by) % size) for i in range(size)])


def ring_pieces(block, axis):
    half = block.shape[0] // 2
    below = shift(block, axis, 1)
    above = shift(block, axis, -1)
    low = shift(below[:half], axis, 1)
    high = shift(above[half:], axis, -1)
    return block, above, low, high, below


def add_up(*parts):
    total = parts[0].astype(f32)
    for part in parts[1:]:
        total = total + part.astype(f32)
    return total


def ring_send(blocks, axis):
    half = blocks[0].shape[0] // 2
    return shift(blocks[2][:half], axis, 1), shift(blocks[2][half:], axis, -1)


def ring_add(blocks, got):
    half = blocks[0].shape[0] // 2
    up = [add_up(blocks[1][:half], got[0]).astype(bf16), blocks[1][half:]]
    down = [blocks[3][:half], add_up(blocks[3][half:], got[1]).astype(bf16)]
    return jnp.concatenate(up, axis=0), jnp.concatenate(down, axis=0)


def ring_next(hops, axis):
    return shift(hops[0], axis, 1), shift(hops[1], axis, -1)


def reduce_ring(blocks, axis):
    hops = ring_add(blocks, ring_send(blocks, axis))
    return add_up(blocks[0], *ring_next(hops, axis))


def tie(*values):
    return lax.optimization_barrier(values)


def ahead(axis, by):
    return lax.rem(lax.axis_index(axis) + by, SIZE[axis])


def distance(axis, place):
    return lax.rem(place - lax.axis_index(axis) + SIZE[axis], SIZE[axis])


def dot_nt(a, b):
    return lax.dot_general(a, b, (((1,), (1,)), ((), ())), preferred_element_type=f32)


def dot_tn(a, b):
    return lax.dot_general(a, b, (((0,), (0,)), ((), ())), preferred_element_type=f32)


def whole(shape):
    zeros = (0,) * len(shape)
    return pl.BlockSpec(shape, lambda *_: zeros)


def once(shape):
    zeros = (0,) * len(shape)
    return pl.BlockSpec(shape, lambda *_: zeros, pipeline_mode=pl.Buffered(1))


def run(body, out_shapes, in_specs, out_specs, grid, args, prefetch=None, scratch=(), micros=0):
    spec = pltpu.PrefetchScalarGridSpec(
        num_scalar_prefetch=0 if prefetch is None else 1,
        grid=grid,
        in_specs=in_specs,
        out_specs=out_specs,
        scratch_shapes=list(scratch),
    )
    head = () if prefetch is None else (prefetch,)
    return pl.pallas_call(
        body,
        grid_spec=spec,
        out_shape=out_shapes,
        compiler_params=pltpu.CompilerParams(vmem_limit_bytes=56 << 20),
        cost_estimate=pl.CostEstimate(flops=1100000000 * micros, bytes_accessed=0, transcendentals=0),
    )(*head, *args)


def struct(shape, dtype):
    return jax.ShapeDtypeStruct(shape, dtype)


def turned(values):
    lane = lax.broadcasted_iota(jnp.int32, values.shape, 1)
    first = (lane % HEAD_DIM) < HEAD_DIM // 2
    return jnp.where(first, -pltpu.roll(values, 96, 1), pltpu.roll(values, 32, 1))


def by_lanes(values, function):
    width = values.shape[1]
    return jnp.concatenate(
        [function(values[:, k : k + 128]) for k in range(0, width, 128)], axis=1
    )


def prepare_body(where, own, above, far_low, far_high, below, moving, xp_ref, scale_ref):
    for k in range(4):
        place = pl.ds(lax.rem(where[0] + k, 4) * TOK, TOK)
        if k == 2:
            block = jnp.concatenate([far_low[...], far_high[...]], axis=0)
        else:
            block = (own, above, None, below)[k][...]
        wide = block.astype(f32)
        scale = lax.rsqrt(jnp.mean(wide * wide, axis=1, keepdims=True) + norm_eps)
        scale_ref[place, :] = jnp.broadcast_to(scale, (TOK, 128))
        xp_ref[place, :] = dot(block, moving[...]).astype(bf16)


def prepare(where, pieces, moving):
    specs = [whole(p.shape) for p in pieces] + [whole(moving.shape)]
    return run(
        prepare_body,
        [struct((HALF, D), bf16), struct((HALF, 128), f32)],
        specs,
        [whole((HALF, D)), whole((HALF, 128))],
        (1,),
        (*pieces, moving),
        prefetch=where,
        micros=7,
    )


def project_body(xp, scale, weight, cosine, sine, n_ref, q_ref, kv_ref, sent_ref):
    pick = lax.broadcasted_iota(jnp.int32, (8, 128), 0) == lax.broadcasted_iota(
        jnp.int32, (8, 128), 1
    )
    gains = dot_nt(pick.astype(bf16), weight[:, 640:])
    normed = (xp[...].astype(f32) * scale[:, :1] * gains[:1]).astype(bf16)
    n_ref[...] = normed
    raw = dot(normed, weight[:, :640])
    cos, sin = cosine[...], sine[...]
    rotated = by_lanes(raw[:, :512], lambda u: u * cos + turned(u) * sin).astype(bf16)
    q_ref[...] = rotated[:, :384]
    both = jnp.concatenate([rotated[:, 384:], raw[:, 512:].astype(bf16)], axis=1)
    kv_ref[...] = both
    sent_ref[...] = swap_groups(both)


def swap_groups(both):
    wide = both.astype(f32)
    return by_lanes(wide, lambda u: pltpu.roll(u, 64, 1)).astype(bf16)


def tile(width):
    return pl.BlockSpec((TOK, width), lambda i, *_: (i, 0))


def project(xp, scale, gathered, cosine, sine):
    return run(
        project_body,
        [
            struct((HALF, D), bf16),
            struct((HALF, 384), bf16),
            struct((HALF, 256), bf16),
            struct((HALF, 256), bf16),
        ],
        [whole((HALF, D)), whole((HALF, 128)), whole((D, 768)), whole((HALF, 128)), whole((HALF, 128))],
        [whole((HALF, D)), whole((HALF, 384)), whole((HALF, 256)), whole((HALF, 256))],
        (1,),
        (xp, scale, gathered, cosine, sine),
        micros=5,
    )


def softmax_parts(where, step, q, own, other, seg_col, seg_row, group):
    place = lax.rem(where[0] + step, 4) * TOK
    row = lax.broadcasted_iota(jnp.int32, (TOK, HALF), 0) + place
    key = lax.broadcasted_iota(jnp.int32, (TOK, HALF), 1)
    segs = seg_col[:, :1]
    own_ok = (segs == seg_row[:, :HALF]) & (key <= row)
    other_ok = (segs == seg_row[:, HALF:]) & (where[1] == 1)
    first = group * HEAD_DIM
    heads = [q[:, (3 * group + h) * HEAD_DIM : (3 * group + h + 1) * HEAD_DIM] for h in range(3)]
    queries = jnp.concatenate(heads, axis=0) * jnp.asarray(0.125, bf16)
    scores = []
    for kv, ok in ((own, own_ok), (other, other_ok)):
        s = dot_nt(queries, kv[:, first : first + HEAD_DIM]).reshape(3, TOK, HALF)
        scores.append(jnp.where(ok[None], s, masked_score))
    top = jnp.maximum(
        jnp.max(scores[0], axis=2, keepdims=True), jnp.max(scores[1], axis=2, keepdims=True)
    )
    exps = [jnp.exp(s - top) for s in scores]
    total = jnp.sum(exps[0], axis=2, keepdims=True) + jnp.sum(exps[1], axis=2, keepdims=True)
    inverse = 1.0 / total
    return queries, [(e * inverse).reshape(3 * TOK, HALF) for e in exps]


def attend_body(where, q, own, other, seg_col, seg_row, w_own, w_other, att_ref, part_ref):
    step = pl.program_id(0)
    columns = []
    for group in range(2):
        _, probs = softmax_parts(where, step, q[...], own, other, seg_col, seg_row, group)
        first = 128 + group * HEAD_DIM
        mixed = dot(probs[0].astype(bf16), own[:, first : first + HEAD_DIM])
        mixed = mixed + dot(probs[1].astype(bf16), other[:, first : first + HEAD_DIM])
        columns += [mixed[h * TOK : (h + 1) * TOK] for h in range(3)]
    att = jnp.concatenate(columns, axis=1).astype(bf16)
    att_ref[...] = att
    part = dot(att[:, :Q_OWN], w_own[...]) + dot(att[:, Q_OWN:], w_other[...])
    part_ref[0] = part.astype(bf16)


def turn(width):
    return pl.BlockSpec((TOK, width), lambda i, where: (lax.rem(where[0] + i, 4), 0))


def step_block(shape):
    return pl.BlockSpec((1,) + shape, lambda i, *_: (i, 0, 0))


def attend(where, q, own, other, seg_col, seg_row, w_own, w_other):
    return run(
        attend_body,
        [struct((HALF, 384), bf16), struct((4, TOK, D), bf16)],
        [
            turn(384),
            whole((HALF, 256)),
            whole((HALF, 256)),
            turn(128),
            whole((1, 2 * HALF)),
            whole((Q_OWN, D)),
            whole((Q_OWN, D)),
        ],
        [turn(384), pl.BlockSpec((1, TOK, D), lambda i, where: (lax.rem(where[0] + i, 4), 0, 0))],
        (4,),
        (q, own, other, seg_col, seg_row, w_own, w_other),
        prefetch=where,
        micros=15,
    )


def attend_back_body(
    where, q, att, own, other, seg_col, seg_row, w_own, w_other, z, cosine,
    sine, q_ref, own_ref, sent_ref, out_ref, sums, out_sum,
):
    step = pl.program_id(0)

    @pl.when(step == 0)
    def _():
        sums[...] = jnp.zeros_like(sums)
        out_sum[...] = jnp.zeros_like(out_sum)

    place = pl.ds(lax.rem(where[0] + step, 4) * TOK, TOK)
    grad_z = z[0]
    out_sum[...] += dot_tn(att[...], grad_z)
    grad_att = jnp.concatenate([dot_nt(grad_z, w_own[...]), dot_nt(grad_z, w_other[...])], axis=1)
    grad_att = grad_att.astype(bf16)
    columns, keys, values = [], [[], []], [[], []]
    for group in range(2):
        queries, probs = softmax_parts(where, step, q[...], own, other, seg_col, seg_row, group)
        grads = jnp.concatenate(
            [
                grad_att[:, (3 * group + h) * HEAD_DIM : (3 * group + h + 1) * HEAD_DIM]
                for h in range(3)
            ],
            axis=0,
        )
        first = group * HEAD_DIM
        grad_probs = [dot_nt(grads, kv[:, 128 + first : 192 + first]) for kv in (own, other)]
        row_dot = jnp.sum(probs[0] * grad_probs[0], axis=1, keepdims=True)
        row_dot = row_dot + jnp.sum(probs[1] * grad_probs[1], axis=1, keepdims=True)
        total = None
        for n, kv in enumerate((own, other)):
            grad_score = (probs[n] * (grad_probs[n] - row_dot)).astype(bf16)
            term = dot(grad_score, kv[:, first : first + HEAD_DIM])
            total = term if total is None else total + term
            keys[n].append(dot_tn(grad_score, queries))
            values[n].append(dot_tn(probs[n].astype(bf16), grads))
        total = total * 0.125
        columns += [total[h * TOK : (h + 1) * TOK] for h in range(3)]
    for n in range(2):
        sums[n] += jnp.concatenate(keys[n] + values[n], axis=1)
    grad_q = jnp.concatenate(columns, axis=1)
    cos, sin = cosine[place, :], sine[place, :]
    q_ref[...] = by_lanes(grad_q, lambda u: u * cos - turned(u) * sin).astype(bf16)

    @pl.when(step == 3)
    def _():
        for b in range(16):
            parts = [
                out_sum[g * Q_OWN + 12 * b : g * Q_OWN + 12 * b + 12, c * 768 : (c + 1) * 768]
                for g in range(2)
                for c in range(2)
            ]
            out_ref[b] = jnp.concatenate(parts, axis=0).astype(bf16)
        for n in range(2):
            at = slice(n * HALF, (n + 1) * HALF)
            grad_k = sums[n, :, :128]
            grad_k = grad_k * cosine[at, :] - turned(grad_k) * sine[at, :]
            both = jnp.concatenate([grad_k, sums[n, :, 128:]], axis=1)
            if n == 0:
                own_ref[...] = both
            else:
                sent_ref[...] = swap_groups(both)


def attend_back(where, q, att, own, other, seg_col, seg_row, w_own, w_other, pieces, cosine, sine):
    return run(
        attend_back_body,
        [
            struct((HALF, 384), bf16),
            struct((HALF, 256), f32),
            struct((HALF, 256), bf16),
            struct((16, 48, 768), bf16),
        ],
        [
            turn(384),
            turn(384),
            whole((HALF, 256)),
            whole((HALF, 256)),
            turn(128),
            whole((1, 2 * HALF)),
            whole((Q_OWN, D)),
            whole((Q_OWN, D)),
        ]
        + [pl.BlockSpec((1, TOK, D), lambda i, where: (lax.rem(where[0] + i, 4), 0, 0))]
        + [whole((2 * HALF, 128)), whole((2 * HALF, 128))],
        [turn(384), whole((HALF, 256)), whole((HALF, 256)), whole((16, 48, 768))],
        (4,),
        (q, att, own, other, seg_col, seg_row, w_own, w_other, pieces, cosine, sine),
        prefetch=where,
        scratch=[
            pltpu.VMEM((2, HALF, 256), f32),
            pltpu.VMEM((384, D), f32),
        ],
        micros=22,
    )


def unproject_body(where, q, own, got, weight, moving, xp, scale, raw_ref, part_ref, gain_ref):
    both = (own[...] + got[...].astype(f32)).astype(bf16)
    raw = jnp.concatenate([q[...], both], axis=1)
    raw_ref[...] = raw
    grad = dot_nt(raw, weight[:, :640])
    term = jnp.sum(grad * (xp[...].astype(f32) * scale[:, :1]), axis=0, keepdims=True)
    gain_ref[...] = jnp.broadcast_to(term, (8, D))
    part = dot_nt(grad.astype(bf16), moving[...]).astype(bf16)
    for k in range(4):
        part_ref[k] = part[k * TOK : (k + 1) * TOK]


def unproject(where, q, own, got, gathered, moving, xp, scale):
    return run(
        unproject_body,
        [struct((HALF, 640), bf16), struct((4, TOK, D), bf16), struct((8, D), f32)],
        [
            whole((HALF, 384)),
            whole((HALF, 256)),
            whole((HALF, 256)),
            whole((D, 768)),
            whole((D, D)),
            whole((HALF, D)),
            whole((HALF, 128)),
        ],
        [whole((HALF, 640)), whole((4, TOK, D)), whole((8, D))],
        (1,),
        (q, own, got, gathered, moving, xp, scale),
        prefetch=where,
        micros=10,
    )


def weight_grad_body(order, normed, raw, gains, out_rows, near_ref, across_ref):
    step = pl.program_id(0)
    grad = dot_tn(normed[...], raw[...]).astype(bf16)
    pick = lax.broadcasted_iota(jnp.int32, (8, 128), 0) == lax.broadcasted_iota(
        jnp.int32, (8, 128), 1
    )
    columns = dot_tn(gains[...].astype(bf16), pick.astype(bf16)).astype(bf16)
    for k in range(4):
        at = slice(k * 96, (k + 1) * 96)
        to = order[step * 4 + k]
        for ref, first in ((near_ref, 0), (across_ref, 8)):

            @pl.when((to >= first) & (to < first + 8))
            def _(ref=ref, first=first, at=at, k=k, to=to):
                ref[to - first, :96, :640] = grad[at]
                ref[to - first, :96, 640:] = columns[at]
                ref[to - first, 96:] = out_rows[k]


def weight_grad(order, normed, raw, gains, out_rows):
    return run(
        weight_grad_body,
        [struct((8, 144, 768), bf16)] * 2,
        [
            pl.BlockSpec((HALF, 384), lambda i, *_: (0, i)),
            whole((HALF, 640)),
            pl.BlockSpec((8, 384), lambda i, *_: (0, i)),
            pl.BlockSpec((4, 48, 768), lambda i, *_: (i, 0, 0)),
        ],
        [whole((8, 144, 768))] * 2,
        (4,),
        (normed, raw, gains, out_rows),
        prefetch=order,
        micros=6,
    )


CAP = 48
BLOCKS = 8
NEAR = BLOCKS // 2
STEP = BLOCKS * CAP


def choices(gates):
    hit = gates > 0
    upper = lax.broadcasted_iota(jnp.int32, (TOK, TOK), 0) <= lax.broadcasted_iota(
        jnp.int32, (TOK, TOK), 1
    )
    count = dot(hit.astype(bf16), upper.astype(bf16))
    slot = lax.broadcasted_iota(jnp.int32, (CAP, TOK), 0).astype(f32) + 1.0
    picks, weights = [], []
    for e in range(2):
        pick = (count[e : e + 1] == slot) & hit[e : e + 1]
        picks.append(pick.astype(bf16))
        weights.append(jnp.sum(jnp.where(pick, gates[e : e + 1], 0.0), axis=1, keepdims=True))
    return jnp.concatenate(picks, axis=0), jnp.concatenate(weights, axis=0)


def block_at(j, shape):
    def index(i, order):
        return (order[i * BLOCKS + j],) + (0,) * len(shape)

    return pl.BlockSpec((1,) + shape, index)


def expert_rows(width):
    return pl.BlockSpec((2, STEP, width), lambda i, *_: (0, i, 0))


def pair_block():
    return pl.BlockSpec((NEAR, TOK, D), lambda i, *_: (i, 0, 0))


def pick_block():
    return pl.BlockSpec((BLOCKS, 2 * CAP, TOK), lambda i, *_: (i, 0, 0))


SLOTS = 16 * CAP


def expert_begin_body(order, *refs):
    grads, gates = (refs[k * BLOCKS : (k + 1) * BLOCKS] for k in range(2))
    w_down, pick_ref, grad_ref, act_ref = refs[2 * BLOCKS :]
    for j in range(BLOCKS):
        pick, weight = choices(gates[j][0])
        pick_ref[j] = pick
        graded = (dot(pick, grads[j][0]) * weight).astype(bf16)
        for e in range(2):
            grad_ref[e, j * CAP : (j + 1) * CAP, :] = graded[e * CAP : (e + 1) * CAP]
    for e in range(2):
        act_ref[e] = dot_nt(grad_ref[e], w_down[e])


def expert_begin(order, grads, gates, w_down):
    return run(
        expert_begin_body,
        [
            struct((16, 2 * CAP, TOK), bf16),
            struct((2, SLOTS, D), bf16),
            struct((2, SLOTS, 512), f32),
        ],
        [block_at(j, (TOK, D)) for j in range(BLOCKS)]
        + [block_at(j, (2, TOK)) for j in range(BLOCKS)]
        + [once(w_down.shape)],
        [pick_block(), expert_rows(D), expert_rows(512)],
        (16 // BLOCKS,),
        (grads,) * BLOCKS + (gates,) * BLOCKS + (w_down,),
        prefetch=order,
        micros=11,
    )


def experts_body(order, *refs):
    rows = refs[:BLOCKS]
    picks, grad_acts, w_gate, w_up = refs[BLOCKS : BLOCKS + 4]
    near_ref, across_ref, in_ref, act_ref, da_ref, db_ref = refs[BLOCKS + 4 :]
    for j in range(BLOCKS):
        taken = dot(picks[j], rows[j][0]).astype(bf16)
        for e in range(2):
            in_ref[e, j * CAP : (j + 1) * CAP, :] = taken[e * CAP : (e + 1) * CAP]
    backs = []
    for e in range(2):
        taken, grad_act = in_ref[e], grad_acts[e]
        gate_pre = dot(taken, w_gate[e])
        up_pre = dot(taken, w_up[e])
        sig = 1.0 / (1.0 + jnp.exp(-gate_pre))
        silu = gate_pre * sig
        act_ref[e] = (silu * up_pre).astype(bf16)
        da = (grad_act * up_pre * sig * (1.0 + gate_pre * (1.0 - sig))).astype(bf16)
        db = (grad_act * silu).astype(bf16)
        da_ref[e] = da
        db_ref[e] = db
        backs.append((dot_nt(da, w_gate[e]) + dot_nt(db, w_up[e])).astype(bf16))
    for j in range(BLOCKS):
        at = slice(j * CAP, (j + 1) * CAP)
        back = dot_tn(picks[j], jnp.concatenate([backs[0][at], backs[1][at]], axis=0))
        target = near_ref if j < NEAR else across_ref
        target[j % NEAR] = back.astype(bf16)


def experts(order, rows, picks, grad_acts, w_gate, w_up):
    return run(
        experts_body,
        [struct((8, TOK, D), bf16)] * 2
        + [struct((2, SLOTS, D), bf16)]
        + [struct((2, SLOTS, 512), bf16)] * 3,
        [block_at(j, (TOK, D)) for j in range(BLOCKS)]
        + [pick_block(), expert_rows(512)]
        + [once(w.shape) for w in (w_gate, w_up)],
        [pair_block(), pair_block(), expert_rows(D)] + [expert_rows(512)] * 3,
        (16 // BLOCKS,),
        (rows,) * BLOCKS + (picks, grad_acts, w_gate, w_up),
        prefetch=order,
        micros=22,
    )


def expert_out_body(order, *refs):
    gates = refs[:BLOCKS]
    picks, act, w_down, out_ref = refs[BLOCKS:]
    step = pl.program_id(0)
    outs = [dot(act[e], w_down[e]) for e in range(2)]
    for j in range(BLOCKS):
        pick = picks[j]
        weights = [
            jnp.sum(pick[e * CAP : (e + 1) * CAP].astype(f32) * gates[j][0, e : e + 1], axis=1, keepdims=True)
            for e in range(2)
        ]
        at = slice(j * CAP, (j + 1) * CAP)
        both = jnp.concatenate([outs[e][at] * weights[e] for e in range(2)], axis=0)
        out_ref[order[step * BLOCKS + j]] = dot_tn(pick, both.astype(bf16)).astype(bf16)


def expert_out(order, gates, picks, act, w_down):
    return run(
        expert_out_body,
        [struct((16, TOK, D), bf16)],
        [block_at(j, (2, TOK)) for j in range(BLOCKS)]
        + [pick_block(), expert_rows(512), once(w_down.shape)],
        [whole((16, TOK, D))],
        (16 // BLOCKS,),
        (gates,) * BLOCKS + (picks, act, w_down),
        prefetch=order,
        micros=13,
    )[0]


def one(rows, width):
    return pl.BlockSpec((1, rows, width), lambda e, *_: (e, 0, 0))


def grad_down_body(act, graded, down_ref):
    down_ref[0] = dot_tn(act[0], graded[0]).astype(bf16)


def expert_grad_down(act, graded):
    return run(
        grad_down_body,
        [struct((2, 512, D), bf16)],
        [one(SLOTS, 512), one(SLOTS, D)],
        [one(512, D)],
        (2,),
        (act, graded),
        micros=5,
    )[0]


def grad_pair_body(order, taken, da, db, pack_ref):
    e = pl.program_id(0)
    gate = dot_tn(taken[0], da[0]).astype(bf16)
    up = dot_tn(taken[0], db[0]).astype(bf16)
    for k in range(8):
        pack_ref[order[k], e, :192] = gate[k * 192 : (k + 1) * 192]
        pack_ref[order[k], e, 192:] = up[k * 192 : (k + 1) * 192]


def expert_grad_pair(order, taken, da, db):
    return run(
        grad_pair_body,
        [struct((8, 2, 384, 512), bf16)],
        [one(SLOTS, D), one(SLOTS, 512), one(SLOTS, 512)],
        [whole((8, 2, 384, 512))],
        (2,),
        (taken, da, db),
        prefetch=order,
        micros=9,
    )[0]


def rms_scale(values):
    return lax.rsqrt(jnp.mean(values * values, axis=-1, keepdims=True) + norm_eps)


def three_parts(values):
    high = lax.reduce_precision(values, 8, 7)
    rest = values - high
    middle = lax.reduce_precision(rest, 8, 7)
    return [v.astype(bf16) for v in (high, middle, rest - middle)]


def shards(
    tokens,
    cotangent,
    segments,
    routes,
    gate_weights,
    w_query,
    w_key,
    w_value,
    w_out,
    norm_one,
    norm_two,
    w_gate,
    w_up,
    w_down,
):
    inputs = tokens[0].astype(f32)
    upstream = cotangent[0].astype(f32)
    yh, x = lax.axis_index("yh"), lax.axis_index("x")
    where = jnp.stack([x, yh]).astype(jnp.int32)
    order = jnp.stack(
        [
            m * 2 + ahead("c", j // NEAR)
            for i in range(16 // BLOCKS)
            for j in range(BLOCKS)
            for m in (NEAR * i + j % NEAR,)
        ]
    ).astype(jnp.int32)
    batch_place = jnp.stack(
        [
            distance("c", b % 2) * 8 + b // 2
            for b in range(16)
        ]
    ).astype(jnp.int32)
    seq_place = jnp.stack(
        [distance("x", s % 4) * 2 + distance("yh", s // 4) for s in range(8)]
    ).astype(jnp.int32)

    def for_heads(weight, width):
        by_head = jnp.swapaxes(weight.reshape(-1, 8, width), 0, 1)
        return [by_head, jnp.concatenate([by_head[4:], by_head[:4]], axis=0)]

    gains = jnp.pad(jnp.stack([norm_one, norm_two], axis=1), ((0, 0), (0, 126)))
    strip = jnp.concatenate(
        for_heads(w_query, Q_OWN)
        + for_heads(w_key, HEAD_DIM)
        + for_heads(w_value, HEAD_DIM)
        + [jnp.broadcast_to(gains[None], (8,) + gains.shape)],
        axis=2,
    )
    strip, w_out = tie(strip, w_out)
    strip = lax.all_to_all(strip, SEQ, 0, 0, tiled=True).reshape(96, 768)
    below, above = shift(tokens[0], "x", 1), shift(tokens[0], "x", -1)
    strip, below, above = tie(strip, below, above)
    half = TOK // 2
    pieces = (
        tokens[0], above, shift(below[:half], "x", 1), shift(above[half:], "x", -1), below
    )
    expert_ids = jnp.arange(EXPERTS, dtype=jnp.int32)[:, None, None]
    gate_dense = jnp.sum(jnp.where(routes[0][None] == expert_ids, gate_weights[0][None], 0.0), axis=2)
    strip = jnp.concatenate(
        [
            strip,
            jnp.concatenate(three_parts(gate_dense), axis=0),
            w_out.reshape(96, 192),
            shift(w_out, "yh", 1).reshape(96, 192),
        ],
        axis=1,
    )
    gathered = lax.all_gather(strip, BATCH, axis=0, tiled=True)
    grad_all = lax.all_gather(cotangent[0], BATCH, axis=0)

    feature = jnp.arange(D, dtype=jnp.int32)
    moved = feature % 192 // 12 * 96 + feature // 192 * 12 + feature % 12
    moving = (moved[:, None] == feature[None, :]).astype(bf16)
    xp, scale_half = prepare(where, pieces, moving)

    pack = jnp.concatenate([w_gate, w_up], axis=1)
    half_pack = pack.shape[1] // 2
    pack, w_down, _ = tie(pack, w_down, strip)
    down_other = shift(w_down, "yh", 1)
    pack_other = shift(pack, "yh", 1)
    downs = jnp.stack([w_down, down_other])
    downs, _, _ = tie(downs, pieces[2], pieces[3])
    down_below, down_above = shift(downs, "x", 1), shift(downs, "x", -1)

    def natural(row):
        return jnp.swapaxes(row.reshape(16, 8, 12), 0, 1).reshape(D)

    place = jnp.arange(2 * HALF, dtype=jnp.int32) + HALF * yh
    place = jnp.where(place >= 2 * HALF, place - 2 * HALF, place)
    seg = jnp.roll(segments[0], -HALF * yh)
    earlier = jnp.sum((seg[None, :] < seg[:, None]).astype(jnp.int32), axis=1)
    freq_index = jnp.arange(HEAD_DIM // 2, dtype=f32) * (2.0 / HEAD_DIM)
    frequency = jnp.tile(rope_base ** (-freq_index), 4)
    angle = (place - earlier).astype(f32)[:, None] * frequency
    cosine, sine = jnp.cos(angle), jnp.sin(angle)
    seg_row = seg[None, :]
    seg_col = jnp.broadcast_to(seg[:HALF, None], (HALF, 128))

    down_below, down_above, xp = tie(down_below, down_above, xp)
    down_low, down_high = shift(down_below[:1], "x", 1), shift(down_above[1:], "x", -1)
    gathered, xp, down_low, down_high = tie(gathered, xp, down_low, down_high)

    normed, queries, own, sent = project(xp, scale_half, gathered, cosine, sine)
    other = shift(sent, "yh", 1)
    pack, _ = tie(pack, normed)
    pack_below, pack_above = shift(pack, "x", 1), shift(pack, "x", -1)
    other, pack_below, pack_above = tie(other, pack_below, pack_above)
    pack_low = shift(pack_below[:, :half_pack], "x", 1)
    pack_high = shift(pack_above[:, half_pack:], "x", -1)
    downs = [downs, down_above, jnp.concatenate([down_low, down_high], axis=0), down_below]
    downs = jnp.stack(downs, axis=1)
    downs = jnp.roll(jnp.roll(downs, yh, axis=0), x, axis=1)
    down_full = jnp.swapaxes(downs.reshape(8, 2, 64, D), 0, 1).reshape(2, 512, D)
    out_rows = gathered[:, 896:1088].reshape(192, D)
    out_other = gathered[:, 1088:].reshape(192, D)
    gain_one = natural(gathered[:, 640].astype(f32))
    gain_two = natural(gathered[:, 641].astype(f32))
    gates = jnp.sum(gathered[:, 768:896].reshape(16, 3, EXPERTS, TOK).astype(f32), axis=1)
    gates = lax.dynamic_slice_in_dim(gates, lax.axis_index(BATCH) * 2, 2, axis=1)
    mixed, partial = attend(where, queries, own, other, seg_col, seg_row, out_rows, out_other)
    partial, pack_low, pack_high = tie(partial, pack_low, pack_high)
    partial = lax.all_to_all(partial, "x", 0, 0, tiled=True)
    hidden = inputs + jnp.sum(partial.astype(f32), axis=0)
    hidden, pack_other = tie(hidden, pack_other)
    both = ring_next((pack_other, pack_other), "x")

    scale_two = rms_scale(hidden)
    normed_two = (hidden * scale_two * gain_two).astype(bf16)
    normed_all = lax.all_gather(normed_two, BATCH, axis=0)
    grad_all, other_below, other_above = tie(grad_all, *both)
    other_low = shift(other_below[:, :half_pack], "x", 1)
    other_high = shift(other_above[:, half_pack:], "x", -1)
    picks, graded, grad_acts = expert_begin(order, grad_all, gates, down_full)
    picks, graded, grad_acts, other_low, other_high = tie(
        picks, graded, grad_acts, other_low, other_high
    )
    blocks = [
        pack,
        pack_above,
        jnp.concatenate([pack_low, pack_high], axis=1),
        pack_below,
        pack_other,
        other_above,
        jnp.concatenate([other_low, other_high], axis=1),
        other_below,
    ]
    gate_full = jnp.zeros((2, D, 512), bf16)
    up_full = jnp.zeros((2, D, 512), bf16)
    for k, block in enumerate(blocks):
        at = ahead("yh", k // 4) * 4 + ahead("x", k % 4)
        gate_full = lax.dynamic_update_slice(gate_full, block[:, :192], (0, at * 192, 0))
        up_full = lax.dynamic_update_slice(up_full, block[:, 192:384], (0, at * 192, 0))
    near, across, taken, act, da, db = experts(
        order, normed_all, picks, grad_acts, gate_full, up_full
    )
    got = shift(across, "c", 1)
    grad_down = expert_grad_down(act, graded)
    grad_down, got = tie(grad_down, got)
    held = add_up(near, got).astype(bf16)
    taken, _ = tie(taken, held)
    held = lax.all_to_all(held, ("yl", "z"), 0, 0, tiled=True)
    grad_pack = expert_grad_pair(seq_place, taken, da, db)
    act, grad_pack = tie(act, grad_pack)
    grad_pack = grad_pack.reshape(4, 2, 2, 384, 512)
    pack_sent = ring_send(grad_pack, "x")
    out_part = expert_out(order, gates, picks, act, down_full)
    out_part, held, *pack_sent = tie(out_part, held, *pack_sent)
    output = lax.psum_scatter(out_part, BATCH, scatter_dimension=0, tiled=True)
    grad_normed_two = jnp.sum(held.astype(f32), axis=0)

    scaled_two = gain_two * grad_normed_two
    grad_gain_two = jnp.sum(grad_normed_two * hidden * scale_two, axis=0)
    grad_hidden = (
        upstream
        + scale_two * scaled_two
        - hidden * scale_two**3 * jnp.mean(scaled_two * hidden, axis=-1, keepdims=True)
    )
    pieces = jnp.broadcast_to(grad_hidden.astype(bf16)[None], (4, TOK, D))
    pieces = lax.all_to_all(pieces, "x", 0, 0, tiled=True)
    pack_hops = [v.swapaxes(0, 1) for v in ring_add(grad_pack, pack_sent)]
    pieces, *pack_hops = tie(pieces, *pack_hops)
    first_hops = ring_next([v[0] for v in pack_hops], "x")
    back = attend_back(
        where, queries, mixed, own, other, seg_col, seg_row, out_rows, out_other,
        pieces, cosine, sine,
    )
    *back, hop_0, hop_1, pack_low, pack_high = tie(*back, *first_hops, *pack_hops)
    first_hops = hop_0, hop_1
    grad_query, grad_own, grad_sent, grad_out_w = back
    last_hops = ring_next([v[1] for v in (pack_low, pack_high)], "x")
    grad_got = shift(grad_sent, "yh", 1)
    back = unproject(where, grad_query, grad_own, grad_got, gathered, moving, xp, scale_half)
    grad_raw, grad_part, gain_one_part, output, *last_hops = tie(*back, output, *last_hops)
    grad_down, _ = tie(grad_down, output)
    sum_down = lax.psum_scatter(grad_down, SEQ, scatter_dimension=1, tiled=True)
    gain_two_part = jnp.swapaxes(grad_gain_two.reshape(8, 16, 12), 0, 1).reshape(1, D)
    gain_rows = jnp.concatenate([gain_one_part[:1], gain_two_part, jnp.zeros((6, D), f32)], axis=0)
    near, across = weight_grad(batch_place, normed, grad_raw, gain_rows, grad_out_w)
    got = shift(across, "c", 1)
    pack_total = add_up(
        grad_pack[0], *(jnp.stack(v, axis=1) for v in zip(first_hops, last_hops))
    )
    got, pack_total = tie(got, pack_total)
    held = add_up(near, got).astype(bf16)
    pack_last = shift(pack_total[1].astype(bf16), "yh", 1)
    grad_part, _ = tie(grad_part, held)
    held = lax.all_to_all(held, ("yl", "z"), 0, 0, tiled=True)
    grad_part = lax.all_to_all(grad_part, "x", 0, 0, tiled=True)
    grad_normed_one = jnp.sum(grad_part.astype(f32), axis=0)
    scaled_one = gain_one * grad_normed_one
    scale_one = rms_scale(inputs)
    grad_inputs = (
        grad_hidden
        + scale_one * scaled_one
        - inputs * scale_one**3 * jnp.mean(scaled_one * inputs, axis=-1, keepdims=True)
    )
    output = hidden + output[0].astype(f32)
    grad_inputs, output = grad_inputs.astype(bf16), output.astype(bf16)
    grad_pack = add_up(pack_total[0], pack_last)
    held, grad_inputs, output, grad_pack = tie(held, grad_inputs, output, grad_pack)
    grad_w = jnp.sum(held.astype(f32), axis=0).astype(bf16)
    out_sum = grad_w[96:].astype(f32).reshape(2, 2, 12, 768)
    out_got = shift(out_sum[1].astype(bf16), "yh", 1)
    grad_w = lax.all_to_all(grad_w[:96].reshape(8, 12, 768), SEQ, 0, 0, tiled=True)
    grad_w, sum_down, out_got = tie(grad_w, sum_down, out_got)
    sum_out = add_up(out_sum[0], out_got)
    sum_out = jnp.swapaxes(sum_out, 0, 1).reshape(12, D)
    grad_w = grad_w.astype(f32)
    sum_gate, sum_up = grad_pack[:, :192], grad_pack[:, 192:]
    sum_down = sum_down.astype(f32)

    def from_heads(first, width):
        total = grad_w[:, :, first : first + width]
        second = grad_w[:, :, first + width : first + 2 * width]
        total = total + jnp.concatenate([second[4:], second[:4]], axis=0)
        return jnp.swapaxes(total, 0, 1).reshape(12, 8 * width)

    gain_sum = jnp.sum(grad_w[:, :, 640:642], axis=0)
    return (
        output[None],
        grad_inputs[None],
        from_heads(0, Q_OWN),
        from_heads(2 * Q_OWN, HEAD_DIM),
        from_heads(2 * Q_OWN + 2 * HEAD_DIM, HEAD_DIM),
        sum_out,
        gain_sum[:, 0],
        gain_sum[:, 1],
        sum_gate,
        sum_up,
        sum_down,
    )


def solution(mesh):
    fine = Mesh(mesh.devices.reshape(2, 4, 2, 4, 2), SEQ + BATCH)
    both = SEQ + BATCH
    placed = (
        P(BATCH, SEQ, None),
        P(BATCH, SEQ, None),
        P(BATCH, None),
        P(BATCH, SEQ, None),
        P(BATCH, SEQ, None),
        P(both, None),
        P(both, None),
        P(both, None),
        P(both, None),
        P(both),
        P(both),
        P(BATCH, SEQ, None),
        P(BATCH, SEQ, None),
        P(BATCH, SEQ, None),
    )
    return jax.shard_map(
        shards,
        mesh=fine,
        in_specs=placed,
        out_specs=(
            P(BATCH, SEQ, None),
            P(BATCH, SEQ, None),
            P(both, None),
            P(both, None),
            P(both, None),
            P(both, None),
            P(both),
            P(both),
            P(BATCH, SEQ, None),
            P(BATCH, SEQ, None),
            P(BATCH, SEQ, None),
        ),
        check_vma=False,
    )
```

```python
import jax
import jax.numpy as jnp
from jax import lax
from jax.experimental import pallas as pl
from jax.experimental.pallas import tpu as pltpu
from jax.sharding import Mesh, PartitionSpec as P

HEAD_DIM = 64
TOPK = 8
GROUP = 3
Q_OWN = GROUP * HEAD_DIM
TOK = 128
HALF = 512
D = 1536
EXPERTS = 32
norm_eps = 1e-06
rope_base = 10000.0
masked_score = -1e30
SEQ = ("yh", "x")
BATCH = ("yl", "z", "c")
SIZE = {"yh": 2, "x": 4, "yl": 2, "z": 4, "c": 2}
bf16 = jnp.bfloat16
f32 = jnp.float32


def dot(a, b):
    return jnp.dot(a, b, preferred_element_type=f32)


def shift(value, axis, by):
    size = SIZE[axis]
    return lax.ppermute(value, axis, [(i, (i + by) % size) for i in range(size)])


def ring_pieces(block, axis):
    half = block.shape[0] // 2
    below = shift(block, axis, 1)
    above = shift(block, axis, -1)
    low = shift(below[:half], axis, 1)
    high = shift(above[half:], axis, -1)
    return block, above, low, high, below


def add_up(*parts):
    total = parts[0].astype(f32)
    for part in parts[1:]:
        total = total + part.astype(f32)
    return total


def ring_send(blocks, axis):
    half = blocks[0].shape[0] // 2
    return shift(blocks[2][:half], axis, 1), shift(blocks[2][half:], axis, -1)


def ring_add(blocks, got):
    half = blocks[0].shape[0] // 2
    up = [add_up(blocks[1][:half], got[0]).astype(bf16), blocks[1][half:]]
    down = [blocks[3][:half], add_up(blocks[3][half:], got[1]).astype(bf16)]
    return jnp.concatenate(up, axis=0), jnp.concatenate(down, axis=0)


def ring_next(hops, axis):
    return shift(hops[0], axis, 1), shift(hops[1], axis, -1)


def reduce_ring(blocks, axis):
    hops = ring_add(blocks, ring_send(blocks, axis))
    return add_up(blocks[0], *ring_next(hops, axis))


def tie(*values):
    return lax.optimization_barrier(values)


def ahead(axis, by):
    return lax.rem(lax.axis_index(axis) + by, SIZE[axis])


def distance(axis, place):
    return lax.rem(place - lax.axis_index(axis) + SIZE[axis], SIZE[axis])


def dot_nt(a, b):
    return lax.dot_general(a, b, (((1,), (1,)), ((), ())), preferred_element_type=f32)


def dot_tn(a, b):
    return lax.dot_general(a, b, (((0,), (0,)), ((), ())), preferred_element_type=f32)


def whole(shape):
    zeros = (0,) * len(shape)
    return pl.BlockSpec(shape, lambda *_: zeros)


def once(shape):
    zeros = (0,) * len(shape)
    return pl.BlockSpec(shape, lambda *_: zeros, pipeline_mode=pl.Buffered(1))


def run(body, out_shapes, in_specs, out_specs, grid, args, prefetch=None, scratch=(), micros=0):
    spec = pltpu.PrefetchScalarGridSpec(
        num_scalar_prefetch=0 if prefetch is None else 1,
        grid=grid,
        in_specs=in_specs,
        out_specs=out_specs,
        scratch_shapes=list(scratch),
    )
    head = () if prefetch is None else (prefetch,)
    return pl.pallas_call(
        body,
        grid_spec=spec,
        out_shape=out_shapes,
        compiler_params=pltpu.CompilerParams(vmem_limit_bytes=56 << 20),
        cost_estimate=pl.CostEstimate(flops=1100000000 * micros, bytes_accessed=0, transcendentals=0),
    )(*head, *args)


def struct(shape, dtype):
    return jax.ShapeDtypeStruct(shape, dtype)


def turned(values):
    lane = lax.broadcasted_iota(jnp.int32, values.shape, 1)
    first = (lane % HEAD_DIM) < HEAD_DIM // 2
    return jnp.where(first, -pltpu.roll(values, 96, 1), pltpu.roll(values, 32, 1))


def by_lanes(values, function):
    width = values.shape[1]
    return jnp.concatenate(
        [function(values[:, k : k + 128]) for k in range(0, width, 128)], axis=1
    )


def prepare_body(where, own, above, far_low, far_high, below, moving, xp_ref, scale_ref):
    for k in range(4):
        place = pl.ds(lax.rem(where[0] + k, 4) * TOK, TOK)
        if k == 2:
            block = jnp.concatenate([far_low[...], far_high[...]], axis=0)
        else:
            block = (own, above, None, below)[k][...]
        wide = block.astype(f32)
        scale = lax.rsqrt(jnp.mean(wide * wide, axis=1, keepdims=True) + norm_eps)
        scale_ref[place, :] = jnp.broadcast_to(scale, (TOK, 128))
        xp_ref[place, :] = dot(block, moving[...]).astype(bf16)


def prepare(where, pieces, moving):
    specs = [whole(p.shape) for p in pieces] + [whole(moving.shape)]
    return run(
        prepare_body,
        [struct((HALF, D), bf16), struct((HALF, 128), f32)],
        specs,
        [whole((HALF, D)), whole((HALF, 128))],
        (1,),
        (*pieces, moving),
        prefetch=where,
        micros=7,
    )


def project_body(xp, scale, weight, cosine, sine, n_ref, q_ref, kv_ref, sent_ref):
    pick = lax.broadcasted_iota(jnp.int32, (8, 128), 0) == lax.broadcasted_iota(
        jnp.int32, (8, 128), 1
    )
    gains = dot_nt(pick.astype(bf16), weight[:, 640:])
    normed = (xp[...].astype(f32) * scale[:, :1] * gains[:1]).astype(bf16)
    n_ref[...] = normed
    raw = dot(normed, weight[:, :640])
    cos, sin = cosine[...], sine[...]
    rotated = by_lanes(raw[:, :512], lambda u: u * cos + turned(u) * sin).astype(bf16)
    q_ref[...] = rotated[:, :384]
    both = jnp.concatenate([rotated[:, 384:], raw[:, 512:].astype(bf16)], axis=1)
    kv_ref[...] = both
    sent_ref[...] = swap_groups(both)


def swap_groups(both):
    wide = both.astype(f32)
    return by_lanes(wide, lambda u: pltpu.roll(u, 64, 1)).astype(bf16)


def tile(width):
    return pl.BlockSpec((TOK, width), lambda i, *_: (i, 0))


def project(xp, scale, gathered, cosine, sine):
    return run(
        project_body,
        [
            struct((HALF, D), bf16),
            struct((HALF, 384), bf16),
            struct((HALF, 256), bf16),
            struct((HALF, 256), bf16),
        ],
        [whole((HALF, D)), whole((HALF, 128)), whole((D, 768)), whole((HALF, 128)), whole((HALF, 128))],
        [whole((HALF, D)), whole((HALF, 384)), whole((HALF, 256)), whole((HALF, 256))],
        (1,),
        (xp, scale, gathered, cosine, sine),
        micros=5,
    )


def softmax_parts(where, step, q, own, other, seg_col, seg_row, group):
    place = lax.rem(where[0] + step, 4) * TOK
    row = lax.broadcasted_iota(jnp.int32, (TOK, HALF), 0) + place
    key = lax.broadcasted_iota(jnp.int32, (TOK, HALF), 1)
    segs = seg_col[:, :1]
    own_ok = (segs == seg_row[:, :HALF]) & (key <= row)
    other_ok = (segs == seg_row[:, HALF:]) & (where[1] == 1)
    first = group * HEAD_DIM
    heads = [q[:, (3 * group + h) * HEAD_DIM : (3 * group + h + 1) * HEAD_DIM] for h in range(3)]
    queries = jnp.concatenate(heads, axis=0) * jnp.asarray(0.125, bf16)
    scores = []
    for kv, ok in ((own, own_ok), (other, other_ok)):
        s = dot_nt(queries, kv[:, first : first + HEAD_DIM]).reshape(3, TOK, HALF)
        scores.append(jnp.where(ok[None], s, masked_score))
    top = jnp.maximum(
        jnp.max(scores[0], axis=2, keepdims=True), jnp.max(scores[1], axis=2, keepdims=True)
    )
    exps = [jnp.exp(s - top) for s in scores]
    total = jnp.sum(exps[0], axis=2, keepdims=True) + jnp.sum(exps[1], axis=2, keepdims=True)
    inverse = 1.0 / total
    return queries, [(e * inverse).reshape(3 * TOK, HALF) for e in exps]


def attend_body(where, q, own, other, seg_col, seg_row, w_own, w_other, att_ref, part_ref):
    step = pl.program_id(0)
    columns = []
    for group in range(2):
        _, probs = softmax_parts(where, step, q[...], own, other, seg_col, seg_row, group)
        first = 128 + group * HEAD_DIM
        mixed = dot(probs[0].astype(bf16), own[:, first : first + HEAD_DIM])
        mixed = mixed + dot(probs[1].astype(bf16), other[:, first : first + HEAD_DIM])
        columns += [mixed[h * TOK : (h + 1) * TOK] for h in range(3)]
    att = jnp.concatenate(columns, axis=1).astype(bf16)
    att_ref[...] = att
    part = dot(att[:, :Q_OWN], w_own[...]) + dot(att[:, Q_OWN:], w_other[...])
    part_ref[0] = part.astype(bf16)


def turn(width):
    return pl.BlockSpec((TOK, width), lambda i, where: (lax.rem(where[0] + i, 4), 0))


def step_block(shape):
    return pl.BlockSpec((1,) + shape, lambda i, *_: (i, 0, 0))


def attend(where, q, own, other, seg_col, seg_row, w_own, w_other):
    return run(
        attend_body,
        [struct((HALF, 384), bf16), struct((4, TOK, D), bf16)],
        [
            turn(384),
            whole((HALF, 256)),
            whole((HALF, 256)),
            turn(128),
            whole((1, 2 * HALF)),
            whole((Q_OWN, D)),
            whole((Q_OWN, D)),
        ],
        [turn(384), pl.BlockSpec((1, TOK, D), lambda i, where: (lax.rem(where[0] + i, 4), 0, 0))],
        (4,),
        (q, own, other, seg_col, seg_row, w_own, w_other),
        prefetch=where,
        micros=15,
    )


def attend_back_body(
    where, q, att, own, other, seg_col, seg_row, w_own, w_other, z, cosine,
    sine, q_ref, own_ref, sent_ref, out_ref, sums, out_sum,
):
    step = pl.program_id(0)

    @pl.when(step == 0)
    def _():
        sums[...] = jnp.zeros_like(sums)
        out_sum[...] = jnp.zeros_like(out_sum)

    place = pl.ds(lax.rem(where[0] + step, 4) * TOK, TOK)
    grad_z = z[0]
    out_sum[...] += dot_tn(att[...], grad_z)
    grad_att = jnp.concatenate([dot_nt(grad_z, w_own[...]), dot_nt(grad_z, w_other[...])], axis=1)
    grad_att = grad_att.astype(bf16)
    columns, keys, values = [], [[], []], [[], []]
    for group in range(2):
        queries, probs = softmax_parts(where, step, q[...], own, other, seg_col, seg_row, group)
        grads = jnp.concatenate(
            [
                grad_att[:, (3 * group + h) * HEAD_DIM : (3 * group + h + 1) * HEAD_DIM]
                for h in range(3)
            ],
            axis=0,
        )
        first = group * HEAD_DIM
        grad_probs = [dot_nt(grads, kv[:, 128 + first : 192 + first]) for kv in (own, other)]
        row_dot = jnp.sum(probs[0] * grad_probs[0], axis=1, keepdims=True)
        row_dot = row_dot + jnp.sum(probs[1] * grad_probs[1], axis=1, keepdims=True)
        total = None
        for n, kv in enumerate((own, other)):
            grad_score = (probs[n] * (grad_probs[n] - row_dot)).astype(bf16)
            term = dot(grad_score, kv[:, first : first + HEAD_DIM])
            total = term if total is None else total + term
            keys[n].append(dot_tn(grad_score, queries))
            values[n].append(dot_tn(probs[n].astype(bf16), grads))
        total = total * 0.125
        columns += [total[h * TOK : (h + 1) * TOK] for h in range(3)]
    for n in range(2):
        sums[n] += jnp.concatenate(keys[n] + values[n], axis=1)
    grad_q = jnp.concatenate(columns, axis=1)
    cos, sin = cosine[place, :], sine[place, :]
    q_ref[...] = by_lanes(grad_q, lambda u: u * cos - turned(u) * sin).astype(bf16)

    @pl.when(step == 3)
    def _():
        for b in range(16):
            parts = [
                out_sum[g * Q_OWN + 12 * b : g * Q_OWN + 12 * b + 12, c * 768 : (c + 1) * 768]
                for g in range(2)
                for c in range(2)
            ]
            out_ref[b] = jnp.concatenate(parts, axis=0).astype(bf16)
        for n in range(2):
            at = slice(n * HALF, (n + 1) * HALF)
            grad_k = sums[n, :, :128]
            grad_k = grad_k * cosine[at, :] - turned(grad_k) * sine[at, :]
            both = jnp.concatenate([grad_k, sums[n, :, 128:]], axis=1)
            if n == 0:
                own_ref[...] = both
            else:
                sent_ref[...] = swap_groups(both)


def attend_back(where, q, att, own, other, seg_col, seg_row, w_own, w_other, pieces, cosine, sine):
    return run(
        attend_back_body,
        [
            struct((HALF, 384), bf16),
            struct((HALF, 256), f32),
            struct((HALF, 256), bf16),
            struct((16, 48, 768), bf16),
        ],
        [
            turn(384),
            turn(384),
            whole((HALF, 256)),
            whole((HALF, 256)),
            turn(128),
            whole((1, 2 * HALF)),
            whole((Q_OWN, D)),
            whole((Q_OWN, D)),
        ]
        + [pl.BlockSpec((1, TOK, D), lambda i, where: (lax.rem(where[0] + i, 4), 0, 0))]
        + [whole((2 * HALF, 128)), whole((2 * HALF, 128))],
        [turn(384), whole((HALF, 256)), whole((HALF, 256)), whole((16, 48, 768))],
        (4,),
        (q, att, own, other, seg_col, seg_row, w_own, w_other, pieces, cosine, sine),
        prefetch=where,
        scratch=[
            pltpu.VMEM((2, HALF, 256), f32),
            pltpu.VMEM((384, D), f32),
        ],
        micros=22,
    )


def unproject_body(where, q, own, got, weight, moving, raw_ref, part_ref):
    both = (own[...] + got[...].astype(f32)).astype(bf16)
    raw = jnp.concatenate([q[...], both], axis=1)
    raw_ref[...] = raw
    grad = dot_nt(raw, weight[:, :640])
    part = dot_nt(grad.astype(bf16), moving[...]).astype(bf16)
    for k in range(4):
        part_ref[lax.rem(k + 4 - where[0], 4)] = part[k * TOK : (k + 1) * TOK]


def unproject(where, q, own, got, gathered, moving):
    return run(
        unproject_body,
        [struct((HALF, 640), bf16), struct((4, TOK, D), bf16)],
        [
            whole((HALF, 384)),
            whole((HALF, 256)),
            whole((HALF, 256)),
            whole((D, 768)),
            whole((D, D)),
        ],
        [whole((HALF, 640)), whole((4, TOK, D))],
        (1,),
        (q, own, got, gathered, moving),
        prefetch=where,
        micros=10,
    )


def weight_grad_body(order, normed, raw, gains, out_rows, near_ref, across_ref):
    step = pl.program_id(0)
    grad = dot_tn(normed[...], raw[...]).astype(bf16)
    pick = lax.broadcasted_iota(jnp.int32, (8, 128), 0) == lax.broadcasted_iota(
        jnp.int32, (8, 128), 1
    )
    columns = dot_tn(gains[...].astype(bf16), pick.astype(bf16)).astype(bf16)
    for k in range(4):
        at = slice(k * 96, (k + 1) * 96)
        to = order[step * 4 + k]
        for ref, first in ((near_ref, 0), (across_ref, 8)):

            @pl.when((to >= first) & (to < first + 8))
            def _(ref=ref, first=first, at=at, k=k, to=to):
                ref[to - first, :96, :640] = grad[at]
                ref[to - first, :96, 640:] = columns[at]
                ref[to - first, 96:] = out_rows[k]


def weight_grad(order, normed, raw, gains, out_rows):
    return run(
        weight_grad_body,
        [struct((8, 144, 768), bf16)] * 2,
        [
            pl.BlockSpec((HALF, 384), lambda i, *_: (0, i)),
            whole((HALF, 640)),
            pl.BlockSpec((8, 384), lambda i, *_: (0, i)),
            pl.BlockSpec((4, 48, 768), lambda i, *_: (i, 0, 0)),
        ],
        [whole((8, 144, 768))] * 2,
        (4,),
        (normed, raw, gains, out_rows),
        prefetch=order,
        micros=6,
    )


def finish_body(held, w_query, w_key, w_value, gain, q_ref, k_ref, v_ref, one_ref, two_ref):
    sums = [held[s].astype(f32) for s in range(8)]

    def columns(first, width):
        own = [t[:, first : first + width] for t in sums]
        other = [t[:, first + width : first + 2 * width] for t in sums]
        return jnp.concatenate([own[s] + other[(s + 4) % 8] for s in range(8)], axis=1)

    along = None
    parts = ((q_ref, w_query, 0, Q_OWN), (k_ref, w_key, 384, 64), (v_ref, w_value, 512, 64))
    for ref, weight, first, width in parts:
        grad = columns(first, width)
        ref[...] = grad
        term = jnp.sum(grad * weight[...].astype(f32), axis=1, keepdims=True)
        along = term if along is None else along + term
    one_ref[...] = along / gain[...]
    two_ref[...] = sum(t[:, 640:] for t in sums)


def finish(held, w_query, w_key, w_value, gain):
    args = (held, w_query, w_key, w_value, gain)
    outs = [struct((12, n), f32) for n in (1536, 512, 512, 128, 128)]
    return run(
        finish_body,
        outs,
        [whole(v.shape) for v in args],
        [whole(v.shape) for v in outs],
        (1,),
        args,
        micros=4,
    )


CAP = 48
BLOCKS = 8
NEAR = BLOCKS // 2
STEP = BLOCKS * CAP


def choices(gates):
    hit = gates > 0
    upper = lax.broadcasted_iota(jnp.int32, (TOK, TOK), 0) <= lax.broadcasted_iota(
        jnp.int32, (TOK, TOK), 1
    )
    count = dot(hit.astype(bf16), upper.astype(bf16))
    slot = lax.broadcasted_iota(jnp.int32, (CAP, TOK), 0).astype(f32) + 1.0
    picks, weights = [], []
    for e in range(2):
        pick = (count[e : e + 1] == slot) & hit[e : e + 1]
        picks.append(pick.astype(bf16))
        weights.append(jnp.sum(jnp.where(pick, gates[e : e + 1], 0.0), axis=1, keepdims=True))
    return jnp.concatenate(picks, axis=0), jnp.concatenate(weights, axis=0)


def block_at(j, shape):
    def index(i, order):
        return (order[i * BLOCKS + j],) + (0,) * len(shape)

    return pl.BlockSpec((1,) + shape, index)


def expert_rows(width):
    return pl.BlockSpec((2, STEP, width), lambda i, *_: (0, i, 0))


def pair_block():
    return pl.BlockSpec((NEAR, TOK, D), lambda i, *_: (i, 0, 0))


def pick_block():
    return pl.BlockSpec((BLOCKS, 2 * CAP, TOK), lambda i, *_: (i, 0, 0))


SLOTS = 16 * CAP


def expert_begin_body(order, *refs):
    grads, gates = (refs[k * BLOCKS : (k + 1) * BLOCKS] for k in range(2))
    start, above, below, low, high = refs[2 * BLOCKS : 2 * BLOCKS + 5]
    pick_ref, grad_ref, act_ref, w_down = refs[2 * BLOCKS + 5 :]

    @pl.when(pl.program_id(0) == 0)
    def _():
        for half, far in enumerate((low, high)):
            for k, block in enumerate((start, above, far, below)):
                at = pl.multiple_of(order[16 + 4 * half + k] * 64, 64)
                for e in range(2):
                    w_down[e, pl.ds(at, 64), :] = block[0 if k == 2 else half, e]

    for j in range(BLOCKS):
        pick, weight = choices(gates[j][0])
        pick_ref[j] = pick
        graded = (dot(pick, grads[j][0]) * weight).astype(bf16)
        for e in range(2):
            grad_ref[e, j * CAP : (j + 1) * CAP, :] = graded[e * CAP : (e + 1) * CAP]
    for e in range(2):
        act_ref[e] = dot_nt(grad_ref[e], w_down[e])


def expert_begin(order, grads, gates, downs):
    return run(
        expert_begin_body,
        [
            struct((16, 2 * CAP, TOK), bf16),
            struct((2, SLOTS, D), bf16),
            struct((2, SLOTS, 512), f32),
            struct((2, 512, D), bf16),
        ],
        [block_at(j, (TOK, D)) for j in range(BLOCKS)]
        + [block_at(j, (2, TOK)) for j in range(BLOCKS)]
        + [once(v.shape) for v in downs],
        [pick_block(), expert_rows(D), expert_rows(512), whole((2, 512, D))],
        (16 // BLOCKS,),
        (grads,) * BLOCKS + (gates,) * BLOCKS + downs,
        prefetch=order,
        micros=11,
    )


def experts_body(order, *refs):
    rows = refs[:BLOCKS]
    picks, grad_acts = refs[BLOCKS : BLOCKS + 2]
    packs = refs[BLOCKS + 2 : BLOCKS + 10]
    near_ref, across_ref, in_ref, act_ref, da_ref, db_ref, w_gate, w_up = refs[BLOCKS + 10 :]

    @pl.when(pl.program_id(0) == 0)
    def _():
        for half in range(2):
            own, above, below = packs[3 * half : 3 * half + 3]
            far = slice(192 * half, 192 * half + 192)
            for k, block in enumerate((own, above, None, below)):
                at = pl.ds(pl.multiple_of(order[16 + 4 * half + k] * 192, 192), 192)
                for e in range(2):
                    w_gate[e, at, :] = packs[6][e, far] if k == 2 else block[e, :192]
                    w_up[e, at, :] = packs[7][e, far] if k == 2 else block[e, 192:]

    for j in range(BLOCKS):
        taken = dot(picks[j], rows[j][0]).astype(bf16)
        for e in range(2):
            in_ref[e, j * CAP : (j + 1) * CAP, :] = taken[e * CAP : (e + 1) * CAP]
    backs = []
    for e in range(2):
        taken, grad_act = in_ref[e], grad_acts[e]
        gate_pre = dot(taken, w_gate[e])
        up_pre = dot(taken, w_up[e])
        sig = 1.0 / (1.0 + jnp.exp(-gate_pre))
        silu = gate_pre * sig
        act_ref[e] = (silu * up_pre).astype(bf16)
        da = (grad_act * up_pre * sig * (1.0 + gate_pre * (1.0 - sig))).astype(bf16)
        db = (grad_act * silu).astype(bf16)
        da_ref[e] = da
        db_ref[e] = db
        backs.append((dot_nt(da, w_gate[e]) + dot_nt(db, w_up[e])).astype(bf16))
    for j in range(BLOCKS):
        at = slice(j * CAP, (j + 1) * CAP)
        back = dot_tn(picks[j], jnp.concatenate([backs[0][at], backs[1][at]], axis=0))
        target = near_ref if j < NEAR else across_ref
        target[j % NEAR] = back.astype(bf16)


def experts(order, rows, picks, grad_acts, packs):
    return run(
        experts_body,
        [struct((8, TOK, D), bf16)] * 2
        + [struct((2, SLOTS, D), bf16)]
        + [struct((2, SLOTS, 512), bf16)] * 3,
        [block_at(j, (TOK, D)) for j in range(BLOCKS)]
        + [pick_block(), expert_rows(512)]
        + [once(v.shape) for v in packs],
        [pair_block(), pair_block(), expert_rows(D)] + [expert_rows(512)] * 3,
        (16 // BLOCKS,),
        (rows,) * BLOCKS + (picks, grad_acts) + packs,
        prefetch=order,
        scratch=[pltpu.VMEM((2, D, 512), bf16)] * 2,
        micros=22,
    )


def expert_out_body(order, *refs):
    gates = refs[:BLOCKS]
    picks, act, w_down, out_ref = refs[BLOCKS:]
    step = pl.program_id(0)
    outs = [dot(act[e], w_down[e]) for e in range(2)]
    for j in range(BLOCKS):
        pick = picks[j]
        weights = [
            jnp.sum(pick[e * CAP : (e + 1) * CAP].astype(f32) * gates[j][0, e : e + 1], axis=1, keepdims=True)
            for e in range(2)
        ]
        at = slice(j * CAP, (j + 1) * CAP)
        both = jnp.concatenate([outs[e][at] * weights[e] for e in range(2)], axis=0)
        out_ref[order[step * BLOCKS + j]] = dot_tn(pick, both.astype(bf16)).astype(bf16)


def expert_out(order, gates, picks, act, w_down):
    return run(
        expert_out_body,
        [struct((16, TOK, D), bf16)],
        [block_at(j, (2, TOK)) for j in range(BLOCKS)]
        + [pick_block(), expert_rows(512), once(w_down.shape)],
        [whole((16, TOK, D))],
        (16 // BLOCKS,),
        (gates,) * BLOCKS + (picks, act, w_down),
        prefetch=order,
        micros=2,
    )[0]


def one(rows, width):
    return pl.BlockSpec((1, rows, width), lambda e, *_: (e, 0, 0))


def grad_down_body(order, act, graded, down_ref):
    e = pl.program_id(0)
    down = dot_tn(act[0], graded[0]).astype(bf16)
    for k in range(8):
        down_ref[order[k], e] = down[k * 64 : (k + 1) * 64]


def expert_grad_down(order, act, graded):
    return run(
        grad_down_body,
        [struct((8, 2, 64, D), bf16)],
        [one(SLOTS, 512), one(SLOTS, D)],
        [whole((8, 2, 64, D))],
        (2,),
        (act, graded),
        prefetch=order,
        micros=2,
    )[0]


def grad_pair_body(order, taken, da, db, pack_ref, fore_ref, back_ref):
    e = pl.program_id(0)
    gate = dot_tn(taken[0], da[0]).astype(bf16)
    up = dot_tn(taken[0], db[0]).astype(bf16)
    for k in range(8):
        to = order[k]
        at = slice(k * 192, (k + 1) * 192)

        @pl.when(to < 6)
        def _(to=to, at=at):
            pack_ref[to // 2, lax.rem(to, 2), e, :192] = gate[at]
            pack_ref[to // 2, lax.rem(to, 2), e, 192:] = up[at]

        for far, ref in ((6, fore_ref), (7, back_ref)):

            @pl.when(to == far)
            def _(ref=ref, at=at):
                ref[e, :192] = gate[at]
                ref[e, 192:] = up[at]


def expert_grad_pair(order, taken, da, db):
    return run(
        grad_pair_body,
        [struct((3, 2, 2, 384, 512), bf16)] + [struct((2, 384, 512), bf16)] * 2,
        [one(SLOTS, D), one(SLOTS, 512), one(SLOTS, 512)],
        [whole((3, 2, 2, 384, 512)), whole((2, 384, 512)), whole((2, 384, 512))],
        (2,),
        (taken, da, db),
        prefetch=order,
        micros=2,
    )


def rms_scale(values):
    return lax.rsqrt(jnp.mean(values * values, axis=-1, keepdims=True) + norm_eps)


def three_parts(values):
    high = lax.reduce_precision(values, 8, 7)
    rest = values - high
    middle = lax.reduce_precision(rest, 8, 7)
    return [v.astype(bf16) for v in (high, middle, rest - middle)]


def shards(
    tokens,
    cotangent,
    segments,
    routes,
    gate_weights,
    w_query,
    w_key,
    w_value,
    w_out,
    norm_one,
    norm_two,
    w_gate,
    w_up,
    w_down,
):
    inputs = tokens[0].astype(f32)
    upstream = cotangent[0].astype(f32)
    yh, x = lax.axis_index("yh"), lax.axis_index("x")
    where = jnp.stack([x, yh]).astype(jnp.int32)
    order = jnp.stack(
        [
            m * 2 + ahead("c", j // NEAR)
            for i in range(16 // BLOCKS)
            for j in range(BLOCKS)
            for m in (NEAR * i + j % NEAR,)
        ]
        + [ahead("yh", k // 4) * 4 + ahead("x", k % 4) for k in range(8)]
    ).astype(jnp.int32)
    batch_place = jnp.stack(
        [
            distance("c", b % 2) * 8 + b // 2
            for b in range(16)
        ]
    ).astype(jnp.int32)
    seq_place = jnp.stack(
        [
            jnp.array([0, 1, 3, 2])[distance("x", s % 4)] * 2 + distance("yh", s // 4)
            for s in range(8)
        ]
    ).astype(jnp.int32)

    def for_heads(weight, width):
        by_head = jnp.swapaxes(weight.reshape(-1, 8, width), 0, 1)
        return [by_head, jnp.concatenate([by_head[4:], by_head[:4]], axis=0)]

    gains = jnp.pad(jnp.stack([norm_one, norm_two], axis=1), ((0, 0), (0, 126)))
    strip = jnp.concatenate(
        for_heads(w_query, Q_OWN)
        + for_heads(w_key, HEAD_DIM)
        + for_heads(w_value, HEAD_DIM)
        + [jnp.broadcast_to(gains[None], (8,) + gains.shape)],
        axis=2,
    )
    strip, w_out = tie(strip, w_out)
    strip = lax.all_to_all(strip, SEQ, 0, 0, tiled=True).reshape(96, 768)
    below, above = shift(tokens[0], "x", 1), shift(tokens[0], "x", -1)
    strip, below, above = tie(strip, below, above)
    half = TOK // 2
    pieces = (
        tokens[0], above, shift(below[:half], "x", 1), shift(above[half:], "x", -1), below
    )
    expert_ids = jnp.arange(EXPERTS, dtype=jnp.int32)[:, None, None]
    gate_dense = jnp.sum(jnp.where(routes[0][None] == expert_ids, gate_weights[0][None], 0.0), axis=2)
    strip = jnp.concatenate(
        [
            strip,
            jnp.concatenate(three_parts(gate_dense), axis=0),
            w_out.reshape(96, 192),
            shift(w_out, "yh", 1).reshape(96, 192),
        ],
        axis=1,
    )
    gathered = lax.all_gather(strip, BATCH, axis=0, tiled=True)
    grad_all = lax.all_gather(cotangent[0], BATCH, axis=0)

    feature = jnp.arange(D, dtype=jnp.int32)
    moved = feature % 192 // 12 * 96 + feature // 192 * 12 + feature % 12
    moving = (moved[:, None] == feature[None, :]).astype(bf16)
    xp, scale_half = prepare(where, pieces, moving)

    pack = jnp.concatenate([w_gate, w_up], axis=1)
    half_pack = pack.shape[1] // 2
    pack, w_down, _ = tie(pack, w_down, strip)
    down_other = shift(w_down, "yh", 1)
    pack_other = shift(pack, "yh", 1)
    downs = jnp.stack([w_down, down_other])
    downs, _, _ = tie(downs, pieces[2], pieces[3])
    down_below, down_above = shift(downs, "x", 1), shift(downs, "x", -1)

    def natural(row):
        return jnp.swapaxes(row.reshape(16, 8, 12), 0, 1).reshape(D)

    place = jnp.arange(2 * HALF, dtype=jnp.int32) + HALF * yh
    place = jnp.where(place >= 2 * HALF, place - 2 * HALF, place)
    seg = jnp.roll(segments[0], -HALF * yh)
    earlier = jnp.sum((seg[None, :] < seg[:, None]).astype(jnp.int32), axis=1)
    freq_index = jnp.arange(HEAD_DIM // 2, dtype=f32) * (2.0 / HEAD_DIM)
    frequency = jnp.tile(rope_base ** (-freq_index), 4)
    angle = (place - earlier).astype(f32)[:, None] * frequency
    cosine, sine = jnp.cos(angle), jnp.sin(angle)
    seg_row = seg[None, :]
    seg_col = jnp.broadcast_to(seg[:HALF, None], (HALF, 128))

    down_below, down_above, xp = tie(down_below, down_above, xp)
    down_low, down_high = shift(down_below[:1], "x", 1), shift(down_above[1:], "x", -1)
    gathered, xp, down_low, down_high = tie(gathered, xp, down_low, down_high)

    normed, queries, own, sent = project(xp, scale_half, gathered, cosine, sine)
    other = shift(sent, "yh", 1)
    pack, _ = tie(pack, normed)
    pack_below, pack_above = shift(pack, "x", 1), shift(pack, "x", -1)
    downs = (downs, down_above, down_below, down_low, down_high)
    out_rows = gathered[:, 896:1088].reshape(192, D)
    out_other = gathered[:, 1088:].reshape(192, D)
    gain_one = natural(gathered[:, 640].astype(f32))
    gain_two = natural(gathered[:, 641].astype(f32))
    gates = jnp.sum(gathered[:, 768:896].reshape(16, 3, EXPERTS, TOK).astype(f32), axis=1)
    gates = lax.dynamic_slice_in_dim(gates, lax.axis_index(BATCH) * 2, 2, axis=1)
    mixed, partial = attend(where, queries, own, other, seg_col, seg_row, out_rows, out_other)
    partial, pack_below, pack_above = tie(partial, pack_below, pack_above)
    partial = lax.all_to_all(partial, "x", 0, 0, tiled=True)
    hidden = inputs + jnp.sum(partial.astype(f32), axis=0)
    hidden, pack_other = tie(hidden, pack_other)
    both = ring_next((pack_other, pack_other), "x")

    scale_two = rms_scale(hidden)
    normed_two = (hidden * scale_two * gain_two).astype(bf16)
    normed_all = lax.all_gather(normed_two, BATCH, axis=0)
    grad_all, other_below, other_above = tie(grad_all, *both)
    low = jnp.concatenate([pack_below[:, :half_pack], other_below[:, :half_pack]], axis=1)
    high = jnp.concatenate([pack_above[:, half_pack:], other_above[:, half_pack:]], axis=1)
    low, high = ring_next((low, high), "x")
    picks, graded, grad_acts, down_full = expert_begin(order, grad_all, gates, downs)
    picks, graded, grad_acts, low, high = tie(picks, graded, grad_acts, low, high)
    packs = (pack, pack_above, pack_below, pack_other, other_above, other_below, low, high)
    near, across, taken, act, da, db = experts(
        order, normed_all, picks, grad_acts, packs
    )
    got = shift(across, "c", 1)
    down_place = jnp.stack([s % 4 * 2 + distance("yh", s // 4) for s in range(8)])
    grad_down = expert_grad_down(down_place.astype(jnp.int32), act, graded)
    grad_down, got = tie(grad_down, got)
    grad_down = grad_down.reshape(8 * 2 * 64, D)
    held = add_up(near, got).astype(bf16)
    taken, _ = tie(taken, held)
    held = lax.all_to_all(held, ("yl", "z"), 0, 0, tiled=True)
    grad_pack, fore, back = expert_grad_pair(seq_place, taken, da, db)
    act, grad_pack = tie(act, grad_pack)
    pack_sent = shift(fore, "x", 1), shift(back, "x", -1)
    out_part = expert_out(order, gates, picks, act, down_full)
    out_part, held, *pack_sent = tie(out_part, held, *pack_sent)
    output = lax.psum_scatter(out_part, BATCH, scatter_dimension=0, tiled=True)
    grad_normed_two = jnp.sum(held.astype(f32), axis=0)

    scaled_two = gain_two * grad_normed_two
    grad_gain_two = jnp.sum(grad_normed_two * hidden * scale_two, axis=0)
    grad_hidden = (
        upstream
        + scale_two * scaled_two
        - hidden * scale_two**3 * jnp.mean(scaled_two * hidden, axis=-1, keepdims=True)
    )
    pieces = jnp.broadcast_to(grad_hidden.astype(bf16)[None], (4, TOK, D))
    pieces = lax.all_to_all(pieces, "x", 0, 0, tiled=True)
    pack_hops = [
        [jnp.stack([add_up(grad_pack[1, 0, e], pack_sent[0][e]).astype(bf16), grad_pack[1, 1, e]]),
         jnp.stack([grad_pack[2, 0, e], add_up(grad_pack[2, 1, e], pack_sent[1][e]).astype(bf16)])]
        for e in range(2)
    ]
    pack_hops = pack_hops[0] + pack_hops[1]
    pieces, *pack_hops = tie(pieces, *pack_hops)
    first_hops = ring_next(pack_hops[:2], "x")
    back = attend_back(
        where, queries, mixed, own, other, seg_col, seg_row, out_rows, out_other,
        pieces, cosine, sine,
    )
    *back, hop_0, hop_1, pack_low, pack_high = tie(*back, *first_hops, *pack_hops[2:])
    first_hops = hop_0, hop_1
    grad_query, grad_own, grad_sent, grad_out_w = back
    last_hops = ring_next((pack_low, pack_high), "x")
    grad_got = shift(grad_sent, "yh", 1)
    first_total = add_up(grad_pack[0, :, 0], *first_hops)
    first_total, _ = tie(first_total, grad_sent)
    first_last = shift(first_total[1].astype(bf16), "yh", 1)
    back = unproject(where, grad_query, grad_own, grad_got, gathered, moving)
    grad_raw, grad_part, first_last, output, *last_hops = tie(
        *back, first_last, output, *last_hops
    )
    grad_down, _ = tie(grad_down, output)
    grad_down = lax.psum_scatter(grad_down, "x", scatter_dimension=0, tiled=True)
    part_sent = ring_send(grad_part, "x")
    gain_two_part = jnp.swapaxes(grad_gain_two.reshape(8, 16, 12), 0, 1).reshape(1, D)
    gain_rows = jnp.concatenate([gain_two_part, jnp.zeros((7, D), f32)], axis=0)
    near, across = weight_grad(batch_place, normed, grad_raw, gain_rows, grad_out_w)
    near, across, *rest = tie(near, across, *last_hops, *part_sent)
    last_hops, part_sent = rest[:2], rest[2:]
    got = shift(across, "c", 1)
    last_total = add_up(grad_pack[0, :, 1], *last_hops)
    last_last = shift(last_total[1].astype(bf16), "yh", 1)
    got, last_total = tie(got, last_total)
    held = add_up(near, got).astype(bf16)
    first_total, output, _ = tie(first_total, output, held)
    held, *part_sent = tie(held, *part_sent)
    held = lax.all_to_all(held, ("yl", "z"), 0, 0, tiled=True)
    grad_normed_one = add_up(grad_part[0], *ring_next(ring_add(grad_part, part_sent), "x"))
    scaled_one = gain_one * grad_normed_one
    scale_one = rms_scale(inputs)
    grad_inputs = (
        grad_hidden
        + scale_one * scaled_one
        - inputs * scale_one**3 * jnp.mean(scaled_one * inputs, axis=-1, keepdims=True)
    ).astype(bf16)
    output = (hidden + output[0].astype(f32)).astype(bf16)
    gain = jnp.broadcast_to(norm_one.astype(f32)[:, None], (12, 128))
    held, output, gain, grad_inputs = tie(held, output, gain, grad_inputs)
    grad_w = jnp.sum(held.astype(f32), axis=0).astype(bf16)
    out_sum = grad_w[96:].astype(f32).reshape(2, 2, 12, 768)
    out_got = shift(out_sum[1].astype(bf16), "yh", 1)
    grad_w = lax.all_to_all(grad_w[:96].reshape(8, 12, 768), SEQ, 0, 0, tiled=True)
    grad_down = grad_down.reshape(2, 2, 64, D)
    down_last = shift(grad_down[1], "yh", 1)
    sum_out = add_up(out_sum[0], out_got)
    sum_out = jnp.swapaxes(sum_out, 0, 1).reshape(12, D)
    grad_w, sum_out, last_last, down_last = tie(grad_w, sum_out, last_last, down_last)
    sum_down = add_up(grad_down[0], down_last)
    grad_pack = [add_up(first_total[0], first_last), add_up(last_total[0], last_last)]
    grad_pack = jnp.stack(grad_pack)
    sum_gate, sum_up = grad_pack[:, :192], grad_pack[:, 192:]
    grad_q, grad_k, grad_v, grad_one, grad_two = finish(grad_w, w_query, w_key, w_value, gain)
    return (
        output[None],
        grad_inputs[None],
        grad_q,
        grad_k,
        grad_v,
        sum_out,
        grad_one[:, 0],
        grad_two[:, 0],
        sum_gate,
        sum_up,
        sum_down,
    )


def solution(mesh):
    fine = Mesh(mesh.devices.reshape(2, 4, 2, 4, 2), SEQ + BATCH)
    both = SEQ + BATCH
    placed = (
        P(BATCH, SEQ, None),
        P(BATCH, SEQ, None),
        P(BATCH, None),
        P(BATCH, SEQ, None),
        P(BATCH, SEQ, None),
        P(both, None),
        P(both, None),
        P(both, None),
        P(both, None),
        P(both),
        P(both),
        P(BATCH, SEQ, None),
        P(BATCH, SEQ, None),
        P(BATCH, SEQ, None),
    )
    return jax.shard_map(
        shards,
        mesh=fine,
        in_specs=placed,
        out_specs=(
            P(BATCH, SEQ, None),
            P(BATCH, SEQ, None),
            P(both, None),
            P(both, None),
            P(both, None),
            P(both, None),
            P(both),
            P(both),
            P(BATCH, SEQ, None),
            P(BATCH, SEQ, None),
            P(BATCH, SEQ, None),
        ),
        check_vma=False,
    )
```

```python
import functools

import jax
import jax.numpy as jnp
from jax import lax
from jax.experimental import pallas as pl
from jax.experimental.pallas import tpu as pltpu
from jax.sharding import Mesh, PartitionSpec as P

HEAD_DIM = 64
TOPK = 8
GROUP = 3
Q_OWN = GROUP * HEAD_DIM
TOK = 128
HALF = 512
D = 1536
EXPERTS = 32
norm_eps = 1e-06
rope_base = 10000.0
masked_score = -1e30
SEQ = ("yh", "x")
BATCH = ("yl", "z", "c")
SIZE = {"yh": 2, "x": 4, "yl": 2, "z": 4, "c": 2}
bf16 = jnp.bfloat16
f32 = jnp.float32


def dot(a, b):
    return jnp.dot(a, b, preferred_element_type=f32)


def shift(value, axis, by):
    size = SIZE[axis]
    return lax.ppermute(value, axis, [(i, (i + by) % size) for i in range(size)])


def ring_pieces(block, axis):
    half = block.shape[0] // 2
    below = shift(block, axis, 1)
    above = shift(block, axis, -1)
    low = shift(below[:half], axis, 1)
    high = shift(above[half:], axis, -1)
    return block, above, low, high, below


def add_up(*parts):
    total = parts[0].astype(f32)
    for part in parts[1:]:
        total = total + part.astype(f32)
    return total


def ring_send(blocks, axis):
    half = blocks[0].shape[0] // 2
    return shift(blocks[2][:half], axis, 1), shift(blocks[2][half:], axis, -1)


def ring_add(blocks, got):
    half = blocks[0].shape[0] // 2
    up = [add_up(blocks[1][:half], got[0]).astype(bf16), blocks[1][half:]]
    down = [blocks[3][:half], add_up(blocks[3][half:], got[1]).astype(bf16)]
    return jnp.concatenate(up, axis=0), jnp.concatenate(down, axis=0)


def ring_next(hops, axis):
    return shift(hops[0], axis, 1), shift(hops[1], axis, -1)


def reduce_ring(blocks, axis):
    hops = ring_add(blocks, ring_send(blocks, axis))
    return add_up(blocks[0], *ring_next(hops, axis))


def tie(*values):
    return lax.optimization_barrier(values)


def ahead(axis, by):
    return lax.rem(lax.axis_index(axis) + by, SIZE[axis])


def distance(axis, place):
    return lax.rem(place - lax.axis_index(axis) + SIZE[axis], SIZE[axis])


def dot_nt(a, b):
    return lax.dot_general(a, b, (((1,), (1,)), ((), ())), preferred_element_type=f32)


def dot_tn(a, b):
    return lax.dot_general(a, b, (((0,), (0,)), ((), ())), preferred_element_type=f32)


def whole(shape):
    zeros = (0,) * len(shape)
    return pl.BlockSpec(shape, lambda *_: zeros)


def once(shape):
    zeros = (0,) * len(shape)
    return pl.BlockSpec(shape, lambda *_: zeros, pipeline_mode=pl.Buffered(1))


def run(body, out_shapes, in_specs, out_specs, grid, args, prefetch=None, scratch=(), micros=0):
    spec = pltpu.PrefetchScalarGridSpec(
        num_scalar_prefetch=0 if prefetch is None else 1,
        grid=grid,
        in_specs=in_specs,
        out_specs=out_specs,
        scratch_shapes=list(scratch),
    )
    head = () if prefetch is None else (prefetch,)
    return pl.pallas_call(
        body,
        grid_spec=spec,
        out_shape=out_shapes,
        compiler_params=pltpu.CompilerParams(vmem_limit_bytes=56 << 20),
        cost_estimate=pl.CostEstimate(flops=1100000000 * micros, bytes_accessed=0, transcendentals=0),
    )(*head, *args)


def struct(shape, dtype):
    return jax.ShapeDtypeStruct(shape, dtype)


def turned(values):
    lane = lax.broadcasted_iota(jnp.int32, values.shape, 1)
    first = (lane % HEAD_DIM) < HEAD_DIM // 2
    return jnp.where(first, -pltpu.roll(values, 96, 1), pltpu.roll(values, 32, 1))


def by_lanes(values, function):
    width = values.shape[1]
    return jnp.concatenate(
        [function(values[:, k : k + 128]) for k in range(0, width, 128)], axis=1
    )


def prepare_body(where, own, above, far_low, far_high, below, moving, xp_ref, scale_ref):
    for k in range(4):
        place = pl.ds(lax.rem(where[0] + k, 4) * TOK, TOK)
        if k == 2:
            block = jnp.concatenate([far_low[...], far_high[...]], axis=0)
        else:
            block = (own, above, None, below)[k][...]
        wide = block.astype(f32)
        scale = lax.rsqrt(jnp.mean(wide * wide, axis=1, keepdims=True) + norm_eps)
        scale_ref[place, :] = jnp.broadcast_to(scale, (TOK, 128))
        xp_ref[place, :] = dot(block, moving[...]).astype(bf16)


def prepare(where, pieces, moving):
    specs = [whole(p.shape) for p in pieces] + [whole(moving.shape)]
    return run(
        prepare_body,
        [struct((HALF, D), bf16), struct((HALF, 128), f32)],
        specs,
        [whole((HALF, D)), whole((HALF, 128))],
        (1,),
        (*pieces, moving),
        prefetch=where,
        micros=7,
    )


def project_body(xp, scale, weight, cosine, sine, n_ref, q_ref, kv_ref, sent_ref):
    pick = lax.broadcasted_iota(jnp.int32, (8, 128), 0) == lax.broadcasted_iota(
        jnp.int32, (8, 128), 1
    )
    gains = dot_nt(pick.astype(bf16), weight[:, 640:])
    normed = (xp[...].astype(f32) * scale[:, :1] * gains[:1]).astype(bf16)
    n_ref[...] = normed
    raw = dot(normed, weight[:, :640])
    cos, sin = cosine[...], sine[...]
    rotated = by_lanes(raw[:, :512], lambda u: u * cos + turned(u) * sin).astype(bf16)
    q_ref[...] = rotated[:, :384]
    both = jnp.concatenate([rotated[:, 384:], raw[:, 512:].astype(bf16)], axis=1)
    kv_ref[...] = both
    sent_ref[...] = swap_groups(both)


def swap_groups(both):
    wide = both.astype(f32)
    return by_lanes(wide, lambda u: pltpu.roll(u, 64, 1)).astype(bf16)


def tile(width):
    return pl.BlockSpec((TOK, width), lambda i, *_: (i, 0))


def project(xp, scale, gathered, cosine, sine):
    return run(
        project_body,
        [
            struct((HALF, D), bf16),
            struct((HALF, 384), bf16),
            struct((HALF, 256), bf16),
            struct((HALF, 256), bf16),
        ],
        [whole((HALF, D)), whole((HALF, 128)), whole((D, 768)), whole((HALF, 128)), whole((HALF, 128))],
        [whole((HALF, D)), whole((HALF, 384)), whole((HALF, 256)), whole((HALF, 256))],
        (1,),
        (xp, scale, gathered, cosine, sine),
        micros=5,
    )


def head_rows(values):
    empty = jnp.zeros((TOK, HEAD_DIM), values.dtype)
    rows = []
    for h in range(6):
        head = values[:, h * HEAD_DIM : (h + 1) * HEAD_DIM]
        rows.append(jnp.concatenate([head, empty] if h < 3 else [empty, head], axis=1))
    return jnp.concatenate(rows, axis=0)


def head_columns(both):
    rows = [
        both[h // 3 * HEAD_DIM : (h // 3 + 1) * HEAD_DIM, h * TOK : (h + 1) * TOK]
        for h in range(6)
    ]
    return jnp.concatenate(rows, axis=0).T


def softmax_parts(tile_at, second, queries, own, other, seg_col, seg_row):
    seen = (tile_at + 1) * TOK
    query = lax.broadcasted_iota(jnp.int32, (seen, TOK), 1) + tile_at * TOK
    key = lax.broadcasted_iota(jnp.int32, (seen, TOK), 0)
    segs = seg_row[:, tile_at * TOK : seen]
    own_ok = (seg_col[:seen, :1] == segs) & (key <= query)
    other_ok = (seg_col[HALF:, :1] == segs) & second
    scores = []
    for kv, ok, keys in ((own, own_ok, seen), (other, other_ok, HALF)):
        s = dot_nt(kv[:keys, :128], queries)
        low = jnp.where(ok, 0.0, masked_score)
        scores.append(s + jnp.concatenate([low] * 6, axis=1))
    top = jnp.maximum(
        jnp.max(scores[0], axis=0, keepdims=True), jnp.max(scores[1], axis=0, keepdims=True)
    )
    exps = [jnp.exp(s - top) for s in scores]
    total = jnp.sum(exps[0], axis=0, keepdims=True) + jnp.sum(exps[1], axis=0, keepdims=True)
    inverse = 1.0 / total
    return [e * inverse for e in exps]


def each_tile(function):
    for tile_at in range(4):
        pl.when(pl.program_id(0) == tile_at)(functools.partial(function, tile_at))


def attend_body(where, q, own, other, seg_col, seg_row, w_own, w_other, att_ref, part_ref):
    second = where[1] == 1

    def one_tile(tile_at):
        queries = head_rows(q[...]) * jnp.asarray(0.125, bf16)
        probs = softmax_parts(tile_at, second, queries, own, other, seg_col, seg_row)
        mixed = dot_tn(own[: (tile_at + 1) * TOK, 128:], probs[0].astype(bf16))
        mixed = mixed + dot_tn(other[:, 128:], probs[1].astype(bf16))
        att_ref[...] = head_columns(mixed).astype(bf16)

    each_tile(one_tile)
    part = dot(att_ref[:, :Q_OWN], w_own[...]) + dot(att_ref[:, Q_OWN:], w_other[...])
    part_ref[0] = part.astype(bf16)


def step_block(shape):
    return pl.BlockSpec((1,) + shape, lambda i, *_: (i, 0, 0))


def attend(where, q, own, other, seg_col, seg_row, w_own, w_other):
    return run(
        attend_body,
        [struct((HALF, 384), bf16), struct((4, TOK, D), bf16)],
        [
            tile(384),
            whole((HALF, 256)),
            whole((HALF, 256)),
            whole((2 * HALF, 128)),
            whole((1, 2 * HALF)),
            whole((Q_OWN, D)),
            whole((Q_OWN, D)),
        ],
        [tile(384), step_block((TOK, D))],
        (4,),
        (q, own, other, seg_col, seg_row, w_own, w_other),
        prefetch=where,
        micros=15,
    )


def attend_back_body(
    where, q, att, own, other, seg_col, seg_row, w_own, w_other, z, cosine,
    sine, q_ref, own_ref, sent_ref, out_ref, sums, out_sum,
):
    step = pl.program_id(0)

    @pl.when(step == 0)
    def _():
        sums[...] = jnp.zeros_like(sums)
        out_sum[...] = jnp.zeros_like(out_sum)

    second = where[1] == 1
    grad_z = z[0]
    out_sum[...] += dot_tn(att[...], grad_z)
    grad_att = jnp.concatenate([dot_nt(grad_z, w_own[...]), dot_nt(grad_z, w_other[...])], axis=1)
    grad_att = grad_att.astype(bf16)

    def one_tile(tile_at):
        queries = head_rows(q[...]) * jnp.asarray(0.125, bf16)
        grads = head_rows(grad_att)
        probs = softmax_parts(tile_at, second, queries, own, other, seg_col, seg_row)
        sides = ((own, (tile_at + 1) * TOK), (other, HALF))
        grad_probs = [dot_nt(kv[:n, 128:], grads) for kv, n in sides]
        row_dot = jnp.sum(probs[0] * grad_probs[0], axis=0, keepdims=True)
        row_dot = row_dot + jnp.sum(probs[1] * grad_probs[1], axis=0, keepdims=True)
        total = None
        for side, (kv, n) in enumerate(sides):
            grad_score = (probs[side] * (grad_probs[side] - row_dot)).astype(bf16)
            term = dot_tn(kv[:n, :128], grad_score)
            total = term if total is None else total + term
            sums[side, :n, :128] += dot(grad_score, queries)
            sums[side, :n, 128:] += dot(probs[side].astype(bf16), grads)
        grad_q = head_columns(total * 0.125)
        at = slice(tile_at * TOK, (tile_at + 1) * TOK)
        cos, sin = cosine[at, :], sine[at, :]
        q_ref[...] = by_lanes(grad_q, lambda u: u * cos - turned(u) * sin).astype(bf16)

    each_tile(one_tile)

    @pl.when(step == 3)
    def _():
        for b in range(16):
            parts = [
                out_sum[g * Q_OWN + 12 * b : g * Q_OWN + 12 * b + 12, c * 768 : (c + 1) * 768]
                for g in range(2)
                for c in range(2)
            ]
            out_ref[b] = jnp.concatenate(parts, axis=0).astype(bf16)
        for n in range(2):
            at = slice(n * HALF, (n + 1) * HALF)
            grad_k = sums[n, :, :128]
            grad_k = grad_k * cosine[at, :] - turned(grad_k) * sine[at, :]
            both = jnp.concatenate([grad_k, sums[n, :, 128:]], axis=1)
            if n == 0:
                own_ref[...] = both
            else:
                sent_ref[...] = swap_groups(both)


def attend_back(where, q, att, own, other, seg_col, seg_row, w_own, w_other, pieces, cosine, sine):
    return run(
        attend_back_body,
        [
            struct((HALF, 384), bf16),
            struct((HALF, 256), f32),
            struct((HALF, 256), bf16),
            struct((16, 48, 768), bf16),
        ],
        [
            tile(384),
            tile(384),
            whole((HALF, 256)),
            whole((HALF, 256)),
            whole((2 * HALF, 128)),
            whole((1, 2 * HALF)),
            whole((Q_OWN, D)),
            whole((Q_OWN, D)),
        ]
        + [step_block((TOK, D))]
        + [whole((2 * HALF, 128)), whole((2 * HALF, 128))],
        [tile(384), whole((HALF, 256)), whole((HALF, 256)), whole((16, 48, 768))],
        (4,),
        (q, att, own, other, seg_col, seg_row, w_own, w_other, pieces, cosine, sine),
        prefetch=where,
        scratch=[
            pltpu.VMEM((2, HALF, 256), f32),
            pltpu.VMEM((384, D), f32),
        ],
        micros=22,
    )


def unproject_body(where, q, own, got, weight, moving, raw_ref, part_ref):
    both = (own[...] + got[...].astype(f32)).astype(bf16)
    raw = jnp.concatenate([q[...], both], axis=1)
    raw_ref[...] = raw
    grad = dot_nt(raw, weight[:, :640])
    part = dot_nt(grad.astype(bf16), moving[...]).astype(bf16)
    for k in range(4):
        part_ref[lax.rem(k + 4 - where[0], 4)] = part[k * TOK : (k + 1) * TOK]


def unproject(where, q, own, got, gathered, moving):
    return run(
        unproject_body,
        [struct((HALF, 640), bf16), struct((4, TOK, D), bf16)],
        [
            whole((HALF, 384)),
            whole((HALF, 256)),
            whole((HALF, 256)),
            whole((D, 768)),
            whole((D, D)),
        ],
        [whole((HALF, 640)), whole((4, TOK, D))],
        (1,),
        (q, own, got, gathered, moving),
        prefetch=where,
        micros=10,
    )


def weight_grad_body(order, normed, raw, gains, out_rows, near_ref, across_ref):
    step = pl.program_id(0)
    grad = dot_tn(normed[...], raw[...]).astype(bf16)
    pick = lax.broadcasted_iota(jnp.int32, (8, 128), 0) == lax.broadcasted_iota(
        jnp.int32, (8, 128), 1
    )
    columns = dot_tn(gains[...].astype(bf16), pick.astype(bf16)).astype(bf16)
    for k in range(4):
        at = slice(k * 96, (k + 1) * 96)
        to = order[step * 4 + k]
        for ref, first in ((near_ref, 0), (across_ref, 8)):

            @pl.when((to >= first) & (to < first + 8))
            def _(ref=ref, first=first, at=at, k=k, to=to):
                ref[to - first, :96, :640] = grad[at]
                ref[to - first, :96, 640:] = columns[at]
                ref[to - first, 96:] = out_rows[k]


def weight_grad(order, normed, raw, gains, out_rows):
    return run(
        weight_grad_body,
        [struct((8, 144, 768), bf16)] * 2,
        [
            pl.BlockSpec((HALF, 384), lambda i, *_: (0, i)),
            whole((HALF, 640)),
            pl.BlockSpec((8, 384), lambda i, *_: (0, i)),
            pl.BlockSpec((4, 48, 768), lambda i, *_: (i, 0, 0)),
        ],
        [whole((8, 144, 768))] * 2,
        (4,),
        (normed, raw, gains, out_rows),
        prefetch=order,
        micros=6,
    )


def finish_body(held, w_query, w_key, w_value, gain, q_ref, k_ref, v_ref, gain_ref):
    sums = [held[s].astype(f32) for s in range(8)]

    def columns(first, width):
        own = [t[:, first : first + width] for t in sums]
        other = [t[:, first + width : first + 2 * width] for t in sums]
        return jnp.concatenate([own[s] + other[(s + 4) % 8] for s in range(8)], axis=1)

    along = None
    parts = ((q_ref, w_query, 0, Q_OWN), (k_ref, w_key, 384, 64), (v_ref, w_value, 512, 64))
    for ref, weight, first, width in parts:
        grad = columns(first, width)
        ref[...] = grad
        term = jnp.sum(grad * weight[...].astype(f32), axis=1, keepdims=True)
        along = term if along is None else along + term
    spot = lax.broadcasted_iota(jnp.int32, (12, 128), 0) == lax.broadcasted_iota(
        jnp.int32, (12, 128), 1
    )
    columns = (along / gain[...], sum(t[:, 640:641] for t in sums))
    rows = [jnp.sum(jnp.where(spot, c, 0.0), axis=0, keepdims=True) for c in columns]
    gain_ref[...] = jnp.concatenate(rows + [jnp.zeros((6, 128), f32)], axis=0)


def finish(held, w_query, w_key, w_value, gain):
    args = (held, w_query, w_key, w_value, gain)
    outs = [struct((12, n), f32) for n in (1536, 512, 512)] + [struct((8, 128), f32)]
    return run(
        finish_body,
        outs,
        [whole(v.shape) for v in args],
        [whole(v.shape) for v in outs],
        (1,),
        args,
        micros=4,
    )


CAP = 48
BLOCKS = 8
NEAR = BLOCKS // 2
STEP = BLOCKS * CAP


def choices(gates):
    hit = gates > 0
    upper = lax.broadcasted_iota(jnp.int32, (TOK, TOK), 0) <= lax.broadcasted_iota(
        jnp.int32, (TOK, TOK), 1
    )
    count = dot(hit.astype(bf16), upper.astype(bf16))
    slot = lax.broadcasted_iota(jnp.int32, (CAP, TOK), 0).astype(f32) + 1.0
    picks, weights = [], []
    for e in range(2):
        pick = (count[e : e + 1] == slot) & hit[e : e + 1]
        picks.append(pick.astype(bf16))
        weights.append(jnp.sum(jnp.where(pick, gates[e : e + 1], 0.0), axis=1, keepdims=True))
    return jnp.concatenate(picks, axis=0), jnp.concatenate(weights, axis=0)


def block_at(j, shape):
    def index(i, order):
        return (order[i * BLOCKS + j],) + (0,) * len(shape)

    return pl.BlockSpec((1,) + shape, index)


def expert_rows(width):
    return pl.BlockSpec((2, STEP, width), lambda i, *_: (0, i, 0))


def pair_block():
    return pl.BlockSpec((NEAR, TOK, D), lambda i, *_: (i, 0, 0))


def pick_block():
    return pl.BlockSpec((BLOCKS, 2 * CAP, TOK), lambda i, *_: (i, 0, 0))


SLOTS = 16 * CAP


def expert_begin_body(order, *refs):
    grads, gates = (refs[k * BLOCKS : (k + 1) * BLOCKS] for k in range(2))
    start, above, below, low, high = refs[2 * BLOCKS : 2 * BLOCKS + 5]
    pick_ref, grad_ref, act_ref, w_down = refs[2 * BLOCKS + 5 :]

    @pl.when(pl.program_id(0) == 0)
    def _():
        for half, far in enumerate((low, high)):
            for k, block in enumerate((start, above, far, below)):
                at = pl.multiple_of(order[16 + 4 * half + k] * 64, 64)
                for e in range(2):
                    w_down[e, pl.ds(at, 64), :] = block[0 if k == 2 else half, e]

    for j in range(BLOCKS):
        pick, weight = choices(gates[j][0])
        pick_ref[j] = pick
        graded = (dot(pick, grads[j][0]) * weight).astype(bf16)
        for e in range(2):
            grad_ref[e, j * CAP : (j + 1) * CAP, :] = graded[e * CAP : (e + 1) * CAP]
    for e in range(2):
        act_ref[e] = dot_nt(grad_ref[e], w_down[e])


def expert_begin(order, grads, gates, downs):
    return run(
        expert_begin_body,
        [
            struct((16, 2 * CAP, TOK), bf16),
            struct((2, SLOTS, D), bf16),
            struct((2, SLOTS, 512), f32),
            struct((2, 512, D), bf16),
        ],
        [block_at(j, (TOK, D)) for j in range(BLOCKS)]
        + [block_at(j, (2, TOK)) for j in range(BLOCKS)]
        + [once(v.shape) for v in downs],
        [pick_block(), expert_rows(D), expert_rows(512), whole((2, 512, D))],
        (16 // BLOCKS,),
        (grads,) * BLOCKS + (gates,) * BLOCKS + downs,
        prefetch=order,
        micros=11,
    )


def experts_body(order, *refs):
    rows = refs[:BLOCKS]
    picks, grad_acts = refs[BLOCKS : BLOCKS + 2]
    packs = refs[BLOCKS + 2 : BLOCKS + 10]
    near_ref, across_ref, in_ref, act_ref, da_ref, db_ref, w_gate, w_up = refs[BLOCKS + 10 :]

    @pl.when(pl.program_id(0) == 0)
    def _():
        for half in range(2):
            own, above, below = packs[3 * half : 3 * half + 3]
            far = slice(192 * half, 192 * half + 192)
            for k, block in enumerate((own, above, None, below)):
                at = pl.ds(pl.multiple_of(order[16 + 4 * half + k] * 192, 192), 192)
                for e in range(2):
                    w_gate[e, at, :] = packs[6][e, far] if k == 2 else block[e, :192]
                    w_up[e, at, :] = packs[7][e, far] if k == 2 else block[e, 192:]

    for j in range(BLOCKS):
        taken = dot(picks[j], rows[j][0]).astype(bf16)
        for e in range(2):
            in_ref[e, j * CAP : (j + 1) * CAP, :] = taken[e * CAP : (e + 1) * CAP]
    backs = []
    for e in range(2):
        taken, grad_act = in_ref[e], grad_acts[e]
        gate_pre = dot(taken, w_gate[e])
        up_pre = dot(taken, w_up[e])
        sig = 1.0 / (1.0 + jnp.exp(-gate_pre))
        silu = gate_pre * sig
        act_ref[e] = (silu * up_pre).astype(bf16)
        da = (grad_act * up_pre * sig * (1.0 + gate_pre * (1.0 - sig))).astype(bf16)
        db = (grad_act * silu).astype(bf16)
        da_ref[e] = da
        db_ref[e] = db
        backs.append((dot_nt(da, w_gate[e]) + dot_nt(db, w_up[e])).astype(bf16))
    for j in range(BLOCKS):
        at = slice(j * CAP, (j + 1) * CAP)
        back = dot_tn(picks[j], jnp.concatenate([backs[0][at], backs[1][at]], axis=0))
        target = near_ref if j < NEAR else across_ref
        target[j % NEAR] = back.astype(bf16)


def experts(order, rows, picks, grad_acts, packs):
    return run(
        experts_body,
        [struct((8, TOK, D), bf16)] * 2
        + [struct((2, SLOTS, D), bf16)]
        + [struct((2, SLOTS, 512), bf16)] * 3,
        [block_at(j, (TOK, D)) for j in range(BLOCKS)]
        + [pick_block(), expert_rows(512)]
        + [once(v.shape) for v in packs],
        [pair_block(), pair_block(), expert_rows(D)] + [expert_rows(512)] * 3,
        (16 // BLOCKS,),
        (rows,) * BLOCKS + (picks, grad_acts) + packs,
        prefetch=order,
        scratch=[pltpu.VMEM((2, D, 512), bf16)] * 2,
        micros=22,
    )


def expert_out_body(order, *refs):
    gates = refs[:BLOCKS]
    picks, act, w_down, out_ref = refs[BLOCKS:]
    step = pl.program_id(0)
    outs = [dot(act[e], w_down[e]) for e in range(2)]
    for j in range(BLOCKS):
        pick = picks[j]
        weights = [
            jnp.sum(pick[e * CAP : (e + 1) * CAP].astype(f32) * gates[j][0, e : e + 1], axis=1, keepdims=True)
            for e in range(2)
        ]
        at = slice(j * CAP, (j + 1) * CAP)
        both = jnp.concatenate([outs[e][at] * weights[e] for e in range(2)], axis=0)
        out_ref[order[step * BLOCKS + j]] = dot_tn(pick, both.astype(bf16)).astype(bf16)


def expert_out(order, gates, picks, act, w_down):
    return run(
        expert_out_body,
        [struct((16, TOK, D), bf16)],
        [block_at(j, (2, TOK)) for j in range(BLOCKS)]
        + [pick_block(), expert_rows(512), once(w_down.shape)],
        [whole((16, TOK, D))],
        (16 // BLOCKS,),
        (gates,) * BLOCKS + (picks, act, w_down),
        prefetch=order,
        micros=2,
    )[0]


def one(rows, width):
    return pl.BlockSpec((1, rows, width), lambda e, *_: (e, 0, 0))


def grad_down_body(order, act, graded, down_ref):
    e = pl.program_id(0)
    down = dot_tn(act[0], graded[0]).astype(bf16)
    for k in range(8):
        down_ref[order[k], e] = down[k * 64 : (k + 1) * 64]


def expert_grad_down(order, act, graded):
    return run(
        grad_down_body,
        [struct((8, 2, 64, D), bf16)],
        [one(SLOTS, 512), one(SLOTS, D)],
        [whole((8, 2, 64, D))],
        (2,),
        (act, graded),
        prefetch=order,
        micros=2,
    )[0]


def grad_pair_body(order, taken, da, db, pack_ref, fore_ref, back_ref):
    e = pl.program_id(0)
    gate = dot_tn(taken[0], da[0]).astype(bf16)
    up = dot_tn(taken[0], db[0]).astype(bf16)
    for k in range(8):
        to = order[k]
        at = slice(k * 192, (k + 1) * 192)

        @pl.when(to < 6)
        def _(to=to, at=at):
            pack_ref[to // 2, lax.rem(to, 2), e, :192] = gate[at]
            pack_ref[to // 2, lax.rem(to, 2), e, 192:] = up[at]

        for far, ref in ((6, fore_ref), (7, back_ref)):

            @pl.when(to == far)
            def _(ref=ref, at=at):
                ref[e, :192] = gate[at]
                ref[e, 192:] = up[at]


def expert_grad_pair(order, taken, da, db):
    return run(
        grad_pair_body,
        [struct((3, 2, 2, 384, 512), bf16)] + [struct((2, 384, 512), bf16)] * 2,
        [one(SLOTS, D), one(SLOTS, 512), one(SLOTS, 512)],
        [whole((3, 2, 2, 384, 512)), whole((2, 384, 512)), whole((2, 384, 512))],
        (2,),
        (taken, da, db),
        prefetch=order,
        micros=2,
    )


def rms_scale(values):
    return lax.rsqrt(jnp.mean(values * values, axis=-1, keepdims=True) + norm_eps)


def three_parts(values):
    high = lax.reduce_precision(values, 8, 7)
    rest = values - high
    middle = lax.reduce_precision(rest, 8, 7)
    return [v.astype(bf16) for v in (high, middle, rest - middle)]


def shards(
    tokens,
    cotangent,
    segments,
    routes,
    gate_weights,
    w_query,
    w_key,
    w_value,
    w_out,
    norm_one,
    norm_two,
    w_gate,
    w_up,
    w_down,
):
    inputs = tokens[0].astype(f32)
    upstream = cotangent[0].astype(f32)
    yh, x = lax.axis_index("yh"), lax.axis_index("x")
    where = jnp.stack([x, yh]).astype(jnp.int32)
    order = jnp.stack(
        [
            m * 2 + ahead("c", j // NEAR)
            for i in range(16 // BLOCKS)
            for j in range(BLOCKS)
            for m in (NEAR * i + j % NEAR,)
        ]
        + [ahead("yh", k // 4) * 4 + ahead("x", k % 4) for k in range(8)]
    ).astype(jnp.int32)
    batch_place = jnp.stack(
        [
            distance("c", b % 2) * 8 + b // 2
            for b in range(16)
        ]
    ).astype(jnp.int32)
    seq_place = jnp.stack(
        [
            jnp.array([0, 1, 3, 2])[distance("x", s % 4)] * 2 + distance("yh", s // 4)
            for s in range(8)
        ]
    ).astype(jnp.int32)

    def for_heads(weight, width):
        by_head = jnp.swapaxes(weight.reshape(-1, 8, width), 0, 1)
        return [by_head, jnp.concatenate([by_head[4:], by_head[:4]], axis=0)]

    gains = jnp.pad(jnp.stack([norm_one, norm_two], axis=1), ((0, 0), (0, 126)))
    strip = jnp.concatenate(
        for_heads(w_query, Q_OWN)
        + for_heads(w_key, HEAD_DIM)
        + for_heads(w_value, HEAD_DIM)
        + [jnp.broadcast_to(gains[None], (8,) + gains.shape)],
        axis=2,
    )
    strip, w_out = tie(strip, w_out)
    strip = lax.all_to_all(strip, SEQ, 0, 0, tiled=True).reshape(96, 768)
    below, above = shift(tokens[0], "x", 1), shift(tokens[0], "x", -1)
    strip, below, above = tie(strip, below, above)
    half = TOK // 2
    pieces = (
        tokens[0], above, shift(below[:half], "x", 1), shift(above[half:], "x", -1), below
    )
    expert_ids = jnp.arange(EXPERTS, dtype=jnp.int32)[:, None, None]
    gate_dense = jnp.sum(jnp.where(routes[0][None] == expert_ids, gate_weights[0][None], 0.0), axis=2)
    strip = jnp.concatenate(
        [
            strip,
            jnp.concatenate(three_parts(gate_dense), axis=0),
            w_out.reshape(96, 192),
            shift(w_out, "yh", 1).reshape(96, 192),
        ],
        axis=1,
    )
    gathered = lax.all_gather(strip, BATCH, axis=0, tiled=True)
    grad_all = lax.all_gather(cotangent[0], BATCH, axis=0)

    feature = jnp.arange(D, dtype=jnp.int32)
    moved = feature % 192 // 12 * 96 + feature // 192 * 12 + feature % 12
    moving = (moved[:, None] == feature[None, :]).astype(bf16)
    xp, scale_half = prepare(where, pieces, moving)

    pack = jnp.concatenate([w_gate, w_up], axis=1)
    half_pack = pack.shape[1] // 2
    pack, w_down, _ = tie(pack, w_down, strip)
    down_other = shift(w_down, "yh", 1)
    pack_other = shift(pack, "yh", 1)
    downs = jnp.stack([w_down, down_other])
    downs, _, _ = tie(downs, pieces[2], pieces[3])
    down_below, down_above = shift(downs, "x", 1), shift(downs, "x", -1)

    def natural(row):
        return jnp.swapaxes(row.reshape(16, 8, 12), 0, 1).reshape(D)

    place = jnp.arange(2 * HALF, dtype=jnp.int32) + HALF * yh
    place = jnp.where(place >= 2 * HALF, place - 2 * HALF, place)
    seg = jnp.roll(segments[0], -HALF * yh)
    earlier = jnp.sum((seg[None, :] < seg[:, None]).astype(jnp.int32), axis=1)
    freq_index = jnp.arange(HEAD_DIM // 2, dtype=f32) * (2.0 / HEAD_DIM)
    frequency = jnp.tile(rope_base ** (-freq_index), 4)
    angle = (place - earlier).astype(f32)[:, None] * frequency
    cosine, sine = jnp.cos(angle), jnp.sin(angle)
    seg_row = seg[None, :]
    seg_col = jnp.broadcast_to(seg[:, None], (2 * HALF, 128))

    down_below, down_above, xp = tie(down_below, down_above, xp)
    down_low, down_high = shift(down_below[:1], "x", 1), shift(down_above[1:], "x", -1)
    gathered, xp, down_low, down_high = tie(gathered, xp, down_low, down_high)

    normed, queries, own, sent = project(xp, scale_half, gathered, cosine, sine)
    other = shift(sent, "yh", 1)
    pack, _ = tie(pack, normed)
    pack_below, pack_above = shift(pack, "x", 1), shift(pack, "x", -1)
    downs = (downs, down_above, down_below, down_low, down_high)
    out_rows = gathered[:, 896:1088].reshape(192, D)
    out_other = gathered[:, 1088:].reshape(192, D)
    gain_one = natural(gathered[:, 640].astype(f32))
    gain_two = natural(gathered[:, 641].astype(f32))
    gates = jnp.sum(gathered[:, 768:896].reshape(16, 3, EXPERTS, TOK).astype(f32), axis=1)
    gates = lax.dynamic_slice_in_dim(gates, lax.axis_index(BATCH) * 2, 2, axis=1)
    mixed, partial = attend(where, queries, own, other, seg_col, seg_row, out_rows, out_other)
    partial, pack_below, pack_above = tie(partial, pack_below, pack_above)
    partial = lax.all_to_all(partial, "x", 0, 0, tiled=True)
    hidden = inputs + jnp.sum(partial.astype(f32), axis=0)
    hidden, pack_other = tie(hidden, pack_other)
    both = ring_next((pack_other, pack_other), "x")

    scale_two = rms_scale(hidden)
    normed_two = (hidden * scale_two * gain_two).astype(bf16)
    normed_all = lax.all_gather(normed_two, BATCH, axis=0)
    grad_all, other_below, other_above = tie(grad_all, *both)
    low = jnp.concatenate([pack_below[:, :half_pack], other_below[:, :half_pack]], axis=1)
    high = jnp.concatenate([pack_above[:, half_pack:], other_above[:, half_pack:]], axis=1)
    low, high = ring_next((low, high), "x")
    picks, graded, grad_acts, down_full = expert_begin(order, grad_all, gates, downs)
    picks, graded, grad_acts, low, high = tie(picks, graded, grad_acts, low, high)
    packs = (pack, pack_above, pack_below, pack_other, other_above, other_below, low, high)
    near, across, taken, act, da, db = experts(
        order, normed_all, picks, grad_acts, packs
    )
    got = shift(across, "c", 1)
    down_place = jnp.stack([s % 4 * 2 + distance("yh", s // 4) for s in range(8)])
    grad_down = expert_grad_down(down_place.astype(jnp.int32), act, graded)
    grad_down, got = tie(grad_down, got)
    grad_down = grad_down.reshape(8 * 2 * 64, D)
    held = add_up(near, got).astype(bf16)
    taken, _ = tie(taken, held)
    held = lax.all_to_all(held, ("yl", "z"), 0, 0, tiled=True)
    grad_pack, fore, back = expert_grad_pair(seq_place, taken, da, db)
    act, grad_pack = tie(act, grad_pack)
    pack_sent = shift(fore, "x", 1), shift(back, "x", -1)
    out_part = expert_out(order, gates, picks, act, down_full)
    out_part, held, *pack_sent = tie(out_part, held, *pack_sent)
    output = lax.psum_scatter(out_part, BATCH, scatter_dimension=0, tiled=True)
    grad_normed_two = jnp.sum(held.astype(f32), axis=0)

    scaled_two = gain_two * grad_normed_two
    grad_gain_two = jnp.sum(grad_normed_two * hidden * scale_two, axis=0)
    grad_hidden = (
        upstream
        + scale_two * scaled_two
        - hidden * scale_two**3 * jnp.mean(scaled_two * hidden, axis=-1, keepdims=True)
    )
    pieces = jnp.broadcast_to(grad_hidden.astype(bf16)[None], (4, TOK, D))
    pieces = lax.all_to_all(pieces, "x", 0, 0, tiled=True)
    pack_hops = [
        [jnp.stack([add_up(grad_pack[1, 0, e], pack_sent[0][e]).astype(bf16), grad_pack[1, 1, e]]),
         jnp.stack([grad_pack[2, 0, e], add_up(grad_pack[2, 1, e], pack_sent[1][e]).astype(bf16)])]
        for e in range(2)
    ]
    pack_hops = pack_hops[0] + pack_hops[1]
    first_hops = ring_next(pack_hops[:2], "x")
    back = attend_back(
        where, queries, mixed, own, other, seg_col, seg_row, out_rows, out_other,
        pieces, cosine, sine,
    )
    *back, hop_0, hop_1, pack_low, pack_high = tie(*back, *first_hops, *pack_hops[2:])
    first_hops = hop_0, hop_1
    grad_query, grad_own, grad_sent, grad_out_w = back
    last_hops = ring_next((pack_low, pack_high), "x")
    grad_got = shift(grad_sent, "yh", 1)
    first_total = add_up(grad_pack[0, :, 0], *first_hops)
    first_total, _ = tie(first_total, grad_sent)
    first_last = shift(first_total[1].astype(bf16), "yh", 1)
    back = unproject(where, grad_query, grad_own, grad_got, gathered, moving)
    grad_raw, grad_part, first_last, output, *last_hops = tie(
        *back, first_last, output, *last_hops
    )
    grad_down, _ = tie(grad_down, output)
    grad_down = lax.psum_scatter(grad_down, "x", scatter_dimension=0, tiled=True)
    part_sent = ring_send(grad_part, "x")
    gain_two_part = jnp.swapaxes(grad_gain_two.reshape(8, 16, 12), 0, 1).reshape(1, D)
    gain_rows = jnp.concatenate([gain_two_part, jnp.zeros((7, D), f32)], axis=0)
    near, across = weight_grad(batch_place, normed, grad_raw, gain_rows, grad_out_w)
    near, across, *rest = tie(near, across, *last_hops, *part_sent)
    last_hops, part_sent = rest[:2], rest[2:]
    got = shift(across, "c", 1)
    last_total = add_up(grad_pack[0, :, 1], *last_hops)
    last_last = shift(last_total[1].astype(bf16), "yh", 1)
    got, last_total = tie(got, last_total)
    held = add_up(near, got).astype(bf16)
    first_total, output, _ = tie(first_total, output, held)
    held, *part_sent = tie(held, *part_sent)
    held = lax.all_to_all(held, ("yl", "z"), 0, 0, tiled=True)
    grad_normed_one = add_up(grad_part[0], *ring_next(ring_add(grad_part, part_sent), "x"))
    scaled_one = gain_one * grad_normed_one
    scale_one = rms_scale(inputs)
    grad_inputs = (
        grad_hidden
        + scale_one * scaled_one
        - inputs * scale_one**3 * jnp.mean(scaled_one * inputs, axis=-1, keepdims=True)
    ).astype(bf16)
    output = (hidden + output[0].astype(f32)).astype(bf16)
    gain = jnp.broadcast_to(norm_one.astype(f32)[:, None], (12, 128))
    grad_down = grad_down.reshape(2, 2, 64, D)
    grad_pack = [add_up(first_total[0], first_last), add_up(last_total[0], last_last)]
    grad_pack = jnp.stack(grad_pack)
    sum_gate, sum_up = grad_pack[:, :192], grad_pack[:, 192:]
    held, output, gain, grad_inputs, sum_gate, sum_up = tie(
        held, output, gain, grad_inputs, sum_gate, sum_up
    )
    down_own, down_far = grad_down[0], grad_down[1]
    grad_w = jnp.sum(held.astype(f32), axis=0).astype(bf16)
    out_sum = grad_w[96:].astype(f32).reshape(2, 2, 12, 768)
    out_got = shift(out_sum[1].astype(bf16), "yh", 1)
    grad_w = lax.all_to_all(grad_w[:96].reshape(8, 12, 768), SEQ, 0, 0, tiled=True)
    down_last = shift(down_far, "yh", 1)
    sum_out = add_up(out_sum[0], out_got)
    sum_out = jnp.swapaxes(sum_out, 0, 1).reshape(12, D)
    sum_down = add_up(down_own, down_last)
    grad_w, sum_out, sum_down = tie(grad_w, sum_out, sum_down)
    grad_q, grad_k, grad_v, grad_gain = finish(grad_w, w_query, w_key, w_value, gain)
    return (
        output[None],
        grad_inputs[None],
        grad_q,
        grad_k,
        grad_v,
        sum_out,
        grad_gain[0, :12],
        grad_gain[1, :12],
        sum_gate,
        sum_up,
        sum_down,
    )


def solution(mesh):
    fine = Mesh(mesh.devices.reshape(2, 4, 2, 4, 2), SEQ + BATCH)
    both = SEQ + BATCH
    placed = (
        P(BATCH, SEQ, None),
        P(BATCH, SEQ, None),
        P(BATCH, None),
        P(BATCH, SEQ, None),
        P(BATCH, SEQ, None),
        P(both, None),
        P(both, None),
        P(both, None),
        P(both, None),
        P(both),
        P(both),
        P(BATCH, SEQ, None),
        P(BATCH, SEQ, None),
        P(BATCH, SEQ, None),
    )
    return jax.shard_map(
        shards,
        mesh=fine,
        in_specs=placed,
        out_specs=(
            P(BATCH, SEQ, None),
            P(BATCH, SEQ, None),
            P(both, None),
            P(both, None),
            P(both, None),
            P(both, None),
            P(both),
            P(both),
            P(BATCH, SEQ, None),
            P(BATCH, SEQ, None),
            P(BATCH, SEQ, None),
        ),
        check_vma=False,
    )
```

```python
import functools

import jax
import jax.numpy as jnp
from jax import lax
from jax.experimental import pallas as pl
from jax.experimental.pallas import tpu as pltpu
from jax.sharding import Mesh, PartitionSpec as P

HEAD_DIM = 64
TOPK = 8
GROUP = 3
Q_OWN = GROUP * HEAD_DIM
TOK = 128
HALF = 512
D = 1536
EXPERTS = 32
norm_eps = 1e-06
rope_base = 10000.0
masked_score = -1e30
SEQ = ("yh", "x")
BATCH = ("yl", "z", "c")
SIZE = {"yh": 2, "x": 4, "yl": 2, "z": 4, "c": 2}
bf16 = jnp.bfloat16
f32 = jnp.float32


def dot(a, b):
    return jnp.dot(a, b, preferred_element_type=f32)


def shift(value, axis, by):
    size = SIZE[axis]
    return lax.ppermute(value, axis, [(i, (i + by) % size) for i in range(size)])


def ring_pieces(block, axis):
    half = block.shape[0] // 2
    below = shift(block, axis, 1)
    above = shift(block, axis, -1)
    low = shift(below[:half], axis, 1)
    high = shift(above[half:], axis, -1)
    return block, above, low, high, below


def add_up(*parts):
    total = parts[0].astype(f32)
    for part in parts[1:]:
        total = total + part.astype(f32)
    return total


def ring_send(blocks, axis):
    half = blocks[0].shape[0] // 2
    return shift(blocks[2][:half], axis, 1), shift(blocks[2][half:], axis, -1)


def ring_add(blocks, got):
    half = blocks[0].shape[0] // 2
    up = [add_up(blocks[1][:half], got[0]).astype(bf16), blocks[1][half:]]
    down = [blocks[3][:half], add_up(blocks[3][half:], got[1]).astype(bf16)]
    return jnp.concatenate(up, axis=0), jnp.concatenate(down, axis=0)


def ring_next(hops, axis):
    return shift(hops[0], axis, 1), shift(hops[1], axis, -1)


def reduce_ring(blocks, axis):
    hops = ring_add(blocks, ring_send(blocks, axis))
    return add_up(blocks[0], *ring_next(hops, axis))


def tie(*values):
    return lax.optimization_barrier(values)


def ahead(axis, by):
    return lax.rem(lax.axis_index(axis) + by, SIZE[axis])


def distance(axis, place):
    return lax.rem(place - lax.axis_index(axis) + SIZE[axis], SIZE[axis])


def dot_nt(a, b):
    return lax.dot_general(a, b, (((1,), (1,)), ((), ())), preferred_element_type=f32)


def dot_tn(a, b):
    return lax.dot_general(a, b, (((0,), (0,)), ((), ())), preferred_element_type=f32)


def whole(shape):
    zeros = (0,) * len(shape)
    return pl.BlockSpec(shape, lambda *_: zeros)


def once(shape):
    zeros = (0,) * len(shape)
    return pl.BlockSpec(shape, lambda *_: zeros, pipeline_mode=pl.Buffered(1))


def run(body, out_shapes, in_specs, out_specs, grid, args, prefetch=None, scratch=(), micros=0):
    spec = pltpu.PrefetchScalarGridSpec(
        num_scalar_prefetch=0 if prefetch is None else 1,
        grid=grid,
        in_specs=in_specs,
        out_specs=out_specs,
        scratch_shapes=list(scratch),
    )
    head = () if prefetch is None else (prefetch,)
    return pl.pallas_call(
        body,
        grid_spec=spec,
        out_shape=out_shapes,
        compiler_params=pltpu.CompilerParams(vmem_limit_bytes=56 << 20),
        cost_estimate=pl.CostEstimate(flops=1100000000 * micros, bytes_accessed=0, transcendentals=0),
    )(*head, *args)


def struct(shape, dtype):
    return jax.ShapeDtypeStruct(shape, dtype)


def turned(values):
    lane = lax.broadcasted_iota(jnp.int32, values.shape, 1)
    first = (lane % HEAD_DIM) < HEAD_DIM // 2
    return jnp.where(first, -pltpu.roll(values, 96, 1), pltpu.roll(values, 32, 1))


def by_lanes(values, function):
    width = values.shape[1]
    return jnp.concatenate(
        [function(values[:, k : k + 128]) for k in range(0, width, 128)], axis=1
    )


def prepare_body(where, own, above, far_low, far_high, below, moving, xp_ref, scale_ref):
    for k in range(4):
        place = pl.ds(lax.rem(where[0] + k, 4) * TOK, TOK)
        if k == 2:
            block = jnp.concatenate([far_low[...], far_high[...]], axis=0)
        else:
            block = (own, above, None, below)[k][...]
        wide = block.astype(f32)
        scale = lax.rsqrt(jnp.mean(wide * wide, axis=1, keepdims=True) + norm_eps)
        scale_ref[place, :] = jnp.broadcast_to(scale, (TOK, 128))
        xp_ref[place, :] = dot(block, moving[...]).astype(bf16)


def prepare(where, pieces, moving):
    specs = [whole(p.shape) for p in pieces] + [whole(moving.shape)]
    return run(
        prepare_body,
        [struct((HALF, D), bf16), struct((HALF, 128), f32)],
        specs,
        [whole((HALF, D)), whole((HALF, 128))],
        (1,),
        (*pieces, moving),
        prefetch=where,
        micros=7,
    )


def project_body(xp, scale, weight, cosine, sine, n_ref, q_ref, kv_ref, sent_ref):
    pick = lax.broadcasted_iota(jnp.int32, (8, 128), 0) == lax.broadcasted_iota(
        jnp.int32, (8, 128), 1
    )
    gains = dot_nt(pick.astype(bf16), weight[:, 640:])
    normed = (xp[...].astype(f32) * scale[:, :1] * gains[:1]).astype(bf16)
    n_ref[...] = normed
    raw = dot(normed, weight[:, :640])
    cos, sin = cosine[...], sine[...]
    rotated = by_lanes(raw[:, :512], lambda u: u * cos + turned(u) * sin).astype(bf16)
    q_ref[...] = rotated[:, :384]
    both = jnp.concatenate([rotated[:, 384:], raw[:, 512:].astype(bf16)], axis=1)
    kv_ref[...] = both
    sent_ref[...] = swap_groups(both)


def swap_groups(both):
    wide = both.astype(f32)
    return by_lanes(wide, lambda u: pltpu.roll(u, 64, 1)).astype(bf16)


def tile(width):
    return pl.BlockSpec((TOK, width), lambda i, *_: (i, 0))


def project(xp, scale, gathered, cosine, sine):
    return run(
        project_body,
        [
            struct((HALF, D), bf16),
            struct((HALF, 384), bf16),
            struct((HALF, 256), bf16),
            struct((HALF, 256), bf16),
        ],
        [whole((HALF, D)), whole((HALF, 128)), whole((D, 768)), whole((HALF, 128)), whole((HALF, 128))],
        [whole((HALF, D)), whole((HALF, 384)), whole((HALF, 256)), whole((HALF, 256))],
        (1,),
        (xp, scale, gathered, cosine, sine),
        micros=5,
    )


def head_rows(values):
    empty = jnp.zeros((TOK, HEAD_DIM), values.dtype)
    rows = []
    for h in range(6):
        head = values[:, h * HEAD_DIM : (h + 1) * HEAD_DIM]
        rows.append(jnp.concatenate([head, empty] if h < 3 else [empty, head], axis=1))
    return jnp.concatenate(rows, axis=0)


def head_columns(both):
    rows = [
        both[h // 3 * HEAD_DIM : (h // 3 + 1) * HEAD_DIM, h * TOK : (h + 1) * TOK]
        for h in range(6)
    ]
    return jnp.concatenate(rows, axis=0).T


def softmax_parts(tile_at, second, queries, own, other, seg_col, seg_row):
    seen = (tile_at + 1) * TOK
    query = lax.broadcasted_iota(jnp.int32, (seen, TOK), 1) + tile_at * TOK
    key = lax.broadcasted_iota(jnp.int32, (seen, TOK), 0)
    segs = seg_row[:, tile_at * TOK : seen]
    own_ok = (seg_col[:seen, :1] == segs) & (key <= query)
    other_ok = (seg_col[HALF:, :1] == segs) & second
    scores = []
    for kv, ok, keys in ((own, own_ok, seen), (other, other_ok, HALF)):
        s = dot_nt(kv[:keys, :128], queries)
        low = jnp.where(ok, 0.0, masked_score)
        scores.append(s + jnp.concatenate([low] * 6, axis=1))
    top = jnp.maximum(
        jnp.max(scores[0], axis=0, keepdims=True), jnp.max(scores[1], axis=0, keepdims=True)
    )
    exps = [jnp.exp(s - top) for s in scores]
    total = jnp.sum(exps[0], axis=0, keepdims=True) + jnp.sum(exps[1], axis=0, keepdims=True)
    inverse = 1.0 / total
    return [e * inverse for e in exps]


def each_tile(function):
    for tile_at in range(4):
        pl.when(pl.program_id(0) == tile_at)(functools.partial(function, tile_at))


def attend_body(where, q, own, other, seg_col, seg_row, w_own, w_other, att_ref, part_ref):
    second = where[1] == 1

    def one_tile(tile_at):
        queries = head_rows(q[...]) * jnp.asarray(0.125, bf16)
        probs = softmax_parts(tile_at, second, queries, own, other, seg_col, seg_row)
        mixed = dot_tn(own[: (tile_at + 1) * TOK, 128:], probs[0].astype(bf16))
        mixed = mixed + dot_tn(other[:, 128:], probs[1].astype(bf16))
        att_ref[...] = head_columns(mixed).astype(bf16)

    each_tile(one_tile)
    part = dot(att_ref[:, :Q_OWN], w_own[...]) + dot(att_ref[:, Q_OWN:], w_other[...])
    part_ref[0] = part.astype(bf16)


def step_block(shape):
    return pl.BlockSpec((1,) + shape, lambda i, *_: (i, 0, 0))


def attend(where, q, own, other, seg_col, seg_row, w_own, w_other):
    return run(
        attend_body,
        [struct((HALF, 384), bf16), struct((4, TOK, D), bf16)],
        [
            tile(384),
            whole((HALF, 256)),
            whole((HALF, 256)),
            whole((2 * HALF, 128)),
            whole((1, 2 * HALF)),
            whole((Q_OWN, D)),
            whole((Q_OWN, D)),
        ],
        [tile(384), step_block((TOK, D))],
        (4,),
        (q, own, other, seg_col, seg_row, w_own, w_other),
        prefetch=where,
        micros=15,
    )


def attend_back_body(
    where, q, att, own, other, seg_col, seg_row, w_own, w_other, z, cosine,
    sine, q_ref, own_ref, sent_ref, out_ref, sums, out_sum,
):
    step = pl.program_id(0)

    @pl.when(step == 0)
    def _():
        sums[...] = jnp.zeros_like(sums)
        out_sum[...] = jnp.zeros_like(out_sum)

    second = where[1] == 1
    grad_z = z[0]
    out_sum[...] += dot_tn(att[...], grad_z)
    grad_att = jnp.concatenate([dot_nt(grad_z, w_own[...]), dot_nt(grad_z, w_other[...])], axis=1)
    grad_att = grad_att.astype(bf16)

    def one_tile(tile_at):
        queries = head_rows(q[...]) * jnp.asarray(0.125, bf16)
        grads = head_rows(grad_att)
        probs = softmax_parts(tile_at, second, queries, own, other, seg_col, seg_row)
        sides = ((own, (tile_at + 1) * TOK), (other, HALF))
        grad_probs = [dot_nt(kv[:n, 128:], grads) for kv, n in sides]
        row_dot = jnp.sum(probs[0] * grad_probs[0], axis=0, keepdims=True)
        row_dot = row_dot + jnp.sum(probs[1] * grad_probs[1], axis=0, keepdims=True)
        total = None
        for side, (kv, n) in enumerate(sides):
            grad_score = (probs[side] * (grad_probs[side] - row_dot)).astype(bf16)
            term = dot_tn(kv[:n, :128], grad_score)
            total = term if total is None else total + term
            sums[side, :n, :128] += dot(grad_score, queries)
            sums[side, :n, 128:] += dot(probs[side].astype(bf16), grads)
        grad_q = head_columns(total * 0.125)
        at = slice(tile_at * TOK, (tile_at + 1) * TOK)
        cos, sin = cosine[at, :], sine[at, :]
        q_ref[...] = by_lanes(grad_q, lambda u: u * cos - turned(u) * sin).astype(bf16)

    each_tile(one_tile)

    @pl.when(step == 3)
    def _():
        for b in range(16):
            parts = [
                out_sum[g * Q_OWN + 12 * b : g * Q_OWN + 12 * b + 12, c * 768 : (c + 1) * 768]
                for g in range(2)
                for c in range(2)
            ]
            out_ref[b] = jnp.concatenate(parts, axis=0).astype(bf16)
        for n in range(2):
            at = slice(n * HALF, (n + 1) * HALF)
            grad_k = sums[n, :, :128]
            grad_k = grad_k * cosine[at, :] - turned(grad_k) * sine[at, :]
            both = jnp.concatenate([grad_k, sums[n, :, 128:]], axis=1)
            if n == 0:
                own_ref[...] = both
            else:
                sent_ref[...] = swap_groups(both)


def attend_back(where, q, att, own, other, seg_col, seg_row, w_own, w_other, pieces, cosine, sine):
    return run(
        attend_back_body,
        [
            struct((HALF, 384), bf16),
            struct((HALF, 256), f32),
            struct((HALF, 256), bf16),
            struct((16, 48, 768), bf16),
        ],
        [
            tile(384),
            tile(384),
            whole((HALF, 256)),
            whole((HALF, 256)),
            whole((2 * HALF, 128)),
            whole((1, 2 * HALF)),
            whole((Q_OWN, D)),
            whole((Q_OWN, D)),
        ]
        + [step_block((TOK, D))]
        + [whole((2 * HALF, 128)), whole((2 * HALF, 128))],
        [tile(384), whole((HALF, 256)), whole((HALF, 256)), whole((16, 48, 768))],
        (4,),
        (q, att, own, other, seg_col, seg_row, w_own, w_other, pieces, cosine, sine),
        prefetch=where,
        scratch=[
            pltpu.VMEM((2, HALF, 256), f32),
            pltpu.VMEM((384, D), f32),
        ],
        micros=22,
    )


def unproject_body(where, q, own, got, weight, moving, raw_ref, part_ref):
    both = (own[...] + got[...].astype(f32)).astype(bf16)
    raw = jnp.concatenate([q[...], both], axis=1)
    raw_ref[...] = raw
    grad = dot_nt(raw, weight[:, :640])
    part = dot_nt(grad.astype(bf16), moving[...]).astype(bf16)
    for k in range(4):
        part_ref[lax.rem(k + 4 - where[0], 4)] = part[k * TOK : (k + 1) * TOK]


def unproject(where, q, own, got, gathered, moving):
    return run(
        unproject_body,
        [struct((HALF, 640), bf16), struct((4, TOK, D), bf16)],
        [
            whole((HALF, 384)),
            whole((HALF, 256)),
            whole((HALF, 256)),
            whole((D, 768)),
            whole((D, D)),
        ],
        [whole((HALF, 640)), whole((4, TOK, D))],
        (1,),
        (q, own, got, gathered, moving),
        prefetch=where,
        micros=10,
    )


def weight_grad_body(order, normed, raw, gains, out_rows, near_ref, across_ref):
    step = pl.program_id(0)
    grad = dot_tn(normed[...], raw[...]).astype(bf16)
    pick = lax.broadcasted_iota(jnp.int32, (8, 128), 0) == lax.broadcasted_iota(
        jnp.int32, (8, 128), 1
    )
    columns = dot_tn(gains[...].astype(bf16), pick.astype(bf16)).astype(bf16)
    for k in range(8):
        at = slice(k * 96, (k + 1) * 96)
        to = order[step * 8 + k]
        for ref, first in ((near_ref, 0), (across_ref, 8)):

            @pl.when((to >= first) & (to < first + 8))
            def _(ref=ref, first=first, at=at, k=k, to=to):
                ref[to - first, :96, :640] = grad[at]
                ref[to - first, :96, 640:] = columns[at]
                ref[to - first, 96:] = out_rows[k]


def weight_grad(order, normed, raw, gains, out_rows):
    return run(
        weight_grad_body,
        [struct((8, 144, 768), bf16)] * 2,
        [
            pl.BlockSpec((HALF, D // 2), lambda i, *_: (0, i)),
            whole((HALF, 640)),
            pl.BlockSpec((8, D // 2), lambda i, *_: (0, i)),
            pl.BlockSpec((8, 48, 768), lambda i, *_: (i, 0, 0)),
        ],
        [whole((8, 144, 768))] * 2,
        (2,),
        (normed, raw, gains, out_rows),
        prefetch=order,
        micros=6,
    )


def finish_body(held, w_query, w_key, w_value, gain, q_ref, k_ref, v_ref, gain_ref):
    sums = [held[s].astype(f32) for s in range(8)]

    def columns(first, width):
        own = [t[:, first : first + width] for t in sums]
        other = [t[:, first + width : first + 2 * width] for t in sums]
        return jnp.concatenate([own[s] + other[(s + 4) % 8] for s in range(8)], axis=1)

    along = None
    parts = ((q_ref, w_query, 0, Q_OWN), (k_ref, w_key, 384, 64), (v_ref, w_value, 512, 64))
    for ref, weight, first, width in parts:
        grad = columns(first, width)
        ref[...] = grad
        term = jnp.sum(grad * weight[...].astype(f32), axis=1, keepdims=True)
        along = term if along is None else along + term
    spot = lax.broadcasted_iota(jnp.int32, (12, 128), 0) == lax.broadcasted_iota(
        jnp.int32, (12, 128), 1
    )
    columns = (along / gain[...], sum(t[:, 640:641] for t in sums))
    rows = [jnp.sum(jnp.where(spot, c, 0.0), axis=0, keepdims=True) for c in columns]
    gain_ref[...] = jnp.concatenate(rows + [jnp.zeros((6, 128), f32)], axis=0)


def finish(held, w_query, w_key, w_value, gain):
    args = (held, w_query, w_key, w_value, gain)
    outs = [struct((12, n), f32) for n in (1536, 512, 512)] + [struct((8, 128), f32)]
    return run(
        finish_body,
        outs,
        [whole(v.shape) for v in args],
        [whole(v.shape) for v in outs],
        (1,),
        args,
        micros=4,
    )


CAP = 48
BLOCKS = 8
NEAR = BLOCKS // 2
STEP = BLOCKS * CAP


def choices(gates):
    hit = gates > 0
    upper = lax.broadcasted_iota(jnp.int32, (TOK, TOK), 0) <= lax.broadcasted_iota(
        jnp.int32, (TOK, TOK), 1
    )
    count = dot(hit.astype(bf16), upper.astype(bf16))
    slot = lax.broadcasted_iota(jnp.int32, (CAP, TOK), 0).astype(f32) + 1.0
    picks, weights = [], []
    for e in range(2):
        pick = (count[e : e + 1] == slot) & hit[e : e + 1]
        picks.append(pick.astype(bf16))
        weights.append(jnp.sum(jnp.where(pick, gates[e : e + 1], 0.0), axis=1, keepdims=True))
    return jnp.concatenate(picks, axis=0), jnp.concatenate(weights, axis=0)


def block_at(j, shape):
    def index(i, order):
        return (order[i * BLOCKS + j],) + (0,) * len(shape)

    return pl.BlockSpec((1,) + shape, index)


def expert_rows(width):
    return pl.BlockSpec((2, STEP, width), lambda i, *_: (0, i, 0))


def pair_block():
    return pl.BlockSpec((NEAR, TOK, D), lambda i, *_: (i, 0, 0))


def pick_block():
    return pl.BlockSpec((BLOCKS, 2 * CAP, TOK), lambda i, *_: (i, 0, 0))


SLOTS = 16 * CAP


def expert_begin_body(order, *refs):
    grads, gates = (refs[k * BLOCKS : (k + 1) * BLOCKS] for k in range(2))
    start, above, below, low, high = refs[2 * BLOCKS : 2 * BLOCKS + 5]
    pick_ref, grad_ref, act_ref, w_down = refs[2 * BLOCKS + 5 :]

    @pl.when(pl.program_id(0) == 0)
    def _():
        for half, far in enumerate((low, high)):
            for k, block in enumerate((start, above, far, below)):
                at = pl.multiple_of(order[16 + 4 * half + k] * 64, 64)
                for e in range(2):
                    w_down[e, pl.ds(at, 64), :] = block[0 if k == 2 else half, e]

    for j in range(BLOCKS):
        pick, weight = choices(gates[j][0])
        pick_ref[j] = pick
        graded = (dot(pick, grads[j][0]) * weight).astype(bf16)
        for e in range(2):
            grad_ref[e, j * CAP : (j + 1) * CAP, :] = graded[e * CAP : (e + 1) * CAP]
    for e in range(2):
        act_ref[e] = dot_nt(grad_ref[e], w_down[e])


def expert_begin(order, grads, gates, downs):
    return run(
        expert_begin_body,
        [
            struct((16, 2 * CAP, TOK), bf16),
            struct((2, SLOTS, D), bf16),
            struct((2, SLOTS, 512), f32),
            struct((2, 512, D), bf16),
        ],
        [block_at(j, (TOK, D)) for j in range(BLOCKS)]
        + [block_at(j, (2, TOK)) for j in range(BLOCKS)]
        + [once(v.shape) for v in downs],
        [pick_block(), expert_rows(D), expert_rows(512), whole((2, 512, D))],
        (16 // BLOCKS,),
        (grads,) * BLOCKS + (gates,) * BLOCKS + downs,
        prefetch=order,
        micros=11,
    )


def experts_body(order, *refs):
    rows = refs[:BLOCKS]
    picks, grad_acts = refs[BLOCKS : BLOCKS + 2]
    packs = refs[BLOCKS + 2 : BLOCKS + 10]
    near_ref, across_ref, in_ref, act_ref, da_ref, db_ref, w_gate, w_up = refs[BLOCKS + 10 :]

    @pl.when(pl.program_id(0) == 0)
    def _():
        for half in range(2):
            own, above, below = packs[3 * half : 3 * half + 3]
            far = slice(192 * half, 192 * half + 192)
            for k, block in enumerate((own, above, None, below)):
                at = pl.ds(pl.multiple_of(order[16 + 4 * half + k] * 192, 192), 192)
                for e in range(2):
                    w_gate[e, at, :] = packs[6][e, far] if k == 2 else block[e, :192]
                    w_up[e, at, :] = packs[7][e, far] if k == 2 else block[e, 192:]

    for j in range(BLOCKS):
        taken = dot(picks[j], rows[j][0]).astype(bf16)
        for e in range(2):
            in_ref[e, j * CAP : (j + 1) * CAP, :] = taken[e * CAP : (e + 1) * CAP]
    backs = []
    for e in range(2):
        taken, grad_act = in_ref[e], grad_acts[e]
        gate_pre = dot(taken, w_gate[e])
        up_pre = dot(taken, w_up[e])
        sig = 1.0 / (1.0 + jnp.exp(-gate_pre))
        silu = gate_pre * sig
        act_ref[e] = (silu * up_pre).astype(bf16)
        da = (grad_act * up_pre * sig * (1.0 + gate_pre * (1.0 - sig))).astype(bf16)
        db = (grad_act * silu).astype(bf16)
        da_ref[e] = da
        db_ref[e] = db
        backs.append((dot_nt(da, w_gate[e]) + dot_nt(db, w_up[e])).astype(bf16))
    for j in range(BLOCKS):
        at = slice(j * CAP, (j + 1) * CAP)
        back = dot_tn(picks[j], jnp.concatenate([backs[0][at], backs[1][at]], axis=0))
        target = near_ref if j < NEAR else across_ref
        target[j % NEAR] = back.astype(bf16)


def experts(order, rows, picks, grad_acts, packs):
    return run(
        experts_body,
        [struct((8, TOK, D), bf16)] * 2
        + [struct((2, SLOTS, D), bf16)]
        + [struct((2, SLOTS, 512), bf16)] * 3,
        [block_at(j, (TOK, D)) for j in range(BLOCKS)]
        + [pick_block(), expert_rows(512)]
        + [once(v.shape) for v in packs],
        [pair_block(), pair_block(), expert_rows(D)] + [expert_rows(512)] * 3,
        (16 // BLOCKS,),
        (rows,) * BLOCKS + (picks, grad_acts) + packs,
        prefetch=order,
        scratch=[pltpu.VMEM((2, D, 512), bf16)] * 2,
        micros=22,
    )


def expert_out_body(order, *refs):
    gates = refs[:BLOCKS]
    picks, act, w_down, out_ref = refs[BLOCKS:]
    step = pl.program_id(0)
    outs = [dot(act[e], w_down[e]) for e in range(2)]
    for j in range(BLOCKS):
        pick = picks[j]
        weights = [
            jnp.sum(pick[e * CAP : (e + 1) * CAP].astype(f32) * gates[j][0, e : e + 1], axis=1, keepdims=True)
            for e in range(2)
        ]
        at = slice(j * CAP, (j + 1) * CAP)
        both = jnp.concatenate([outs[e][at] * weights[e] for e in range(2)], axis=0)
        out_ref[order[step * BLOCKS + j]] = dot_tn(pick, both.astype(bf16)).astype(bf16)


def expert_out(order, gates, picks, act, w_down):
    return run(
        expert_out_body,
        [struct((16, TOK, D), bf16)],
        [block_at(j, (2, TOK)) for j in range(BLOCKS)]
        + [pick_block(), expert_rows(512), once(w_down.shape)],
        [whole((16, TOK, D))],
        (16 // BLOCKS,),
        (gates,) * BLOCKS + (picks, act, w_down),
        prefetch=order,
        micros=2,
    )[0]


def one(rows, width):
    return pl.BlockSpec((1, rows, width), lambda e, *_: (e, 0, 0))


def grad_down_body(order, act, graded, down_ref):
    e = pl.program_id(0)
    down = dot_tn(act[0], graded[0]).astype(bf16)
    for k in range(8):
        down_ref[order[k], e] = down[k * 64 : (k + 1) * 64]


def expert_grad_down(order, act, graded):
    return run(
        grad_down_body,
        [struct((8, 2, 64, D), bf16)],
        [one(SLOTS, 512), one(SLOTS, D)],
        [whole((8, 2, 64, D))],
        (2,),
        (act, graded),
        prefetch=order,
        micros=2,
    )[0]


def grad_pair_body(order, taken, da, db, pack_ref, fore_ref, back_ref):
    e = pl.program_id(0)
    both = dot_tn(taken[0], jnp.concatenate([da[0], db[0]], axis=1)).astype(bf16)
    gate, up = both[:, :512], both[:, 512:]
    for k in range(8):
        to = order[k]
        at = slice(k * 192, (k + 1) * 192)

        @pl.when(to < 6)
        def _(to=to, at=at):
            pack_ref[to // 2, lax.rem(to, 2), e, :192] = gate[at]
            pack_ref[to // 2, lax.rem(to, 2), e, 192:] = up[at]

        for far, ref in ((6, fore_ref), (7, back_ref)):

            @pl.when(to == far)
            def _(ref=ref, at=at):
                ref[e, :192] = gate[at]
                ref[e, 192:] = up[at]


def expert_grad_pair(order, taken, da, db):
    return run(
        grad_pair_body,
        [struct((3, 2, 2, 384, 512), bf16)] + [struct((2, 384, 512), bf16)] * 2,
        [one(SLOTS, D), one(SLOTS, 512), one(SLOTS, 512)],
        [whole((3, 2, 2, 384, 512)), whole((2, 384, 512)), whole((2, 384, 512))],
        (2,),
        (taken, da, db),
        prefetch=order,
        micros=2,
    )


def rms_scale(values):
    return lax.rsqrt(jnp.mean(values * values, axis=-1, keepdims=True) + norm_eps)


def three_parts(values):
    high = lax.reduce_precision(values, 8, 7)
    rest = values - high
    middle = lax.reduce_precision(rest, 8, 7)
    return [v.astype(bf16) for v in (high, middle, rest - middle)]


def shards(
    tokens,
    cotangent,
    segments,
    routes,
    gate_weights,
    w_query,
    w_key,
    w_value,
    w_out,
    norm_one,
    norm_two,
    w_gate,
    w_up,
    w_down,
):
    inputs = tokens[0].astype(f32)
    upstream = cotangent[0].astype(f32)
    yh, x = lax.axis_index("yh"), lax.axis_index("x")
    where = jnp.stack([x, yh]).astype(jnp.int32)
    order = jnp.stack(
        [
            m * 2 + ahead("c", j // NEAR)
            for i in range(16 // BLOCKS)
            for j in range(BLOCKS)
            for m in (NEAR * i + j % NEAR,)
        ]
        + [ahead("yh", k // 4) * 4 + ahead("x", k % 4) for k in range(8)]
    ).astype(jnp.int32)
    batch_place = jnp.stack(
        [
            distance("c", b % 2) * 8 + b // 2
            for b in range(16)
        ]
    ).astype(jnp.int32)
    seq_place = jnp.stack(
        [
            jnp.array([0, 1, 3, 2])[distance("x", s % 4)] * 2 + distance("yh", s // 4)
            for s in range(8)
        ]
    ).astype(jnp.int32)

    def for_heads(weight, width):
        by_head = jnp.swapaxes(weight.reshape(-1, 8, width), 0, 1)
        return [by_head, jnp.concatenate([by_head[4:], by_head[:4]], axis=0)]

    gains = jnp.pad(jnp.stack([norm_one, norm_two], axis=1), ((0, 0), (0, 126)))
    strip = jnp.concatenate(
        for_heads(w_query, Q_OWN)
        + for_heads(w_key, HEAD_DIM)
        + for_heads(w_value, HEAD_DIM)
        + [jnp.broadcast_to(gains[None], (8,) + gains.shape)],
        axis=2,
    )
    strip, w_out = tie(strip, w_out)
    strip = lax.all_to_all(strip, SEQ, 0, 0, tiled=True).reshape(96, 768)
    below, above = shift(tokens[0], "x", 1), shift(tokens[0], "x", -1)
    strip, below, above = tie(strip, below, above)
    half = TOK // 2
    pieces = (
        tokens[0], above, shift(below[:half], "x", 1), shift(above[half:], "x", -1), below
    )
    expert_ids = jnp.arange(EXPERTS, dtype=jnp.int32)[:, None, None]
    gate_dense = jnp.sum(jnp.where(routes[0][None] == expert_ids, gate_weights[0][None], 0.0), axis=2)
    strip = jnp.concatenate(
        [
            strip,
            jnp.concatenate(three_parts(gate_dense), axis=0),
            w_out.reshape(96, 192),
            shift(w_out, "yh", 1).reshape(96, 192),
        ],
        axis=1,
    )
    gathered = lax.all_gather(strip, BATCH, axis=0, tiled=True)
    grad_all = lax.all_gather(cotangent[0], BATCH, axis=0)

    feature = jnp.arange(D, dtype=jnp.int32)
    moved = feature % 192 // 12 * 96 + feature // 192 * 12 + feature % 12
    moving = (moved[:, None] == feature[None, :]).astype(bf16)
    xp, scale_half = prepare(where, pieces, moving)

    pack = jnp.concatenate([w_gate, w_up], axis=1)
    half_pack = pack.shape[1] // 2
    pack, w_down, _ = tie(pack, w_down, strip)
    down_other = shift(w_down, "yh", 1)
    pack_other = shift(pack, "yh", 1)
    downs = jnp.stack([w_down, down_other])
    downs, _, _ = tie(downs, pieces[2], pieces[3])
    down_below, down_above = shift(downs, "x", 1), shift(downs, "x", -1)

    def natural(row):
        return jnp.swapaxes(row.reshape(16, 8, 12), 0, 1).reshape(D)

    place = jnp.arange(2 * HALF, dtype=jnp.int32) + HALF * yh
    place = jnp.where(place >= 2 * HALF, place - 2 * HALF, place)
    seg = jnp.roll(segments[0], -HALF * yh)
    earlier = jnp.sum((seg[None, :] < seg[:, None]).astype(jnp.int32), axis=1)
    freq_index = jnp.arange(HEAD_DIM // 2, dtype=f32) * (2.0 / HEAD_DIM)
    frequency = jnp.tile(rope_base ** (-freq_index), 4)
    angle = (place - earlier).astype(f32)[:, None] * frequency
    cosine, sine = jnp.cos(angle), jnp.sin(angle)
    seg_row = seg[None, :]
    seg_col = jnp.broadcast_to(seg[:, None], (2 * HALF, 128))

    down_below, down_above, xp = tie(down_below, down_above, xp)
    down_low, down_high = shift(down_below[:1], "x", 1), shift(down_above[1:], "x", -1)
    gathered, xp, down_low, down_high = tie(gathered, xp, down_low, down_high)

    normed, queries, own, sent = project(xp, scale_half, gathered, cosine, sine)
    other = shift(sent, "yh", 1)
    pack, _ = tie(pack, normed)
    pack_below, pack_above = shift(pack, "x", 1), shift(pack, "x", -1)
    downs = (downs, down_above, down_below, down_low, down_high)
    out_rows = gathered[:, 896:1088].reshape(192, D)
    out_other = gathered[:, 1088:].reshape(192, D)
    gain_one = natural(gathered[:, 640].astype(f32))
    gain_two = natural(gathered[:, 641].astype(f32))
    gates = jnp.sum(gathered[:, 768:896].reshape(16, 3, EXPERTS, TOK).astype(f32), axis=1)
    gates = lax.dynamic_slice_in_dim(gates, lax.axis_index(BATCH) * 2, 2, axis=1)
    mixed, partial = attend(where, queries, own, other, seg_col, seg_row, out_rows, out_other)
    partial, pack_below, pack_above = tie(partial, pack_below, pack_above)
    partial = lax.all_to_all(partial, "x", 0, 0, tiled=True)
    hidden = inputs + jnp.sum(partial.astype(f32), axis=0)
    hidden, pack_other = tie(hidden, pack_other)
    both = ring_next((pack_other, pack_other), "x")

    scale_two = rms_scale(hidden)
    normed_two = (hidden * scale_two * gain_two).astype(bf16)
    normed_all = lax.all_gather(normed_two, BATCH, axis=0)
    grad_all, other_below, other_above = tie(grad_all, *both)
    low = jnp.concatenate([pack_below[:, :half_pack], other_below[:, :half_pack]], axis=1)
    high = jnp.concatenate([pack_above[:, half_pack:], other_above[:, half_pack:]], axis=1)
    low, high = ring_next((low, high), "x")
    picks, graded, grad_acts, down_full = expert_begin(order, grad_all, gates, downs)
    picks, graded, grad_acts, low, high = tie(picks, graded, grad_acts, low, high)
    packs = (pack, pack_above, pack_below, pack_other, other_above, other_below, low, high)
    near, across, taken, act, da, db = experts(
        order, normed_all, picks, grad_acts, packs
    )
    got = shift(across, "c", 1)
    down_place = jnp.stack([s % 4 * 2 + distance("yh", s // 4) for s in range(8)])
    grad_down = expert_grad_down(down_place.astype(jnp.int32), act, graded)
    grad_down, got = tie(grad_down, got)
    grad_down = grad_down.reshape(8 * 2 * 64, D)
    held = add_up(near, got).astype(bf16)
    taken, _ = tie(taken, held)
    held = lax.all_to_all(held, ("yl", "z"), 0, 0, tiled=True)
    grad_pack, fore, back = expert_grad_pair(seq_place, taken, da, db)
    act, grad_pack = tie(act, grad_pack)
    pack_sent = shift(fore, "x", 1), shift(back, "x", -1)
    out_part = expert_out(order, gates, picks, act, down_full)
    out_part, held, *pack_sent = tie(out_part, held, *pack_sent)
    output = lax.psum_scatter(out_part, BATCH, scatter_dimension=0, tiled=True)
    grad_normed_two = jnp.sum(held.astype(f32), axis=0)

    scaled_two = gain_two * grad_normed_two
    grad_gain_two = jnp.sum(grad_normed_two * hidden * scale_two, axis=0)
    grad_hidden = (
        upstream
        + scale_two * scaled_two
        - hidden * scale_two**3 * jnp.mean(scaled_two * hidden, axis=-1, keepdims=True)
    )
    pieces = jnp.broadcast_to(grad_hidden.astype(bf16)[None], (4, TOK, D))
    pieces = lax.all_to_all(pieces, "x", 0, 0, tiled=True)
    pack_hops = [
        [jnp.stack([add_up(grad_pack[1, 0, e], pack_sent[0][e]).astype(bf16), grad_pack[1, 1, e]]),
         jnp.stack([grad_pack[2, 0, e], add_up(grad_pack[2, 1, e], pack_sent[1][e]).astype(bf16)])]
        for e in range(2)
    ]
    pack_hops = pack_hops[0] + pack_hops[1]
    first_hops = ring_next(pack_hops[:2], "x")
    back = attend_back(
        where, queries, mixed, own, other, seg_col, seg_row, out_rows, out_other,
        pieces, cosine, sine,
    )
    *back, hop_0, hop_1, pack_low, pack_high = tie(*back, *first_hops, *pack_hops[2:])
    first_hops = hop_0, hop_1
    grad_query, grad_own, grad_sent, grad_out_w = back
    last_hops = ring_next((pack_low, pack_high), "x")
    grad_got = shift(grad_sent, "yh", 1)
    first_total = add_up(grad_pack[0, :, 0], *first_hops)
    first_total, _ = tie(first_total, grad_sent)
    first_last = shift(first_total[1].astype(bf16), "yh", 1)
    back = unproject(where, grad_query, grad_own, grad_got, gathered, moving)
    grad_raw, grad_part, first_last, output, *last_hops = tie(
        *back, first_last, output, *last_hops
    )
    grad_down, _ = tie(grad_down, output)
    grad_down = lax.psum_scatter(grad_down, "x", scatter_dimension=0, tiled=True)
    part_sent = ring_send(grad_part, "x")
    gain_two_part = jnp.swapaxes(grad_gain_two.reshape(8, 16, 12), 0, 1).reshape(1, D)
    gain_rows = jnp.concatenate([gain_two_part, jnp.zeros((7, D), f32)], axis=0)
    near, across = weight_grad(batch_place, normed, grad_raw, gain_rows, grad_out_w)
    near, across, *rest = tie(near, across, *last_hops, *part_sent)
    last_hops, part_sent = rest[:2], rest[2:]
    got = shift(across, "c", 1)
    last_total = add_up(grad_pack[0, :, 1], *last_hops)
    last_last = shift(last_total[1].astype(bf16), "yh", 1)
    got, last_total = tie(got, last_total)
    held = add_up(near, got).astype(bf16)
    first_total, output, _ = tie(first_total, output, held)
    held, *part_sent = tie(held, *part_sent)
    held = lax.all_to_all(held, ("yl", "z"), 0, 0, tiled=True)
    grad_normed_one = add_up(grad_part[0], *ring_next(ring_add(grad_part, part_sent), "x"))
    scaled_one = gain_one * grad_normed_one
    scale_one = rms_scale(inputs)
    grad_inputs = (
        grad_hidden
        + scale_one * scaled_one
        - inputs * scale_one**3 * jnp.mean(scaled_one * inputs, axis=-1, keepdims=True)
    ).astype(bf16)
    output = (hidden + output[0].astype(f32)).astype(bf16)
    gain = jnp.broadcast_to(norm_one.astype(f32)[:, None], (12, 128))
    grad_down = grad_down.reshape(2, 2, 64, D)
    grad_pack = [add_up(first_total[0], first_last), add_up(last_total[0], last_last)]
    grad_pack = jnp.stack(grad_pack)
    sum_gate, sum_up = grad_pack[:, :192], grad_pack[:, 192:]
    held, output, gain, grad_inputs, sum_gate, sum_up = tie(
        held, output, gain, grad_inputs, sum_gate, sum_up
    )
    down_own, down_far = grad_down[0], grad_down[1]
    grad_w = jnp.sum(held.astype(f32), axis=0).astype(bf16)
    out_sum = grad_w[96:].astype(f32).reshape(2, 2, 12, 768)
    out_got = shift(out_sum[1].astype(bf16), "yh", 1)
    grad_w = lax.all_to_all(grad_w[:96].reshape(8, 12, 768), SEQ, 0, 0, tiled=True)
    down_last = shift(down_far, "yh", 1)
    sum_out = add_up(out_sum[0], out_got)
    sum_out = jnp.swapaxes(sum_out, 0, 1).reshape(12, D)
    sum_down = add_up(down_own, down_last)
    grad_w, sum_out, sum_down = tie(grad_w, sum_out, sum_down)
    grad_q, grad_k, grad_v, grad_gain = finish(grad_w, w_query, w_key, w_value, gain)
    return (
        output[None],
        grad_inputs[None],
        grad_q,
        grad_k,
        grad_v,
        sum_out,
        grad_gain[0, :12],
        grad_gain[1, :12],
        sum_gate,
        sum_up,
        sum_down,
    )


def solution(mesh):
    fine = Mesh(mesh.devices.reshape(2, 4, 2, 4, 2), SEQ + BATCH)
    both = SEQ + BATCH
    placed = (
        P(BATCH, SEQ, None),
        P(BATCH, SEQ, None),
        P(BATCH, None),
        P(BATCH, SEQ, None),
        P(BATCH, SEQ, None),
        P(both, None),
        P(both, None),
        P(both, None),
        P(both, None),
        P(both),
        P(both),
        P(BATCH, SEQ, None),
        P(BATCH, SEQ, None),
        P(BATCH, SEQ, None),
    )
    return jax.shard_map(
        shards,
        mesh=fine,
        in_specs=placed,
        out_specs=(
            P(BATCH, SEQ, None),
            P(BATCH, SEQ, None),
            P(both, None),
            P(both, None),
            P(both, None),
            P(both, None),
            P(both),
            P(both),
            P(BATCH, SEQ, None),
            P(BATCH, SEQ, None),
            P(BATCH, SEQ, None),
        ),
        check_vma=False,
    )
```
